512 devices in a mesh: seq: 128 (over x, y_lo, z, core), head: 4 (over y_hi).
Axes of the slice: x: 4, y: 8 (y_hi: 4, y_lo: 2; y = y_hi * 2 + y_lo), z: 8, core: 2. Of those that a mesh axis runs over, the one named last changes fastest.
Arguments:
- tokens: bfloat16 [32768, 768], P('seq'), may hold values from -9 to 9
- valid: int32 [32768], P('seq'), may hold values from 0 to 1, as said below
- offsets: int32 [16, 2], P('head'), may hold values from 0 to 15, as said below
- qkv_weight: bfloat16 [768, 2304], P(None, 'head'), may hold values from -0.21875 to 0.21875
- out_weight: bfloat16 [768, 768], P('head'), may hold values from -0.21875 to 0.21875
- out_grad: bfloat16 [32768, 768], P('seq'), may hold values from -6 to 6
Outputs:
- grad_tokens: bfloat16 [32768, 768], P('seq', 'head')
- grad_qkv_weight: float32 [768, 2304], P('seq', 'head')
- grad_out_weight: float32 [768, 768], P('head', 'seq')
The draws below stay inside these ranges and needn't reach their ends.
Inputs may be any that keep to these rules, and one draw needn't show every extreme that they name: `valid`: for every j, among the tokens 256 * j to 256 * (j + 1) - 1 at least one is 1. `offsets`: column 0 lies in 0 to 3, column 1 in 0 to 15.
All inputs are finite; a program needn't handle non-finite values.
Results may differ from the reference program's by a relative error of at most 0.03.
The reference program's roundings to bfloat16 on the way count: a program that leaves them out, or rounds other values in their place, can miss the bound.
Values may be sent and summed in bfloat16 or wider, within the bound.
A program may use at most 64 MiB of HBM per device.

```python
import math
import jax
import jax.numpy as jnp
from jax import lax

D = 768
HEADS = 16
TOK_DEV = 256
SPAN2 = 4
HD = 48
TOKENS = 32768
SPAN3 = 16
N_HEAD = 4


def draw_tokens(key, part):
    key = jax.random.fold_in(key, 5)
    first_key = jax.random.fold_in(key, 0)
    base_vals = jax.random.truncated_normal(first_key, -4.0, 4.0, (TOKENS, D), jnp.float32)
    return base_vals.astype(jnp.bfloat16)


def draw_valid(key, part):
    key = jax.random.fold_in(key, 7)
    level_key, random_flip_key, forced_key = jax.random.split(key, 3)
    block_count = TOKENS // TOK_DEV
    density = jax.random.randint(level_key, (block_count,), 1, 9)
    coin_flip = jax.random.randint(random_flip_key, (TOKENS,), 0, 8)
    forced = jax.random.randint(forced_key, (block_count,), 0, TOK_DEV)
    position = jnp.arange(TOKENS, dtype=jnp.int32)
    block_density = jnp.repeat(density, TOK_DEV)
    block_forced = jnp.repeat(forced, TOK_DEV)
    tissue = (coin_flip < block_density) | (position % TOK_DEV == block_forced)
    return tissue.astype(jnp.int32)


def draw_offsets(key, part):
    key = jax.random.fold_in(key, 9)
    near_key, far_key = jax.random.split(key)
    near_col = jax.random.permutation(near_key, HEADS) % SPAN2
    far_col = jax.random.permutation(far_key, HEADS) % SPAN3
    return jnp.stack([near_col, far_col], axis=1).astype(jnp.int32)


def block_scale(own_key, shape, cuts, smallest, high):
    factor_of, own = 1.0, jax.random.fold_in(own_key, 6)
    for dim, parts in cuts:
        steps = jnp.exp(jax.random.uniform(jax.random.fold_in(own, dim), (parts,), jnp.float32, smallest / len(cuts), high / len(cuts)))
        factor_of = factor_of * jnp.repeat(steps, shape[dim] // parts).reshape([-1 if axis == dim else 1 for axis in range(len(shape))])
    return factor_of


def noise(rng, dims, spread, limit, pieces=(), kind=jnp.bfloat16):
    result = jax.random.normal(rng, dims, jnp.float32) * spread
    if len(pieces) > 0:
        result = block_scale(rng, dims, pieces, -0.22, 0.18) * result
    return jnp.clip(result, min=-limit, max=limit).astype(kind)


def setup_inputs(seed: int = 0) -> dict:
    streams_of = jax.random.split(jax.random.key(seed), 7)
    return {
        "tokens": draw_tokens(jax.random.fold_in(streams_of[6], 71), 0),
        "valid": draw_valid(jax.random.fold_in(streams_of[6], 71), 0),
        "offsets": draw_offsets(jax.random.fold_in(streams_of[6], 71), 0),
        "qkv_weight": noise(streams_of[3], (D, 3 * D), D ** -0.5, 0.21875, ((1, 4),)),
        "out_weight": noise(streams_of[4], (D, D), D ** -0.5, 0.21875, ((0, 4),)),
        "out_grad": noise(streams_of[5], (TOKENS, D), 1.0, 6.0, ((0, 128),)),
    }


def select_rows(values, stride, phase):
    if stride == 1:
        return values
    blocks = values.reshape((values.shape[0] // stride, stride) + values.shape[1:])
    return lax.dynamic_index_in_dim(blocks, phase, 1, keepdims=False)

def spread_rows(values, stride, phase, filler):
    if stride == 1:
        return values
    chosen = (jnp.arange(stride, dtype=jnp.int32) == phase).reshape((1, stride) + (1,) * (values.ndim - 1))
    full = jnp.where(chosen, values[:, None], filler)
    return full.reshape((values.shape[0] * stride,) + values.shape[1:])

def segment_view(values, stride, phase):
    picked = select_rows(values, stride, phase)
    return picked.reshape((-1, TOK_DEV) + values.shape[1:])

def to_bf16_and_back(values):
    return lax.optimization_barrier(values.astype(jnp.bfloat16)).astype(jnp.float32)

def reference(tokens, valid, offsets, qkv_weight, out_weight, out_grad):
    row_count = tokens.shape[0]
    factor = 1.0 / math.sqrt(HD)
    projected = jnp.dot(tokens, qkv_weight, preferred_element_type=jnp.float32).astype(jnp.bfloat16)
    projected = projected.reshape(row_count, HEADS, 3, HD)
    d_attention = jnp.dot(out_grad, out_weight.T, preferred_element_type=jnp.float32).astype(jnp.bfloat16)
    d_attention = d_attention.reshape(row_count, HEADS, HD)
    live_tile = valid > 0
    strides = (1, SPAN2, SPAN3)

    def one_head(head_idx):
        queries = projected[:, head_idx, 0]
        keys_all = projected[:, head_idx, 1]
        values_all = projected[:, head_idx, 2]
        d_here = d_attention[:, head_idx].astype(jnp.float32)
        phases = (jnp.int32(0), offsets[head_idx, 0], offsets[head_idx, 1])
        score_list = []
        mask_list = []
        top_score = None
        for stride, phase in zip(strides, phases):
            q_seg = segment_view(queries, stride, phase).astype(jnp.float32)
            k_seg = segment_view(keys_all, stride, phase).astype(jnp.float32)
            mask_seg = segment_view(live_tile, stride, phase)
            scores = jnp.einsum('gid,gjd->gij', q_seg, k_seg) * factor
            row_max = lax.optimization_barrier(jnp.max(jnp.where(mask_seg[:, None, :], scores, -1e+30), axis=-1)).reshape(-1)
            score_list.append(scores)
            mask_list.append(mask_seg)
            if top_score is None:
                top_score = row_max
            else:
                top_score = jnp.maximum(top_score, spread_rows(row_max, stride, phase, -1e+30))
        numer = jnp.zeros((row_count, HD), jnp.float32)
        denom = jnp.zeros((row_count,), jnp.float32)
        weight_list = []
        for level_idx in range(3):
            stride, phase = (strides[level_idx], phases[level_idx])
            top_at = segment_view(top_score, stride, phase)
            weights = jnp.where(mask_list[level_idx][:, None, :], jnp.exp(score_list[level_idx] - top_at[..., None]), 0.0)
            weight_list.append(weights)
            v_seg = segment_view(values_all, stride, phase).astype(jnp.float32)
            numer_part = jnp.einsum('gij,gjd->gid', to_bf16_and_back(weights), v_seg)
            numer = numer + spread_rows(numer_part.reshape(-1, HD), stride, phase, 0.0)
            denom = denom + spread_rows(lax.optimization_barrier(jnp.sum(weights, axis=-1)).reshape(-1), stride, phase, 0.0)
        attention = (numer / denom[:, None]).astype(jnp.bfloat16)
        delta = lax.optimization_barrier(jnp.sum(d_here * attention.astype(jnp.float32), axis=-1))
        query_gradient_rows = jnp.zeros((row_count, HD), jnp.float32)
        key_grad = jnp.zeros((row_count, HD), jnp.float32)
        value_grad = jnp.zeros((row_count, HD), jnp.float32)
        for level_idx in range(3):
            stride, phase = (strides[level_idx], phases[level_idx])
            q_seg = segment_view(queries, stride, phase).astype(jnp.float32)
            k_seg = segment_view(keys_all, stride, phase).astype(jnp.float32)
            v_seg = segment_view(values_all, stride, phase).astype(jnp.float32)
            den_at = segment_view(denom, stride, phase)
            normalized_scores = weight_list[level_idx] / den_at[..., None]
            d_seg = segment_view(d_here, stride, phase)
            delta_seg = segment_view(delta, stride, phase)
            prob_grad = jnp.einsum('gid,gjd->gij', d_seg, v_seg)
            score_gradient = to_bf16_and_back(normalized_scores * (prob_grad - delta_seg[..., None]))
            q_part = jnp.einsum('gij,gjd->gid', score_gradient, k_seg) * factor
            k_part = jnp.einsum('gij,gid->gjd', score_gradient, q_seg) * factor
            v_part = jnp.einsum('gij,gid->gjd', to_bf16_and_back(normalized_scores), d_seg)
            query_gradient_rows = query_gradient_rows + spread_rows(q_part.reshape(-1, HD), stride, phase, 0.0)
            key_grad = key_grad + spread_rows(k_part.reshape(-1, HD), stride, phase, 0.0)
            value_grad = value_grad + spread_rows(v_part.reshape(-1, HD), stride, phase, 0.0)
        stacked = jnp.stack([query_gradient_rows, key_grad, value_grad], axis=1).astype(jnp.bfloat16)
        return (attention, stacked)
    attn_all, grads_all = lax.map(one_head, jnp.arange(HEADS, dtype=jnp.int32))
    attention_flat = jnp.transpose(attn_all, (1, 0, 2)).reshape(row_count, D)
    qkv_grads = jnp.transpose(grads_all, (1, 0, 2, 3)).reshape(row_count, 3 * D)
    grad_out_weight = jnp.dot(attention_flat.T, out_grad, preferred_element_type=jnp.float32)
    grad_qkv_weight = jnp.dot(tokens.T, qkv_grads, preferred_element_type=jnp.float32)
    group_cols = 3 * D // N_HEAD
    summed = jnp.zeros((row_count, D), jnp.float32)
    for group_idx in range(N_HEAD):
        cols_grad = qkv_grads[:, group_idx * group_cols:(group_idx + 1) * group_cols]
        cols_weight = qkv_weight[:, group_idx * group_cols:(group_idx + 1) * group_cols]
        partial_sum = jnp.dot(cols_grad, cols_weight.T, preferred_element_type=jnp.float32)
        summed = summed + to_bf16_and_back(partial_sum)
    grad_tokens = summed.astype(jnp.bfloat16)
    return (grad_tokens, grad_qkv_weight, grad_out_weight)
```

```python
import functools
import math

import jax
import jax.numpy as jnp
from jax import lax
from jax.experimental import pallas as pl
from jax.experimental.pallas import tpu as pltpu
from jax.sharding import PartitionSpec as P

BF = jnp.bfloat16
F32 = jnp.float32
MESH = pl.DeviceIdType.MESH

HEADS = 4
HD = 48
TOK = 256
D = 768
KV = 2 * HD * HEADS
QW = HD * HEADS
CORES = 2
ZN = 8
GROUP2 = 4
GROUP3 = 16
ROWS2 = TOK // GROUP2
ROWS3 = TOK // GROUP3
MARK = 2.0**100
MARK_TEST = 2.0**90
LOW = -1e30


def nn(a, b):
    return lax.dot_general(a, b, (((1,), (0,)), ((), ())), preferred_element_type=F32)


def nt(a, b):
    return lax.dot_general(a, b, (((1,), (1,)), ((), ())), preferred_element_type=F32)


def iota(shape, dim):
    return lax.broadcasted_iota(jnp.int32, shape, dim)


def one_hot(mask):
    return jnp.where(mask, 1.0, 0.0).astype(BF)


class Plan:
    def __init__(self, n_seq, n_head):
        self.n_seq = n_seq
        self.n_head = n_head
        self.yn = 2 if n_seq >= 32 else 1
        self.xn = n_seq // (CORES * ZN * self.yn)
        self.chips = n_seq // CORES
        self.rows_dev = D // n_seq
        self.rows_pad = -(-self.rows_dev // 8) * 8
        self.chunk = CORES * self.rows_pad
        self.rows = self.chips * self.chunk
        self.xrows = self.rows // self.xn
        self.zrows = self.xrows // ZN


def body(plan, offs, valid, tokens, wqkv, wout, ograd, gt_out, gw_out, go_out,
         proj, kv1, kv2, kv3, g2, g3, r2, r3, own, att_t, dq_t, dat_t, dat, tok_t, og_t,
         m, m_in, xs, xr, zs, zr, ys, yr, fin, pt, pr,
         a2s, a2r, a3s, a3r, b2s, b2r, b3s, b3r, cs, cr, ms, mr, xss, xrs, zss, zrs, yss, yrs):
    xn, yn, nh = plan.xn, plan.yn, plan.n_head
    factor = 1.0 / math.sqrt(HD)
    seq = lax.axis_index("seq")
    head = lax.axis_index("head")
    core = seq % CORES
    z = (seq // CORES) % ZN
    y = (seq // (CORES * ZN)) % yn
    x = seq // (CORES * ZN * yn)

    def place(xi, yi, zi, ci):
        return (((xi * yn + yi) * ZN + zi) * CORES + ci, head)

    pos3 = seq % GROUP3
    base3 = seq - pos3
    pos2 = seq % GROUP2
    base2 = seq - pos2
    other = 1 - core

    def peer3(d):
        return (base3 + (pos3 + d) % GROUP3, head)

    def peer2(d):
        return (base2 + (pos2 + d) % GROUP2, head)

    x_peers = [((x + d) % xn, d) for d in range(1, xn)]
    y_peers = [place(x, (y + 1) % yn, z, core), place(x, (y + 1) % yn, z, other)] if yn > 1 else []
    h_peers = [(seq, (head + d) % nh) for d in range(1, nh)]

    barrier = pltpu.get_barrier_semaphore()
    greeted = [peer3(d) for d in range(1, GROUP3)]
    greeted += [place(xi, y, z, core) for xi, _ in x_peers] + y_peers + h_peers
    for who in greeted:
        pl.semaphore_signal(barrier, inc=1, device_id=who, device_id_type=MESH)

    started = []

    def send(src, dst, ssem, rsem, who):
        copy = pltpu.make_async_remote_copy(
            src_ref=src, dst_ref=dst, send_sem=ssem, recv_sem=rsem,
            device_id=who, device_id_type=MESH)
        copy.start()
        started.append(copy)
        return copy

    proj[...] = nn(tokens[...], wqkv[...]).astype(BF)
    eye = iota((TOK, TOK), 0) == iota((TOK, TOK), 1)
    alive = jnp.sum(jnp.where(eye, valid[...].astype(F32), 0.0), axis=1, keepdims=True)
    packed = jnp.concatenate(
        [proj[:, 3 * HD * h + HD:3 * HD * (h + 1)] for h in range(HEADS)], axis=1)
    marked = (iota((TOK, KV), 1) % (2 * HD) == 0) & (alive == 0.0)
    kv1[...] = jnp.where(marked, MARK, packed.astype(F32)).astype(BF)
    for h in range(HEADS):
        rows = iota((ROWS2 + ROWS3, TOK), 0)
        want = jnp.where(rows < ROWS2, rows * GROUP2 + offs[h, 0],
                         (rows - ROWS2) * GROUP3 + offs[h, 1])
        pick = one_hot(iota((ROWS2 + ROWS3, TOK), 1) == want)
        cols = slice(2 * HD * h, 2 * HD * (h + 1))
        chosen = nn(pick, kv1[:, cols]).astype(BF)
        kv2[pos2, :, cols] = chosen[:ROWS2]
        kv3[pos3, :, cols] = chosen[ROWS2:]

    pl.semaphore_wait(barrier, len(greeted))
    a_copies = []
    for d in range(1, GROUP2):
        a_copies.append(send(kv2.at[pos2], kv2.at[pos2], a2s.at[d], a2r.at[d], peer2(d)))
    for d in range(1, GROUP3):
        a_copies.append(send(kv3.at[pos3], kv3.at[pos3], a3s.at[d], a3r.at[d], peer3(d)))

    dat[...] = nt(ograd[...], wout[...]).astype(BF)
    dat_t[...] = nt(wout[...], ograd[...]).astype(BF)
    half = plan.rows // 2
    rr = iota((half, 1), 0)
    spot = rr // plan.chunk
    inner = rr % plan.chunk
    y_of = spot % yn
    z_of = (spot // yn) % ZN
    x_of = spot // (yn * ZN)
    chip = (x_of * yn + y_of) * ZN + z_of
    j = inner % plan.rows_pad
    source = jnp.where(j < plan.rows_dev,
                       (chip * CORES + inner // plan.rows_pad) * plan.rows_dev + j, -1)
    place_rows = one_hot(iota((half, D // 2), 1) == source)
    for part in range(2):
        cols = slice(part * D // 2, (part + 1) * D // 2)
        to = slice(part * half, (part + 1) * half)
        tok_t[to] = nt(place_rows, tokens[:, cols]).astype(BF)
        og_t[to] = nt(place_rows, ograd[:, cols]).astype(BF)

    for copy in a_copies:
        copy.wait_recv()

    lane = iota((1, TOK), 1)
    eye_kv = one_hot(iota((KV, KV), 0) == iota((KV, KV), 1))
    keys = [kv1[...], kv2[...].reshape(TOK, KV), kv3[...].reshape(TOK, KV)]
    keys_t = [nt(eye_kv, k).astype(BF) for k in keys]
    for h in range(HEADS):
        kc = slice(2 * HD * h, 2 * HD * h + HD)
        vc = slice(2 * HD * h + HD, 2 * HD * (h + 1))
        hr = slice(HD * h, HD * (h + 1))
        q = proj[:, 3 * HD * h:3 * HD * h + HD]
        d = dat[:, hr]
        d_t = dat_t[hr, :]
        inside = [None, lane % GROUP2 == offs[h, 0], lane % GROUP3 == offs[h, 1]]
        scores = []
        top = None
        for level in range(3):
            k = keys[level][:, kc]
            keep = k[:, 0:1].astype(F32) < MARK_TEST
            if level:
                keep = keep & inside[level]
            s = jnp.where(keep, nt(k, q) * factor, LOW)
            peak = jnp.max(s, axis=0, keepdims=True)
            top = peak if top is None else jnp.maximum(top, peak)
            scores.append(s)
        weights = [jnp.exp(s - top) for s in scores]
        den = sum(jnp.sum(w, axis=0, keepdims=True) for w in weights)
        num = sum(nn(keys_t[level][vc, :], weights[level].astype(BF)) for level in range(3))
        inv = 1.0 / den
        att = (num * inv).astype(BF)
        att_t[hr, :] = att
        delta = jnp.sum(d_t.astype(F32) * att.astype(F32), axis=0, keepdims=True)
        dq = None
        for level in range(3):
            normed = weights[level] * inv
            v = keys[level][:, vc]
            ds = (normed * (nn(v, d_t) - delta)).astype(BF)
            dq_part = nn(keys_t[level][kc, :], ds)
            dq = dq_part if dq is None else dq + dq_part
            dk = nn(ds, q) * factor
            dv = nn(normed.astype(BF), d)
            if level == 0:
                own[:, kc] = dk
                own[:, vc] = dv
            elif level == 1:
                g2[:, :, kc] = dk.astype(BF).reshape(GROUP2, ROWS2, HD)
                g2[:, :, vc] = dv.astype(BF).reshape(GROUP2, ROWS2, HD)
            else:
                g3[:, :, kc] = dk.astype(BF).reshape(GROUP3, ROWS3, HD)
                g3[:, :, vc] = dv.astype(BF).reshape(GROUP3, ROWS3, HD)
        dq_t[hr, :] = (dq * factor).astype(BF)

    b_copies = []
    for d in range(1, GROUP2):
        b_copies.append(send(g2.at[(pos2 + d) % GROUP2], r2.at[pos2], b2s.at[d], b2r.at[d], peer2(d)))
    for d in range(1, GROUP3):
        b_copies.append(send(g3.at[(pos3 + d) % GROUP3], r3.at[pos3], b3s.at[d], b3r.at[d], peer3(d)))
    r2[pos2] = g2[pos2]
    r3[pos3] = g3[pos3]
    m[0, :, 0:QW] = nt(og_t[...], att_t[...]).astype(BF)
    m[0, :, QW:2 * QW] = nt(tok_t[...], dq_t[...]).astype(BF)
    for copy in b_copies:
        copy.wait_recv()

    parts = []
    for h in range(HEADS):
        cols = slice(2 * HD * h, 2 * HD * (h + 1))
        row, col = iota((TOK, TOK), 0), iota((TOK, TOK), 1)
        spread2 = one_hot(row == (col % ROWS2) * GROUP2 + offs[h, 0])
        spread3 = one_hot(row == (col % ROWS3) * GROUP3 + offs[h, 1])
        parts.append(own[:, cols]
                     + nn(spread2, r2[...].reshape(TOK, KV)[:, cols])
                     + nn(spread3, r3[...].reshape(TOK, KV)[:, cols]))
    dkv = jnp.concatenate(parts, axis=1).astype(BF)

    w = wqkv[...]
    wq = jnp.concatenate([w[:, 3 * HD * h:3 * HD * h + HD] for h in range(HEADS)], axis=1)
    wkv = jnp.concatenate([w[:, 3 * HD * h + HD:3 * HD * (h + 1)] for h in range(HEADS)], axis=1)
    pt[...] = (nn(wq, dq_t[...]) + nt(wkv, dkv)).astype(BF).reshape(pt.shape)
    c_copies = []
    for d in range(1, nh):
        to = (head + d) % nh
        c_copies.append(send(pt.at[to], pr.at[d], cs.at[d], cr.at[d], (seq, to)))

    m[1] = nn(tok_t[...], dkv).astype(BF)
    sibling = send(m.at[other], m_in, ms, mr, place(x, y, z, other))
    sibling.wait_recv()
    total = m[core].astype(F32) + m_in[...].astype(F32)
    xs[...] = total.astype(BF).reshape(xs.shape)
    x_copies = []
    for xi, d in x_peers:
        x_copies.append(send(xs.at[xi], xr.at[d], xss.at[d], xrs.at[d], place(xi, y, z, core)))
    total = xs[x].astype(F32)
    for copy, (_, d) in zip(x_copies, x_peers):
        copy.wait_recv()
        total = total + xr[d].astype(F32)
    zs[...] = total.astype(BF).reshape(zs.shape)
    z_copies = []
    for d in range(1, ZN):
        zi = (z + d) % ZN
        z_copies.append(send(zs.at[zi], zr.at[d], zss.at[d], zrs.at[d], place(x, y, zi, core)))
    total = zs[z].astype(F32)
    for d in range(1, ZN):
        z_copies[d - 1].wait_recv()
        total = total + zr[d].astype(F32)
    ys[...] = total.astype(BF).reshape(ys.shape)
    far = (y + 1) % yn
    y_copies = [send(ys.at[y], yr.at[0], yss.at[0], yrs.at[0], place(x, y, z, other))]
    if yn > 1:
        y_copies.append(send(ys.at[far], yr.at[1], yss.at[1], yrs.at[1], y_peers[0]))
        y_copies.append(send(ys.at[far], yr.at[2], yss.at[2], yrs.at[2], y_peers[1]))

    total = pt[head].astype(F32)
    for d in range(1, nh):
        c_copies[d - 1].wait_recv()
        total = total + pr[d].astype(F32)
    eye_b = one_hot(eye)
    gt_out[...] = nt(eye_b, total.astype(BF)).astype(BF)

    for copy in y_copies:
        copy.wait_recv()
    mine = ys[y].astype(F32)
    theirs = yr[0].astype(F32)
    if yn > 1:
        mine = mine + yr[1].astype(F32)
        theirs = theirs + yr[2].astype(F32)
    fin[core] = mine
    fin[other] = theirs
    rows = pl.ds(pl.multiple_of(core * plan.rows_pad, 8), plan.rows_pad)
    first = fin[0, rows, :][:plan.rows_dev]
    second = fin[1, rows, :][:plan.rows_dev]
    go_out[...] = first[:, :QW]
    gw_out[...] = jnp.concatenate(
        [piece for h in range(HEADS)
         for piece in (first[:, QW + HD * h:QW + HD * (h + 1)],
                       second[:, 2 * HD * h:2 * HD * (h + 1)])], axis=1)
    for copy in started:
        copy.wait_send()


def per_device(plan, tokens, valid, offsets, qkv_weight, out_weight, out_grad):
    vm = pl.BlockSpec(memory_space=pltpu.VMEM)
    sm = pl.BlockSpec(memory_space=pltpu.SMEM)
    dma = pltpu.SemaphoreType.DMA
    nh, xn, yn, rows = plan.n_head, plan.xn, plan.yn, plan.rows
    scratch = [
        pltpu.VMEM((TOK, 3 * QW), BF),
        pltpu.VMEM((TOK, KV), BF),
        pltpu.VMEM((GROUP2, ROWS2, KV), BF),
        pltpu.VMEM((GROUP3, ROWS3, KV), BF),
        pltpu.VMEM((GROUP2, ROWS2, KV), BF),
        pltpu.VMEM((GROUP3, ROWS3, KV), BF),
        pltpu.VMEM((GROUP2, ROWS2, KV), BF),
        pltpu.VMEM((GROUP3, ROWS3, KV), BF),
        pltpu.VMEM((TOK, KV), F32),
        pltpu.VMEM((QW, TOK), BF),
        pltpu.VMEM((QW, TOK), BF),
        pltpu.VMEM((QW, TOK), BF),
        pltpu.VMEM((TOK, QW), BF),
        pltpu.VMEM((rows, TOK), BF),
        pltpu.VMEM((rows, TOK), BF),
        pltpu.VMEM((2, rows, KV), BF),
        pltpu.VMEM((rows, KV), BF),
        pltpu.VMEM((xn, plan.xrows, KV), BF),
        pltpu.VMEM((xn, plan.xrows, KV), BF),
        pltpu.VMEM((ZN, plan.zrows, KV), BF),
        pltpu.VMEM((ZN, plan.zrows, KV), BF),
        pltpu.VMEM((yn, plan.chunk, KV), BF),
        pltpu.VMEM((3, plan.chunk, KV), BF),
        pltpu.VMEM((2, plan.chunk, KV), F32),
        pltpu.VMEM((4, D // 4, TOK), BF),
        pltpu.VMEM((4, D // 4, TOK), BF),
        dma((GROUP2,)), dma((GROUP2,)), dma((GROUP3,)), dma((GROUP3,)),
        dma((GROUP2,)), dma((GROUP2,)), dma((GROUP3,)), dma((GROUP3,)),
        dma((4,)), dma((4,)), dma, dma,
        dma((4,)), dma((4,)), dma((ZN,)), dma((ZN,)), dma((3,)), dma((3,)),
    ]
    gt, gw, go = pl.pallas_call(
        functools.partial(body, plan),
        out_shape=(
            jax.ShapeDtypeStruct((TOK, D // 4), BF),
            jax.ShapeDtypeStruct((plan.rows_dev, 3 * QW), F32),
            jax.ShapeDtypeStruct((plan.rows_dev, QW), F32),
        ),
        in_specs=[sm] + [vm] * 5,
        out_specs=(vm, vm, vm),
        scratch_shapes=scratch,
        compiler_params=pltpu.CompilerParams(
            collective_id=0, has_side_effects=True, vmem_limit_bytes=48 * 1024 * 1024),
        cost_estimate=pl.CostEstimate(flops=2_000_000_000, bytes_accessed=4_000_000,
                                      transcendentals=800_000),
    )(offsets, valid.reshape(1, TOK), tokens, qkv_weight, out_weight, out_grad)
    return gt, gw, go.T


def solution(mesh):
    plan = Plan(mesh.shape["seq"], mesh.shape["head"])
    return jax.shard_map(
        functools.partial(per_device, plan),
        mesh=mesh,
        in_specs=(
            P("seq", None),
            P("seq"),
            P("head", None),
            P(None, "head"),
            P("head", None),
            P("seq", None),
        ),
        out_specs=(P("seq", "head"), P("seq", "head"), P("head", "seq")),
        check_vma=False,
    )
```

```python
import functools
import math

import jax
import jax.numpy as jnp
from jax import lax
from jax.experimental import pallas as pl
from jax.experimental.pallas import tpu as pltpu
from jax.sharding import PartitionSpec as P

BF = jnp.bfloat16
F32 = jnp.float32
MESH = pl.DeviceIdType.MESH

HEADS = 4
HD = 48
TOK = 256
D = 768
CORES = 2
MINE = HEADS // CORES
KV = 2 * HD * MINE
QW = HD * MINE
ALL = KV + QW
PAY = CORES * KV
ZN = 8
PAIR = 2
SPAN2 = 4
SPAN3 = 16
ROWS2 = TOK // SPAN2
ROWS3 = TOK // SPAN3
MARK = 2.0**100
MARK_TEST = 2.0**90
LOW = -1e30


def nn(a, b):
    return lax.dot_general(a, b, (((1,), (0,)), ((), ())), preferred_element_type=F32)


def nt(a, b):
    return lax.dot_general(a, b, (((1,), (1,)), ((), ())), preferred_element_type=F32)


def iota(shape, dim):
    return lax.broadcasted_iota(jnp.int32, shape, dim)


def one_hot(mask):
    return jnp.where(mask, 1.0, 0.0).astype(BF)


class Plan:
    def __init__(self, n_seq, n_head):
        self.n_head = n_head
        self.yn = 2 if n_seq >= 32 else 1
        self.xn = n_seq // (CORES * ZN * self.yn)
        self.rows_dev = D // n_seq
        self.rows_pad = -(-self.rows_dev // 8) * 8
        self.chunk = CORES * self.rows_pad
        self.rows = (n_seq // CORES) * self.chunk
        self.xrows = ZN * self.chunk
        self.lanes = self.yn * KV


def body(plan, offs, valid, tokens, wqkv, wout, ograd, gt_out, gw_out, go_out,
         p_out, tok_in, og_in, proj, kv2, kv3, g2, g3, r2, r3, own, att_t, dq_t,
         dat_t, tok_t, og_t, wn, d_out, d_in, q_out, q_in,
         xs, xr, zs, zr, ys, yr, fin, pt, pr,
         es, er, a2s, a2r, a3s, a3r, b2s, b2r, b3s, b3r, ds_, dr_, cs, cr,
         xss, xrs, zss, zrs, yss, yrs):
    xn, yn, nh = plan.xn, plan.yn, plan.n_head
    factor = 1.0 / math.sqrt(HD)
    seq = lax.axis_index("seq")
    head = lax.axis_index("head")
    core = seq % CORES
    other = 1 - core
    z = (seq // CORES) % ZN
    y = (seq // (CORES * ZN)) % yn
    x = seq // (CORES * ZN * yn)

    def place(xi, yi, zi, ci):
        return (((xi * yn + yi) * ZN + zi) * CORES + ci, head)

    pos2 = z % PAIR
    mate = z - pos2 + 1 - pos2
    sibling = place(x, y, z, other)
    z_peers = [(z + d) % ZN for d in range(1, ZN)]
    x_peers = [(x + d) % xn for d in range(1, xn)]
    far = (y + 1) % yn
    y_peers = [sibling]
    if yn > 1:
        y_peers += [place(x, far, z, core), place(x, far, z, other)]

    barrier = pltpu.get_barrier_semaphore()
    greeted = y_peers + [place(x, y, zi, core) for zi in z_peers]
    greeted += [place(xi, y, z, core) for xi in x_peers]
    greeted += [(seq, (head + d) % nh) for d in range(1, nh)]
    for who in greeted:
        pl.semaphore_signal(barrier, inc=1, device_id=who, device_id_type=MESH)

    started = []

    def send(src, dst, ssem, rsem, who):
        copy = pltpu.make_async_remote_copy(
            src_ref=src, dst_ref=dst, send_sem=ssem, recv_sem=rsem,
            device_id=who, device_id_type=MESH)
        copy.start()
        started.append(copy)
        return copy

    def heads_of(c):
        base = c * (MINE * 3 * HD)
        rows = [wqkv[pl.ds(pl.multiple_of(base + 3 * HD * h + HD, 16), 2 * HD), :]
                for h in range(MINE)]
        rows += [wqkv[pl.ds(pl.multiple_of(base + 3 * HD * h, 16), HD), :]
                 for h in range(MINE)]
        return (jnp.concatenate(rows, axis=0),
                wout[pl.ds(pl.multiple_of(c * QW, 16), QW), :])

    eye = iota((TOK, TOK), 0) == iota((TOK, TOK), 1)
    eye_b = one_hot(eye)
    alive = jnp.sum(jnp.where(eye, valid[...].astype(F32), 0.0), axis=1, keepdims=True)
    lane = iota((TOK, ALL), 1)
    marked = (lane % (2 * HD) == 0) & (lane < KV) & (alive == 0.0)

    def project(to, weights):
        to[:, :ALL] = jnp.where(marked, MARK, nt(tokens[...], weights[0])).astype(BF)
        to[:, ALL:] = nt(ograd[...], weights[1]).astype(BF)

    w_other = heads_of(other)
    project(p_out, w_other)
    pl.semaphore_wait(barrier, len(greeted))
    swap = send(p_out, proj.at[1], es.at[0], er.at[0], sibling)

    w_mine = heads_of(core)
    project(proj.at[0], w_mine)
    phase2 = [offs[0, core * MINE + h] for h in range(MINE)]
    phase3 = [offs[1, core * MINE + h] for h in range(MINE)]
    picks = []
    for h in range(MINE):
        rows = iota((ROWS2 + ROWS3, TOK), 0)
        want = jnp.where(rows < ROWS2, rows * SPAN2 + phase2[h],
                         (rows - ROWS2) * SPAN3 + phase3[h])
        picks.append(one_hot(iota((ROWS2 + ROWS3, TOK), 1) == want))

    def choose(b):
        for h in range(MINE):
            chosen = nn(picks[h], proj[b, :, 2 * HD * h:2 * HD * (h + 1)]).astype(BF)
            cols = slice(b * KV + 2 * HD * h, b * KV + 2 * HD * (h + 1))
            kv2[pos2, :, cols] = chosen[:ROWS2]
            kv3[z, :, cols] = chosen[ROWS2:]

    choose(0)
    swap.wait_recv()
    choose(1)

    a_copies = [send(kv2.at[pos2], kv2.at[pos2], a2s, a2r, place(x, y, mate, core))]
    for d, zi in enumerate(z_peers):
        a_copies.append(send(kv3.at[z], kv3.at[z], a3s.at[d], a3r.at[d], place(x, y, zi, core)))

    tok_swap = send(tokens, tok_in, es.at[1], er.at[1], sibling)
    og_swap = send(ograd, og_in, es.at[2], er.at[2], sibling)

    dat_t[:, :TOK] = nt(w_mine[1], ograd[...]).astype(BF)
    dat_t[:, TOK:] = nt(eye_b[:QW, :QW], proj[1, :, ALL:]).astype(BF)
    half = plan.rows // 2
    rr = iota((half, 1), 0)
    inner = rr % plan.chunk
    j = inner % plan.rows_pad
    source = jnp.where(
        j < plan.rows_dev,
        ((rr // plan.chunk) * CORES + inner // plan.rows_pad) * plan.rows_dev + j, -1)
    place_rows = one_hot(iota((half, D // 2), 1) == source)

    def place_block(to, block, b):
        for part in range(2):
            cols = slice(part * D // 2, (part + 1) * D // 2)
            to[part * half:(part + 1) * half, b * TOK:(b + 1) * TOK] = nt(
                place_rows, block[:, cols]).astype(BF)

    place_block(tok_t, tokens, 0)
    place_block(og_t, ograd, 0)
    eye_d = one_hot(iota((D, D), 0) == iota((D, D), 1))
    wn[0] = nt(eye_d, w_mine[0]).astype(BF)
    wn[1] = nt(eye_d, w_other[0]).astype(BF)

    for copy in a_copies:
        copy.wait_recv()

    lane = iota((1, TOK), 1)
    eye_kv = one_hot(iota((PAY, PAY), 0) == iota((PAY, PAY), 1))
    near, wide = kv2[...].reshape(PAIR * ROWS2, PAY), kv3[...].reshape(ZN * ROWS3, PAY)
    near_t, wide_t = nt(eye_kv, near).astype(BF), nt(eye_kv, wide).astype(BF)
    local_t = [nt(eye_kv[:KV, :KV], proj[b, :, :KV]).astype(BF) for b in range(2)]
    far_grads = {}
    for h in range(MINE):
        lo, mid, hi = 2 * HD * h, 2 * HD * h + HD, 2 * HD * (h + 1)
        hr = slice(HD * h, HD * (h + 1))
        keys, values, keys_t, values_t = {}, {}, {}, {}
        for level, rows, cols in ((1, near, near_t), (2, wide, wide_t)):
            keys[level] = jnp.concatenate([rows[:, lo:mid], rows[:, KV + lo:KV + mid]], axis=0)
            values[level] = jnp.concatenate([rows[:, mid:hi], rows[:, KV + mid:KV + hi]], axis=0)
            keys_t[level] = jnp.concatenate([cols[lo:mid], cols[KV + lo:KV + mid]], axis=1)
            values_t[level] = jnp.concatenate([cols[mid:hi], cols[KV + mid:KV + hi]], axis=1)
        inside = [None, lane % SPAN2 == phase2[h], lane % SPAN3 == phase3[h]]
        for b in range(2):
            at = slice(b * TOK, (b + 1) * TOK)
            keys[0], values[0] = proj[b, :, lo:mid], proj[b, :, mid:hi]
            keys_t[0], values_t[0] = local_t[b][lo:mid], local_t[b][mid:hi]
            q = proj[b, :, KV + HD * h:KV + HD * (h + 1)]
            d = proj[b, :, ALL + HD * h:ALL + HD * (h + 1)]
            d_t = dat_t[hr, at]
            scores = []
            top = None
            for level in range(3):
                k = keys[level]
                keep = k[:, 0:1].astype(F32) < MARK_TEST
                if level:
                    keep = keep & inside[level]
                s = jnp.where(keep, nt(k, q) * factor, LOW)
                peak = jnp.max(s, axis=0, keepdims=True)
                top = peak if top is None else jnp.maximum(top, peak)
                scores.append(s)
            weights = [jnp.exp(s - top) for s in scores]
            den = sum(jnp.sum(w, axis=0, keepdims=True) for w in weights)
            num = sum(nn(values_t[level], weights[level].astype(BF)) for level in range(3))
            inv = 1.0 / den
            att = (num * inv).astype(BF)
            att_t[hr, at] = att
            delta = jnp.sum(d_t.astype(F32) * att.astype(F32), axis=0, keepdims=True)
            dq = None
            for level in range(3):
                normed = weights[level] * inv
                grad = (normed * (nn(values[level], d_t) - delta)).astype(BF)
                dq_part = nn(keys_t[level], grad)
                dq = dq_part if dq is None else dq + dq_part
                dk = nn(grad, q) * factor
                dv = nn(normed.astype(BF), d)
                if level == 0:
                    own[b, :, lo:mid] = dk
                    own[b, :, mid:hi] = dv
                elif b == 0:
                    far_grads[level] = (dk, dv)
                else:
                    dk, dv = dk + far_grads[level][0], dv + far_grads[level][1]
                    to, n = (g2, PAIR) if level == 1 else (g3, ZN)
                    for part in range(2):
                        pick = slice(part * 2 * TOK // 4, (part + 1) * 2 * TOK // 4)
                        put = part * KV
                        to[:, :, put + lo:put + mid] = dk[pick].astype(BF).reshape(n, -1, HD)
                        to[:, :, put + mid:put + hi] = dv[pick].astype(BF).reshape(n, -1, HD)
            dq_t[hr, at] = (dq * factor).astype(BF)

    b_copies = [send(g2.at[1 - pos2], r2.at[pos2], b2s, b2r, place(x, y, mate, core))]
    for d, zi in enumerate(z_peers):
        b_copies.append(send(g3.at[zi], r3.at[z], b3s.at[d], b3r.at[d], place(x, y, zi, core)))
    r2[pos2] = g2[pos2]
    r3[z] = g3[z]

    def pack(i, col, block):
        width = block.shape[1]
        block = block.astype(BF).reshape(xn, yn, plan.xrows, width)
        for yi in range(yn):
            xs[i, :, :, yi * KV + col:yi * KV + col + width] = block[:, yi]

    def start_x(i):
        return [send(xs.at[i, xi], xr.at[i, d], xss.at[i, d], xrs.at[i, d], place(xi, y, z, core))
                for d, xi in enumerate(x_peers)]

    def start_z(i, copies):
        total = xs[i, x].astype(F32)
        for d, copy in enumerate(copies):
            copy.wait_recv()
            total = total + xr[i, d].astype(F32)
        zs[i] = total.astype(BF).reshape(ZN, plan.chunk, plan.lanes)
        return [send(zs.at[i, zi], zr.at[i, d], zss.at[i, d], zrs.at[i, d], place(x, y, zi, core))
                for d, zi in enumerate(z_peers)]

    def start_y(i, copies):
        total = zs[i, z].astype(F32)
        for d, copy in enumerate(copies):
            copy.wait_recv()
            total = total + zr[i, d].astype(F32)
        ys[i] = total.astype(BF)
        return [send(ys.at[i], yr.at[d, i], yss.at[d, i], yrs.at[d, i], who)
                for d, who in enumerate(y_peers)]

    dq = [nt(eye_b, dq_t[:, b * TOK:(b + 1) * TOK]).astype(BF) for b in range(2)]
    q_out[...] = dq[1]
    q_swap = send(q_out, q_in, ds_.at[0], dr_.at[0], sibling)
    og_swap.wait_recv()
    place_block(og_t, og_in, 1)
    pack(0, 0, nt(og_t[...], att_t[...]))
    tok_swap.wait_recv()
    place_block(tok_t, tok_in, 1)
    pack(0, QW, nt(tok_t[...], dq_t[...]))
    x_first = start_x(0)
    spreads = []
    for h in range(MINE):
        row, col = iota((TOK, TOK), 0), iota((TOK, TOK), 1)
        spreads.append(one_hot(row == jnp.where(
            col < PAIR * ROWS2, (col % ROWS2) * SPAN2 + phase2[h],
            (col % ROWS3) * SPAN3 + phase3[h])))
    for copy in b_copies:
        copy.wait_recv()
    back = jnp.concatenate([r2[...].reshape(PAIR * ROWS2, PAY),
                            r3[...].reshape(ZN * ROWS3, PAY)], axis=0)
    dkv = []
    for b in range(2):
        parts = []
        for h in range(MINE):
            cols = slice(2 * HD * h, 2 * HD * (h + 1))
            got = slice(b * KV + 2 * HD * h, b * KV + 2 * HD * (h + 1))
            parts.append(own[b, :, cols] + nn(spreads[h], back[:, got]))
        dkv.append(jnp.concatenate(parts, axis=1).astype(BF))
    d_out[...] = dkv[1]
    swap = send(d_out, d_in, ds_.at[1], dr_.at[1], sibling)
    pack(1, 0, nn(tok_t[...], jnp.concatenate(dkv, axis=0)))
    x_second = start_x(1)

    shares = nt(wn[0], jnp.concatenate([dkv[0], dq[0]], axis=1))
    q_swap.wait_recv()
    swap.wait_recv()
    shares = shares + nt(wn[1], jnp.concatenate([d_in[...], q_in[...]], axis=1))
    pt[...] = shares.astype(BF).reshape(pt.shape)
    c_copies = []
    for d in range(1, nh):
        to = (head + d) % nh
        c_copies.append(send(pt.at[to], pr.at[d], cs.at[d], cr.at[d], (seq, to)))

    z_first = start_z(0, x_first)
    z_second = start_z(1, x_second)
    y_first = start_y(0, z_first)
    y_second = start_y(1, z_second)

    total = pt[head].astype(F32)
    for d in range(1, nh):
        c_copies[d - 1].wait_recv()
        total = total + pr[d].astype(F32)
    gt_out[...] = total.astype(BF)

    for i, copies in enumerate((y_first, y_second)):
        for copy in copies:
            copy.wait_recv()
        mine = ys[i].astype(F32)
        theirs = yr[0, i].astype(F32)
        if yn > 1:
            mine = mine + yr[1, i].astype(F32)
            theirs = theirs + yr[2, i].astype(F32)
            mine = jnp.where(y == 0, mine[:, :KV], mine[:, KV:])
            theirs = jnp.where(y == 0, theirs[:, :KV], theirs[:, KV:])
        fin[core, :, i * KV:(i + 1) * KV] = mine
        fin[other, :, i * KV:(i + 1) * KV] = theirs
    rows = pl.ds(pl.multiple_of(core * plan.rows_pad, 8), plan.rows_pad)
    done = [fin[c, rows, :][:plan.rows_dev] for c in range(CORES)]
    go_out[...] = jnp.concatenate([f[:, :QW] for f in done], axis=1)
    gw_out[...] = jnp.concatenate(
        [piece for f in done for h in range(MINE)
         for piece in (f[:, QW + HD * h:QW + HD * (h + 1)],
                       f[:, KV + 2 * HD * h:KV + 2 * HD * (h + 1)])], axis=1)
    for copy in started:
        copy.wait_send()


def per_device(plan, tokens, valid, offsets, qkv_weight, out_weight, out_grad):
    vm = pl.BlockSpec(memory_space=pltpu.VMEM)
    sm = pl.BlockSpec(memory_space=pltpu.SMEM)
    dma = pltpu.SemaphoreType.DMA
    xn, rows, lanes = plan.xn, plan.rows, plan.lanes
    near, wide = pltpu.VMEM((PAIR, ROWS2, PAY), BF), pltpu.VMEM((ZN, ROWS3, PAY), BF)
    scratch = [
        pltpu.VMEM((TOK, ALL + QW), BF),
        pltpu.VMEM((TOK, D), BF),
        pltpu.VMEM((TOK, D), BF),
        pltpu.VMEM((2, TOK, ALL + QW), BF),
        near, wide, near, wide, near, wide,
        pltpu.VMEM((2, TOK, KV), F32),
        pltpu.VMEM((QW, 2 * TOK), BF),
        pltpu.VMEM((QW, 2 * TOK), BF),
        pltpu.VMEM((QW, 2 * TOK), BF),
        pltpu.VMEM((rows, 2 * TOK), BF),
        pltpu.VMEM((rows, 2 * TOK), BF),
        pltpu.VMEM((2, D, ALL), BF),
        pltpu.VMEM((TOK, KV), BF),
        pltpu.VMEM((TOK, KV), BF),
        pltpu.VMEM((TOK, QW), BF),
        pltpu.VMEM((TOK, QW), BF),
        pltpu.VMEM((2, xn, plan.xrows, lanes), BF),
        pltpu.VMEM((2, xn, plan.xrows, lanes), BF),
        pltpu.VMEM((2, ZN, plan.chunk, lanes), BF),
        pltpu.VMEM((2, ZN, plan.chunk, lanes), BF),
        pltpu.VMEM((2, plan.chunk, lanes), BF),
        pltpu.VMEM((3, 2, plan.chunk, lanes), BF),
        pltpu.VMEM((2, plan.chunk, 2 * KV), F32),
        pltpu.VMEM((4, D // 4, TOK), BF),
        pltpu.VMEM((4, D // 4, TOK), BF),
        dma((3,)), dma((3,)), dma, dma, dma((ZN,)), dma((ZN,)),
        dma, dma, dma((ZN,)), dma((ZN,)), dma((2,)), dma((2,)), dma((4,)), dma((4,)),
        dma((2, 4)), dma((2, 4)), dma((2, ZN)), dma((2, ZN)), dma((3, 2)), dma((3, 2)),
    ]
    gt, gw, go = pl.pallas_call(
        functools.partial(body, plan),
        out_shape=(
            jax.ShapeDtypeStruct((D // 4, TOK), BF),
            jax.ShapeDtypeStruct((plan.rows_dev, HEADS * 3 * HD), F32),
            jax.ShapeDtypeStruct((plan.rows_dev, HEADS * HD), F32),
        ),
        in_specs=[sm] + [vm] * 5,
        out_specs=(vm, vm, vm),
        scratch_shapes=scratch,
        compiler_params=pltpu.CompilerParams(
            collective_id=0, has_side_effects=True, vmem_limit_bytes=48 * 1024 * 1024),
        cost_estimate=pl.CostEstimate(flops=2_000_000_000, bytes_accessed=4_000_000,
                                      transcendentals=800_000),
    )(offsets.T, valid.reshape(1, TOK), tokens, qkv_weight.T, out_weight, out_grad)
    return gt.T, gw, go.T


def solution(mesh):
    plan = Plan(mesh.shape["seq"], mesh.shape["head"])
    return jax.shard_map(
        functools.partial(per_device, plan),
        mesh=mesh,
        in_specs=(
            P("seq", None),
            P("seq"),
            P("head", None),
            P(None, "head"),
            P("head", None),
            P("seq", None),
        ),
        out_specs=(P("seq", "head"), P("seq", "head"), P("head", "seq")),
        check_vma=False,
    )
```

```python
import functools
import math

import jax
import jax.numpy as jnp
from jax import lax
from jax.experimental import pallas as pl
from jax.experimental.pallas import tpu as pltpu
from jax.sharding import PartitionSpec as P

BF = jnp.bfloat16
F32 = jnp.float32
MESH = pl.DeviceIdType.MESH

HEADS = 4
HD = 48
TOK = 256
D = 768
CORES = 2
MINE = HEADS // CORES
KV = 2 * HD * MINE
QW = HD * MINE
ALL = KV + QW
PAY = CORES * KV
ZN = 8
PAIR = 2
SPAN2 = 4
SPAN3 = 16
ROWS2 = TOK // SPAN2
ROWS3 = TOK // SPAN3
PICKED = ROWS2 + ROWS3
FAR_FIRST = (4, 3, 5, 2, 6, 1, 7)
MARK = 2.0**100
MARK_TEST = 2.0**90
LOW = -1e30
VMEM_BYTES = 58 * 1024 * 1024


def nn(a, b):
    return lax.dot_general(a, b, (((1,), (0,)), ((), ())), preferred_element_type=F32)


def nt(a, b):
    return lax.dot_general(a, b, (((1,), (1,)), ((), ())), preferred_element_type=F32)


def iota(shape, dim):
    return lax.broadcasted_iota(jnp.int32, shape, dim)


def one_hot(mask):
    return jnp.where(mask, 1.0, 0.0).astype(BF)


def thirds(x):
    high = x.astype(BF).astype(F32)
    mid = (x - high).astype(BF).astype(F32)
    return [high, mid, (x - high - mid).astype(BF).astype(F32)]


def stack_rows(rows):
    at = iota((16, rows[0].shape[1]), 0)
    out = jnp.zeros(at.shape, F32)
    for i, row in enumerate(rows):
        out = jnp.where(at == i, row, out)
    return out.astype(BF)


def halves(x):
    high = x.astype(BF)
    return [high, (x - high.astype(F32)).astype(BF)]


class Plan:
    def __init__(self, n_seq, n_head):
        self.n_head = n_head
        self.yn = 2 if n_seq >= 32 else 1
        self.xn = n_seq // (CORES * ZN * self.yn)
        self.rows_dev = D // n_seq
        self.rows_pad = -(-self.rows_dev // 8) * 8
        self.chunk = CORES * self.rows_pad
        self.rows = (n_seq // CORES) * self.chunk
        self.xrows = ZN * self.chunk
        self.lanes = self.yn * KV


def body(plan, offs_h, valid_h, tokens_h, wqkv_h, wout_h, ograd_h, gt_out, gw_out, go_out,
         offs, valid, tokens, wqkv, wout, ograd,
         p_out, s2, s3, tok_in, og_in, proj, w_loc, p_loc, kv2, kv3, g2, g3, r2, r3, own, att_t, dq_t,
         dat_t, tok_t, og_t, wn, d_out, d_in, q_out, q_in,
         xs, xr, zs, zr, ys, yr, fin, pt, pr,
         ls, es, er, a2s, a2r, a3s, a3r, b2s, b2r, b3s, b3r, ds_, dr_, cs, cr,
         xss, xrs, zss, zrs, yss, yrs):
    xn, yn, nh = plan.xn, plan.yn, plan.n_head
    factor = 1.0 / math.sqrt(HD)
    seq = lax.axis_index("seq")
    head = lax.axis_index("head")
    core = seq % CORES
    other = 1 - core
    z = (seq // CORES) % ZN
    y = (seq // (CORES * ZN)) % yn
    x = seq // (CORES * ZN * yn)

    def place(xi, yi, zi, ci):
        return (((xi * yn + yi) * ZN + zi) * CORES + ci, head)

    near_z = z % PAIR
    mate = z - near_z + 1 - near_z
    pos2 = near_z * CORES
    pos3 = z * CORES
    sibling = place(x, y, z, other)
    z_peers = {d: (z + d) % ZN for d in FAR_FIRST}
    x_peers = {d: (x + d) % xn for d in (2, 1, 3) if d < xn}
    h_peers = {d: (head + d) % nh for d in (2, 1, 3) if d < nh}
    far = (y + 1) % yn
    y_peers = [sibling]
    if yn > 1:
        y_peers += [place(x, far, z, core), place(x, far, z, other)]

    loads = []

    def load(src, dst):
        copy = pltpu.make_async_copy(src, dst, ls.at[len(loads)])
        copy.start()
        loads.append(copy)
        return copy

    def load_rows(src, dst, base, rows, pieces):
        size = rows // pieces
        return [load(src.at[at], dst.at[at]) for at in
                [pl.ds(pl.multiple_of(base + size * i, 16), size) for i in range(pieces)]]

    w_rows = MINE * 3 * HD
    need_first = [load(valid_h, valid), load(offs_h, offs)]
    need_first += load_rows(tokens_h, tokens, 0, TOK, 2)
    need_first += load_rows(wqkv_h, wqkv, 0, CORES * w_rows, 4)
    need_then = load_rows(ograd_h, ograd, 0, TOK, 2)
    need_then += load_rows(wout_h, wout, 0, CORES * QW, 1)

    barrier = pltpu.get_barrier_semaphore()
    greeted = [place(x, y, zi, c) for zi in z_peers.values() for c in (core, other)] + y_peers
    greeted += [place(xi, y, z, core) for xi in x_peers.values()]
    greeted += [(seq, to) for to in h_peers.values()]
    for who in greeted:
        pl.semaphore_signal(barrier, inc=1, device_id=who, device_id_type=MESH)

    started = []

    def send(src, dst, ssem, rsem, who):
        copy = pltpu.make_async_remote_copy(
            src_ref=src, dst_ref=dst, send_sem=ssem, recv_sem=rsem,
            device_id=who, device_id_type=MESH)
        copy.start()
        started.append(copy)
        return copy

    def qkv_of(c):
        base = c * w_rows
        rows = [wqkv[pl.ds(pl.multiple_of(base + 3 * HD * h + HD, 16), 2 * HD), :]
                for h in range(MINE)]
        rows += [wqkv[pl.ds(pl.multiple_of(base + 3 * HD * h, 16), HD), :]
                 for h in range(MINE)]
        return jnp.concatenate(rows, axis=0)

    def out_of(c):
        return wout[pl.ds(pl.multiple_of(c * QW, 16), QW), :]

    eye = iota((TOK, TOK), 0) == iota((TOK, TOK), 1)
    eye_b = one_hot(eye)
    lane = iota((TOK, ALL), 1)
    can_mark = (lane % (2 * HD) == 0) & (lane < KV)
    for copy in need_first:
        copy.wait()
    alive = jnp.sum(jnp.where(eye, valid[...].astype(F32), 0.0), axis=1, keepdims=True)
    marked = can_mark & (alive == 0.0)
    w_mine, w_other = qkv_of(core), qkv_of(other)
    proj[0, :, :ALL] = jnp.where(marked, MARK, nt(tokens[...], w_mine)).astype(BF)
    p_out[:, :ALL] = jnp.where(marked, MARK, nt(tokens[...], w_other)).astype(BF)

    def pick_of(g):
        rows = iota((PICKED, TOK), 0)
        want = jnp.where(rows < ROWS2, rows * SPAN2 + offs[0, g],
                         (rows - ROWS2) * SPAN3 + offs[1, g])
        return one_hot(iota((PICKED, TOK), 1) == want)

    picks = [pick_of(core * MINE + h) for h in range(MINE)]
    for h in range(MINE):
        cols = slice(2 * HD * h, 2 * HD * (h + 1))
        chosen = nn(picks[h], proj[0, :, cols]).astype(BF)
        kv2[pos2, :, cols] = chosen[:ROWS2]
        kv3[pos3, :, cols] = chosen[ROWS2:]
        chosen = nn(pick_of(other * MINE + h), p_out[:, cols]).astype(BF)
        s2[:, cols] = chosen[:ROWS2]
        s3[:, cols] = chosen[ROWS2:]

    pl.semaphore_wait(barrier, len(greeted))
    a_copies = []

    def spread_out(d, zi, c, same):
        if d in (0, 4):
            to = mate if d else z
            a_copies.append(send(kv2.at[pos2] if same else s2, kv2.at[pos2 + 1 - same],
                                 a2s.at[d // 4, same], a2r.at[d // 4, same], place(x, y, to, c)))
        a_copies.append(send(kv3.at[pos3] if same else s3, kv3.at[pos3 + 1 - same],
                             a3s.at[d, same], a3r.at[d, same], place(x, y, zi, c)))

    for d, zi in z_peers.items():
        spread_out(d, zi, core, 1)
        spread_out(d, zi, other, 0)
    spread_out(0, z, other, 0)

    for copy in need_then:
        copy.wait()
    p_out[:, ALL:] = nt(ograd[...], out_of(other)).astype(BF)
    swap = send(p_out, proj.at[1], es.at[0], er.at[0], sibling)
    tok_swap = send(tokens, tok_in, es.at[1], er.at[1], sibling)
    og_swap = send(ograd, og_in, es.at[2], er.at[2], sibling)

    phase2 = [offs[0, core * MINE + h] for h in range(MINE)]
    phase3 = [offs[1, core * MINE + h] for h in range(MINE)]
    proj[0, :, ALL:] = nt(ograd[...], out_of(core)).astype(BF)
    dat_t[:, :TOK] = nt(out_of(core), ograd[...]).astype(BF)
    swap.wait_recv()
    dat_t[:, TOK:] = nt(eye_b[:QW, :QW], proj[1, :, ALL:]).astype(BF)
    eye_kv = one_hot(iota((KV, KV), 0) == iota((KV, KV), 1))
    local_t = [nt(eye_kv, proj[b, :, :KV]).astype(BF) for b in range(2)]
    spots = []
    for h in range(MINE):
        zero2, zero3 = jnp.zeros((ROWS2, TOK), BF), jnp.zeros((ROWS3, TOK), BF)
        one2, one3 = picks[h][:ROWS2], picks[h][ROWS2:]
        spots.append([
            jnp.concatenate([jnp.concatenate([one, zero], axis=1),
                             jnp.concatenate([zero, one], axis=1)], axis=0)
            for one, zero in ((one2, zero2), (one3, zero3))])

    def columns(h):
        return (slice(2 * HD * h, 2 * HD * h + HD), slice(2 * HD * h + HD, 2 * HD * (h + 1)),
                slice(KV + HD * h, KV + HD * (h + 1)), slice(ALL + HD * h, ALL + HD * (h + 1)))

    def soft(k, q):
        keep = k[:, 0:1].astype(F32) < MARK_TEST
        s = jnp.where(keep, nt(k, q) * factor, LOW)
        peak = jnp.max(s, axis=0, keepdims=True)
        w = jnp.exp(s - peak)
        return peak, w, jnp.sum(w, axis=0, keepdims=True)

    local = []
    few = []
    for h in range(MINE):
        kc, vc, qc, dc = columns(h)
        parts = []
        for b in range(2):
            peak, w, den = soft(proj[b, :, kc], proj[b, :, qc])
            w_loc[h, b] = w
            p_loc[h, b] = nt(proj[b, :, vc], proj[b, :, dc])
            parts.append((peak, den, nn(local_t[b][vc, :], w.astype(BF))))
        local.append([jnp.concatenate([parts[0][i], parts[1][i]], axis=1) for i in range(3)])
        chosen = [[nn(picks[h], proj[b, :, c]).astype(BF) for b in range(2)] for c in (qc, dc)]
        few.append([[jnp.concatenate([pair[0][at], pair[1][at]], axis=0) for pair in chosen]
                    for at in (slice(0, ROWS2), slice(ROWS2, PICKED))])

    half = plan.rows // 2
    rr = iota((half, 1), 0)
    inner = rr % plan.chunk
    j = inner % plan.rows_pad
    source = jnp.where(
        j < plan.rows_dev,
        ((rr // plan.chunk) * CORES + inner // plan.rows_pad) * plan.rows_dev + j, -1)
    place_rows = one_hot(iota((half, D // 2), 1) == source)

    def place_block(to, block, b):
        for part in range(2):
            cols = slice(part * D // 2, (part + 1) * D // 2)
            to[part * half:(part + 1) * half, b * TOK:(b + 1) * TOK] = nt(
                place_rows, block[:, cols]).astype(BF)

    place_block(tok_t, tokens, 0)
    place_block(og_t, ograd, 0)
    eye_d = one_hot(iota((D, D), 0) == iota((D, D), 1))
    wn[0] = nt(eye_d, w_mine).astype(BF)
    wn[1] = nt(eye_d, w_other).astype(BF)

    for copy in a_copies:
        copy.wait_recv()

    lane = iota((1, 2 * TOK), 1)
    rows_far = [kv2[...].reshape(TOK, KV), kv3[...].reshape(TOK, KV)]
    cols_far = [nt(eye_kv, r).astype(BF) for r in rows_far]
    scale_loc, delta_loc, dq_far = [], [], []
    for h in range(MINE):
        kc, vc, _, _ = columns(h)
        inside = [lane % SPAN2 == phase2[h], lane % SPAN3 == phase3[h]]
        peaks, dens, nums, far_w = [local[h][0]], [local[h][1]], [local[h][2]], []
        for level in range(2):
            peak, w, den = soft(rows_far[level][:, kc], few[h][level][0])
            num = nn(cols_far[level][vc, :], w.astype(BF))
            got = nn(jnp.concatenate([stack_rows(thirds(peak) + thirds(den))] + halves(num), axis=0),
                     spots[h][level])
            peaks.append(jnp.where(inside[level], got[0:1] + got[1:2] + got[2:3], LOW))
            dens.append(got[3:4] + got[4:5] + got[5:6])
            nums.append(got[16:16 + HD] + got[16 + HD:16 + 2 * HD])
            far_w.append(w)
        top = jnp.maximum(jnp.maximum(peaks[0], peaks[1]), peaks[2])
        scales = [jnp.exp(peak - top) for peak in peaks]
        inv = 1.0 / sum(scale * den for scale, den in zip(scales, dens))
        att = (sum(scale * num for scale, num in zip(scales, nums)) * inv).astype(BF)
        hr = slice(HD * h, HD * (h + 1))
        att_t[hr, :] = att
        delta = jnp.sum(dat_t[hr, :].astype(F32) * att.astype(F32), axis=0, keepdims=True)
        scale_loc.append(scales[0] * inv)
        delta_loc.append(delta)
        wanted = stack_rows(thirds(scales[1] * inv) + thirds(scales[2] * inv) + thirds(delta))
        dq = None
        for level, (to, n) in enumerate(((g2, PAIR), (g3, ZN))):
            got = nt(wanted, spots[h][level])
            i = 3 * level
            scale = got[i:i + 1] + got[i + 1:i + 2] + got[i + 2:i + 3]
            delta_few = got[6:7] + got[7:8] + got[8:9]
            normed = far_w[level] * scale
            q, d = few[h][level]
            grad = (normed * (nt(rows_far[level][:, vc], d) - delta_few)).astype(BF)
            dk = (nn(grad, q) * factor).astype(BF).reshape(n, CORES, -1, HD)
            dv = nn(normed.astype(BF), d).astype(BF).reshape(n, CORES, -1, HD)
            for part in range(CORES):
                put = part * KV
                to[:, :, put + kc.start:put + kc.stop] = dk[:, part]
                to[:, :, put + vc.start:put + vc.stop] = dv[:, part]
            back = nn(jnp.concatenate(halves(nn(cols_far[level][kc, :], grad)), axis=0),
                      spots[h][level])
            part = back[:HD] + back[HD:]
            dq = part if dq is None else dq + part
        dq_far.append(dq)

    b_copies = []
    for d, zi in z_peers.items():
        b_copies.append(send(g3.at[zi], r3.at[z], b3s.at[d], b3r.at[d], place(x, y, zi, core)))
        if d == 4:
            b_copies.append(send(g2.at[1 - near_z], r2.at[near_z], b2s, b2r,
                                 place(x, y, mate, core)))
    r2[near_z] = g2[near_z]
    r3[z] = g3[z]

    for h in range(MINE):
        kc, vc, qc, dc = columns(h)
        for b in range(2):
            at = slice(b * TOK, (b + 1) * TOK)
            normed = w_loc[h, b] * scale_loc[h][:, at]
            grad = (normed * (p_loc[h, b] - delta_loc[h][:, at])).astype(BF)
            own[b, :, kc] = nn(grad, proj[b, :, qc]) * factor
            own[b, :, vc] = nn(normed.astype(BF), proj[b, :, dc])
            dq = nn(local_t[b][kc, :], grad) + dq_far[h][:, at]
            dq_t[HD * h:HD * (h + 1), at] = (dq * factor).astype(BF)

    def pack(i, col, block):
        width = block.shape[1]
        block = block.astype(BF).reshape(xn, yn, plan.xrows, width)
        for yi in range(yn):
            xs[i, :, :, yi * KV + col:yi * KV + col + width] = block[:, yi]

    def parts_of(i):
        count = 2 if i else 1
        size = plan.xrows // count
        return [(k, pl.ds(k * size, size)) for k in range(count)]

    def start_x(i):
        return [[send(xs.at[i, xi, at], xr.at[i, d, at], xss.at[i, k, d], xrs.at[i, k, d],
                      place(xi, y, z, core)) for d, xi in x_peers.items()]
                for k, at in parts_of(i)]

    def start_z(i, copies):
        parts = parts_of(i)
        deep = ZN // len(parts)
        flying = {}
        for (k, at), some in zip(parts, copies):
            total = xs[i, x, at].astype(F32)
            for d, copy in zip(x_peers, some):
                copy.wait_recv()
                total = total + xr[i, d, at].astype(F32)
            zs[i, k * deep:(k + 1) * deep] = total.astype(BF).reshape(
                deep, plan.chunk, plan.lanes)
            for d, zi in z_peers.items():
                copy = pltpu.make_async_remote_copy(
                    src_ref=zs.at[i, zi], dst_ref=zr.at[i, d], send_sem=zss.at[i, d],
                    recv_sem=zrs.at[i, d], device_id=place(x, y, zi, core),
                    device_id_type=MESH)
                flying[d] = copy
                if len(parts) == 1:
                    copy.start()
                else:
                    pl.when(zi // deep == k)(copy.start)
        started.extend(flying.values())
        return flying

    def start_y(i, copies):
        total = zs[i, z].astype(F32)
        for d, copy in copies.items():
            copy.wait_recv()
            total = total + zr[i, d].astype(F32)
        ys[i] = total.astype(BF)
        return [send(ys.at[i], yr.at[d, i], yss.at[d, i], yrs.at[d, i], who)
                for d, who in enumerate(y_peers)]

    dq = [nt(eye_b, dq_t[:, b * TOK:(b + 1) * TOK]).astype(BF) for b in range(2)]
    q_out[...] = dq[1]
    q_swap = send(q_out, q_in, ds_.at[0], dr_.at[0], sibling)
    og_swap.wait_recv()
    place_block(og_t, og_in, 1)
    pack(0, 0, nt(og_t[...], att_t[...]))
    tok_swap.wait_recv()
    place_block(tok_t, tok_in, 1)
    pack(0, QW, nt(tok_t[...], dq_t[...]))
    x_first = start_x(0)
    spreads = []
    for h in range(MINE):
        row, col = iota((TOK, TOK), 0), iota((TOK, TOK), 1)
        spreads.append(one_hot(row == jnp.where(
            col < PAIR * ROWS2, (col % ROWS2) * SPAN2 + phase2[h],
            (col % ROWS3) * SPAN3 + phase3[h])))
    for copy in b_copies:
        copy.wait_recv()
    back = jnp.concatenate([r2[...].reshape(PAIR * ROWS2, PAY),
                            r3[...].reshape(ZN * ROWS3, PAY)], axis=0)

    def finish(b):
        parts = []
        for h in range(MINE):
            cols = slice(2 * HD * h, 2 * HD * (h + 1))
            got = slice(b * KV + 2 * HD * h, b * KV + 2 * HD * (h + 1))
            parts.append(own[b, :, cols] + nn(spreads[h], back[:, got]))
        return jnp.concatenate(parts, axis=1).astype(BF)

    theirs = finish(1)
    d_out[...] = theirs
    swap = send(d_out, d_in, ds_.at[1], dr_.at[1], sibling)
    mine = finish(0)
    pack(1, 0, nn(tok_t[...], jnp.concatenate([mine, theirs], axis=0)))
    x_second = start_x(1)

    shares = nt(wn[0], jnp.concatenate([mine, dq[0]], axis=1))
    q_swap.wait_recv()
    swap.wait_recv()
    shares = shares + nt(wn[1], jnp.concatenate([d_in[...], q_in[...]], axis=1))
    pt[...] = shares.astype(BF).reshape(pt.shape)
    c_copies = []
    for d, to in h_peers.items():
        c_copies.append(send(pt.at[to], pr.at[d], cs.at[d], cr.at[d], (seq, to)))

    z_first = start_z(0, x_first)
    z_second = start_z(1, x_second)
    y_first = start_y(0, z_first)
    y_second = start_y(1, z_second)

    total = pt[head].astype(F32)
    for d, copy in zip(h_peers, c_copies):
        copy.wait_recv()
        total = total + pr[d].astype(F32)
    gt_out[...] = total.astype(BF)

    for i, copies in enumerate((y_first, y_second)):
        for copy in copies:
            copy.wait_recv()
        mine = ys[i].astype(F32)
        theirs = yr[0, i].astype(F32)
        if yn > 1:
            mine = mine + yr[1, i].astype(F32)
            theirs = theirs + yr[2, i].astype(F32)
            mine = jnp.where(y == 0, mine[:, :KV], mine[:, KV:])
            theirs = jnp.where(y == 0, theirs[:, :KV], theirs[:, KV:])
        fin[core, :, i * KV:(i + 1) * KV] = mine
        fin[other, :, i * KV:(i + 1) * KV] = theirs
    rows = pl.ds(pl.multiple_of(core * plan.rows_pad, 8), plan.rows_pad)
    done = [fin[c, rows, :][:plan.rows_dev] for c in range(CORES)]
    go_out[...] = jnp.concatenate([f[:, :QW] for f in done], axis=1)
    gw_out[...] = jnp.concatenate(
        [piece for f in done for h in range(MINE)
         for piece in (f[:, QW + HD * h:QW + HD * (h + 1)],
                       f[:, KV + 2 * HD * h:KV + 2 * HD * (h + 1)])], axis=1)
    for copy in started:
        copy.wait_send()


def write_out(gt, gw, go, gt_out, gw_out, go_out, sems):
    copies = [pltpu.make_async_copy(a, b, sems.at[i]) for i, (a, b) in enumerate(
        ((gt, gt_out), (gw, gw_out), (go, go_out)))]
    for copy in copies:
        copy.start()
    for copy in copies:
        copy.wait()


def per_device(plan, tokens, valid, offsets, qkv_weight, out_weight, out_grad):
    vm = pl.BlockSpec(memory_space=pltpu.VMEM)
    hbm = pl.BlockSpec(memory_space=pltpu.HBM)
    dma = pltpu.SemaphoreType.DMA
    xn, rows, lanes = plan.xn, plan.rows, plan.lanes
    near, wide = pltpu.VMEM((PAIR, ROWS2, PAY), BF), pltpu.VMEM((ZN, ROWS3, PAY), BF)
    square = pltpu.VMEM((MINE, 2, TOK, TOK), F32)
    scratch = [
        pltpu.SMEM((2, HEADS), jnp.int32),
        pltpu.VMEM((1, TOK), jnp.int32),
        pltpu.VMEM((TOK, D), BF),
        pltpu.VMEM((HEADS * 3 * HD, D), BF),
        pltpu.VMEM((HEADS * HD, D), BF),
        pltpu.VMEM((TOK, D), BF),
        pltpu.VMEM((TOK, ALL + QW), BF),
        pltpu.VMEM((ROWS2, KV), BF),
        pltpu.VMEM((ROWS3, KV), BF),
        pltpu.VMEM((TOK, D), BF),
        pltpu.VMEM((TOK, D), BF),
        pltpu.VMEM((2, TOK, ALL + QW), BF),
        square, square,
        pltpu.VMEM((PAIR * CORES, ROWS2, KV), BF),
        pltpu.VMEM((ZN * CORES, ROWS3, KV), BF),
        near, wide, near, wide,
        pltpu.VMEM((2, TOK, KV), F32),
        pltpu.VMEM((QW, 2 * TOK), BF),
        pltpu.VMEM((QW, 2 * TOK), BF),
        pltpu.VMEM((QW, 2 * TOK), BF),
        pltpu.VMEM((rows, 2 * TOK), BF),
        pltpu.VMEM((rows, 2 * TOK), BF),
        pltpu.VMEM((2, D, ALL), BF),
        pltpu.VMEM((TOK, KV), BF),
        pltpu.VMEM((TOK, KV), BF),
        pltpu.VMEM((TOK, QW), BF),
        pltpu.VMEM((TOK, QW), BF),
        pltpu.VMEM((2, xn, plan.xrows, lanes), BF),
        pltpu.VMEM((2, xn, plan.xrows, lanes), BF),
        pltpu.VMEM((2, ZN, plan.chunk, lanes), BF),
        pltpu.VMEM((2, ZN, plan.chunk, lanes), BF),
        pltpu.VMEM((2, plan.chunk, lanes), BF),
        pltpu.VMEM((3, 2, plan.chunk, lanes), BF),
        pltpu.VMEM((2, plan.chunk, 2 * KV), F32),
        pltpu.VMEM((4, D // 4, TOK), BF),
        pltpu.VMEM((4, D // 4, TOK), BF),
        dma((16,)), dma((3,)), dma((3,)),
        dma((2, 2)), dma((2, 2)), dma((ZN, 2)), dma((ZN, 2)),
        dma, dma, dma((ZN,)), dma((ZN,)), dma((2,)), dma((2,)), dma((4,)), dma((4,)),
        dma((2, 2, 4)), dma((2, 2, 4)), dma((2, ZN)), dma((2, ZN)), dma((3, 2)), dma((3, 2)),
    ]
    gt, gw, go = pl.pallas_call(
        functools.partial(body, plan),
        out_shape=(
            jax.ShapeDtypeStruct((D // 4, TOK), BF),
            jax.ShapeDtypeStruct((plan.rows_dev, HEADS * 3 * HD), F32),
            jax.ShapeDtypeStruct((plan.rows_dev, HEADS * HD), F32),
        ),
        in_specs=[hbm] * 6,
        out_specs=(vm, vm, vm),
        scratch_shapes=scratch,
        compiler_params=pltpu.CompilerParams(
            collective_id=0, has_side_effects=True, vmem_limit_bytes=VMEM_BYTES),
        cost_estimate=pl.CostEstimate(flops=2_000_000_000, bytes_accessed=4_000_000,
                                      transcendentals=800_000),
    )(offsets.T, valid.reshape(1, TOK), tokens, qkv_weight.T, out_weight, out_grad)
    hold = pl.pallas_call(
        write_out,
        out_shape=tuple(jax.ShapeDtypeStruct(a.shape, a.dtype) for a in (gt, gw, go)),
        in_specs=[hbm] * 3,
        out_specs=(hbm, hbm, hbm),
        scratch_shapes=[dma((3,))],
        compiler_params=pltpu.CompilerParams(vmem_limit_bytes=VMEM_BYTES),
    )(gt, gw, go)
    return hold[0].T, hold[1], hold[2].T


def solution(mesh):
    plan = Plan(mesh.shape["seq"], mesh.shape["head"])
    return jax.shard_map(
        functools.partial(per_device, plan),
        mesh=mesh,
        in_specs=(
            P("seq", None),
            P("seq"),
            P("head", None),
            P(None, "head"),
            P("head", None),
            P("seq", None),
        ),
        out_specs=(P("seq", "head"), P("seq", "head"), P("head", "seq")),
        check_vma=False,
    )
```

```python
import functools
import math

import jax
import jax.numpy as jnp
from jax import lax
from jax.experimental import pallas as pl
from jax.experimental.pallas import tpu as pltpu
from jax.sharding import PartitionSpec as P

BF = jnp.bfloat16
F32 = jnp.float32
MESH = pl.DeviceIdType.MESH

HEADS = 4
HD = 48
TOK = 256
D = 768
CORES = 2
MINE = HEADS // CORES
KV = 2 * HD * MINE
QW = HD * MINE
ALL = KV + QW
PAY = CORES * KV
ZN = 8
PAIR = 2
SPAN2 = 4
SPAN3 = 16
ROWS2 = TOK // SPAN2
ROWS3 = TOK // SPAN3
PICKED = ROWS2 + ROWS3
FAR_FIRST = (4, 3, 5, 2, 6, 1, 7)
MARK = 2.0**100
MARK_TEST = 2.0**90
LOW = -1e30
VMEM_BYTES = 58 * 1024 * 1024


def nn(a, b):
    return lax.dot_general(a, b, (((1,), (0,)), ((), ())), preferred_element_type=F32)


def nt(a, b):
    return lax.dot_general(a, b, (((1,), (1,)), ((), ())), preferred_element_type=F32)


def iota(shape, dim):
    return lax.broadcasted_iota(jnp.int32, shape, dim)


def one_hot(mask):
    return jnp.where(mask, 1.0, 0.0).astype(BF)


def thirds(x):
    high = x.astype(BF).astype(F32)
    mid = (x - high).astype(BF).astype(F32)
    return [high, mid, (x - high - mid).astype(BF).astype(F32)]


def stack_rows(rows):
    at = iota((16, rows[0].shape[1]), 0)
    out = jnp.zeros(at.shape, F32)
    for i, row in enumerate(rows):
        out = jnp.where(at == i, row, out)
    return out.astype(BF)


def halves(x):
    high = x.astype(BF)
    return [high, (x - high.astype(F32)).astype(BF)]


class Plan:
    def __init__(self, n_seq, n_head):
        self.n_head = n_head
        self.yn = 2 if n_seq >= 32 else 1
        self.xn = n_seq // (CORES * ZN * self.yn)
        self.rows_dev = D // n_seq
        self.rows_chip = CORES * self.rows_dev
        self.chunk = -(-self.rows_chip // 16) * 16
        self.xrows = ZN * self.rows_chip
        self.lanes = self.yn * KV


def body(plan, offs_h, valid_h, tokens_h, wqkv_h, wout_h, ograd_h, gt_out, gw_out, go_out,
         offs, valid, tokens, wqkv, wout, ograd,
         p_out, s2, s3, tok_in, og_in, proj, w_loc, p_loc, kv2, kv3, g2, g3, r2, r3, own, att_t, dq_t,
         dat_t, tok_t, og_t, wn, d_out, d_in, q_out, q_in,
         xs, xr, zs, zr, ys, yr, pt, pr, pv,
         ls, es, er, a2s, a2r, a3s, a3r, b2s, b2r, b3s, b3r, ds_, dr_, cs, cr,
         xss, xrs, zss, zrs, yss, yrs):
    xn, yn, nh = plan.xn, plan.yn, plan.n_head
    factor = 1.0 / math.sqrt(HD)
    seq = lax.axis_index("seq")
    head = lax.axis_index("head")
    core = seq % CORES
    other = 1 - core
    z = (seq // CORES) % ZN
    y = (seq // (CORES * ZN)) % yn
    x = seq // (CORES * ZN * yn)

    def place(xi, yi, zi, ci):
        return (((xi * yn + yi) * ZN + zi) * CORES + ci, head)

    near_z = z % PAIR
    mate = z - near_z + 1 - near_z
    pos2 = near_z * CORES
    pos3 = z * CORES
    sibling = place(x, y, z, other)
    z_peers = {d: (z + d) % ZN for d in FAR_FIRST}
    x_peers = {d: (x + d) % xn for d in (2, 1, 3) if d < xn}
    h_peers = {d: (head + d) % nh for d in (1, 3) if d < nh}
    far = (y + 1) % yn
    y_peers = [sibling]
    if yn > 1:
        y_peers += [place(x, far, z, core), place(x, far, z, other)]

    loads = []

    def load(src, dst):
        copy = pltpu.make_async_copy(src, dst, ls.at[len(loads)])
        copy.start()
        loads.append(copy)
        return copy

    def load_rows(src, dst, base, rows, pieces):
        size = rows // pieces
        return [load(src.at[at], dst.at[at]) for at in
                [pl.ds(pl.multiple_of(base + size * i, 16), size) for i in range(pieces)]]

    w_rows = MINE * 3 * HD
    need_first = [load(valid_h, valid), load(offs_h, offs)]
    need_first += load_rows(tokens_h, tokens, 0, TOK, 2)
    need_first += load_rows(wqkv_h, wqkv, 0, CORES * w_rows, 4)
    need_then = load_rows(ograd_h, ograd, 0, TOK, 2)
    need_then += load_rows(wout_h, wout, 0, CORES * QW, 1)

    barrier = pltpu.get_barrier_semaphore()
    greeted = [place(x, y, zi, c) for zi in z_peers.values() for c in (core, other)] + y_peers
    greeted += [place(xi, y, z, core) for xi in x_peers.values()]
    greeted += [(seq, to) for to in h_peers.values()]
    for who in greeted:
        pl.semaphore_signal(barrier, inc=1, device_id=who, device_id_type=MESH)

    started = []

    def send(src, dst, ssem, rsem, who):
        copy = pltpu.make_async_remote_copy(
            src_ref=src, dst_ref=dst, send_sem=ssem, recv_sem=rsem,
            device_id=who, device_id_type=MESH)
        copy.start()
        started.append(copy)
        return copy

    def qkv_of(c):
        base = c * w_rows
        rows = [wqkv[pl.ds(pl.multiple_of(base + 3 * HD * h + HD, 16), 2 * HD), :]
                for h in range(MINE)]
        rows += [wqkv[pl.ds(pl.multiple_of(base + 3 * HD * h, 16), HD), :]
                 for h in range(MINE)]
        return jnp.concatenate(rows, axis=0)

    def out_of(c):
        return wout[pl.ds(pl.multiple_of(c * QW, 16), QW), :]

    eye = iota((TOK, TOK), 0) == iota((TOK, TOK), 1)
    eye_b = one_hot(eye)
    lane = iota((TOK, ALL), 1)
    can_mark = (lane % (2 * HD) == 0) & (lane < KV)
    for copy in need_first:
        copy.wait()
    alive = jnp.sum(jnp.where(eye, valid[...].astype(F32), 0.0), axis=1, keepdims=True)
    marked = can_mark & (alive == 0.0)
    w_mine, w_other = qkv_of(core), qkv_of(other)
    proj[0, :, :ALL] = jnp.where(marked, MARK, nt(tokens[...], w_mine)).astype(BF)
    p_out[:, :ALL] = jnp.where(marked, MARK, nt(tokens[...], w_other)).astype(BF)

    def pick_of(g):
        rows = iota((PICKED, TOK), 0)
        want = jnp.where(rows < ROWS2, rows * SPAN2 + offs[0, g],
                         (rows - ROWS2) * SPAN3 + offs[1, g])
        return one_hot(iota((PICKED, TOK), 1) == want)

    picks = [pick_of(core * MINE + h) for h in range(MINE)]
    for h in range(MINE):
        cols = slice(2 * HD * h, 2 * HD * (h + 1))
        chosen = nn(picks[h], proj[0, :, cols]).astype(BF)
        kv2[pos2, :, cols] = chosen[:ROWS2]
        kv3[pos3, :, cols] = chosen[ROWS2:]
        chosen = nn(pick_of(other * MINE + h), p_out[:, cols]).astype(BF)
        s2[:, cols] = chosen[:ROWS2]
        s3[:, cols] = chosen[ROWS2:]

    pl.semaphore_wait(barrier, len(greeted))
    a_copies = []

    def give(source, other_source, to, sems, at, slot, zi, c):
        same = 0 if c is other else 1
        a_copies.append(send(source if same else other_source, to.at[slot + 1 - same],
                             sems[0].at[at, same], sems[1].at[at, same], place(x, y, zi, c)))

    for d, zi in z_peers.items():
        for c in (core, other):
            give(kv3.at[pos3], s3, kv3, (a3s, a3r), d, pos3, zi, c)
    for c in (core, other):
        give(kv2.at[pos2], s2, kv2, (a2s, a2r), 1, pos2, mate, c)
    give(kv3.at[pos3], s3, kv3, (a3s, a3r), 0, pos3, z, other)
    give(kv2.at[pos2], s2, kv2, (a2s, a2r), 0, pos2, z, other)

    for copy in need_then:
        copy.wait()
    p_out[:, ALL:] = nt(ograd[...], out_of(other)).astype(BF)
    swap = send(p_out, proj.at[1], es.at[0], er.at[0], sibling)
    tok_swap = send(tokens, tok_in, es.at[1], er.at[1], sibling)
    og_swap = send(ograd, og_in, es.at[2], er.at[2], sibling)

    phase2 = [offs[0, core * MINE + h] for h in range(MINE)]
    phase3 = [offs[1, core * MINE + h] for h in range(MINE)]
    proj[0, :, ALL:] = nt(ograd[...], out_of(core)).astype(BF)
    dat_t[:, :TOK] = nt(out_of(core), ograd[...]).astype(BF)
    swap.wait_recv()
    dat_t[:, TOK:] = nt(eye_b[:QW, :QW], proj[1, :, ALL:]).astype(BF)
    eye_kv = one_hot(iota((KV, KV), 0) == iota((KV, KV), 1))
    local_t = [nt(eye_kv, proj[b, :, :KV]).astype(BF) for b in range(2)]
    spots = []
    for h in range(MINE):
        zero2, zero3 = jnp.zeros((ROWS2, TOK), BF), jnp.zeros((ROWS3, TOK), BF)
        one2, one3 = picks[h][:ROWS2], picks[h][ROWS2:]
        spots.append([
            jnp.concatenate([jnp.concatenate([one, zero], axis=1),
                             jnp.concatenate([zero, one], axis=1)], axis=0)
            for one, zero in ((one2, zero2), (one3, zero3))])

    def columns(h):
        return (slice(2 * HD * h, 2 * HD * h + HD), slice(2 * HD * h + HD, 2 * HD * (h + 1)),
                slice(KV + HD * h, KV + HD * (h + 1)), slice(ALL + HD * h, ALL + HD * (h + 1)))

    def soft(k, q):
        keep = k[:, 0:1].astype(F32) < MARK_TEST
        s = jnp.where(keep, nt(k, q) * factor, LOW)
        peak = jnp.max(s, axis=0, keepdims=True)
        w = jnp.exp(s - peak)
        return peak, w, jnp.sum(w, axis=0, keepdims=True)

    local = []
    few = []
    for h in range(MINE):
        kc, vc, qc, dc = columns(h)
        parts = []
        for b in range(2):
            peak, w, den = soft(proj[b, :, kc], proj[b, :, qc])
            w_loc[h, b] = w
            p_loc[h, b] = nt(proj[b, :, vc], proj[b, :, dc])
            parts.append((peak, den, nn(local_t[b][vc, :], w.astype(BF))))
        local.append([jnp.concatenate([parts[0][i], parts[1][i]], axis=1) for i in range(3)])
        chosen = [[nn(picks[h], proj[b, :, c]).astype(BF) for b in range(2)] for c in (qc, dc)]
        few.append([[jnp.concatenate([pair[0][at], pair[1][at]], axis=0) for pair in chosen]
                    for at in (slice(0, ROWS2), slice(ROWS2, PICKED))])

    half = D // 2
    eye_half = one_hot(iota((half, half), 0) == iota((half, half), 1))

    def turn(to, block, b):
        for part in range(2):
            at = slice(part * half, (part + 1) * half)
            to[at, b * TOK:(b + 1) * TOK] = nt(eye_half, block[:, at]).astype(BF)

    turn(tok_t, tokens, 0)
    turn(og_t, ograd, 0)
    eye_d = one_hot(iota((D, D), 0) == iota((D, D), 1))
    wn[0] = nt(eye_d, w_mine).astype(BF)
    wn[1] = nt(eye_d, w_other).astype(BF)

    for copy in a_copies:
        copy.wait_recv()

    lane = iota((1, 2 * TOK), 1)
    rows_far = [kv2[...].reshape(TOK, KV), kv3[...].reshape(TOK, KV)]
    cols_far = [nt(eye_kv, r).astype(BF) for r in rows_far]
    scale_loc, delta_loc, dq_far = [], [], []
    for h in range(MINE):
        kc, vc, _, _ = columns(h)
        inside = [lane % SPAN2 == phase2[h], lane % SPAN3 == phase3[h]]
        peaks, dens, nums, far_w = [local[h][0]], [local[h][1]], [local[h][2]], []
        for level in range(2):
            peak, w, den = soft(rows_far[level][:, kc], few[h][level][0])
            num = nn(cols_far[level][vc, :], w.astype(BF))
            got = nn(jnp.concatenate([stack_rows(thirds(peak) + thirds(den))] + halves(num), axis=0),
                     spots[h][level])
            peaks.append(jnp.where(inside[level], got[0:1] + got[1:2] + got[2:3], LOW))
            dens.append(got[3:4] + got[4:5] + got[5:6])
            nums.append(got[16:16 + HD] + got[16 + HD:16 + 2 * HD])
            far_w.append(w)
        top = jnp.maximum(jnp.maximum(peaks[0], peaks[1]), peaks[2])
        scales = [jnp.exp(peak - top) for peak in peaks]
        inv = 1.0 / sum(scale * den for scale, den in zip(scales, dens))
        att = (sum(scale * num for scale, num in zip(scales, nums)) * inv).astype(BF)
        hr = slice(HD * h, HD * (h + 1))
        att_t[hr, :] = att
        delta = jnp.sum(dat_t[hr, :].astype(F32) * att.astype(F32), axis=0, keepdims=True)
        scale_loc.append(scales[0] * inv)
        delta_loc.append(delta)
        wanted = stack_rows(thirds(scales[1] * inv) + thirds(scales[2] * inv) + thirds(delta))
        dq = None
        for level, (to, n) in enumerate(((g2, PAIR), (g3, ZN))):
            got = nt(wanted, spots[h][level])
            i = 3 * level
            scale = got[i:i + 1] + got[i + 1:i + 2] + got[i + 2:i + 3]
            delta_few = got[6:7] + got[7:8] + got[8:9]
            normed = far_w[level] * scale
            q, d = few[h][level]
            grad = (normed * (nt(rows_far[level][:, vc], d) - delta_few)).astype(BF)
            dk = (nn(grad, q) * factor).astype(BF).reshape(n, CORES, -1, HD)
            dv = nn(normed.astype(BF), d).astype(BF).reshape(n, CORES, -1, HD)
            for part in range(CORES):
                put = part * KV
                to[:, :, put + kc.start:put + kc.stop] = dk[:, part]
                to[:, :, put + vc.start:put + vc.stop] = dv[:, part]
            back = nn(jnp.concatenate(halves(nn(cols_far[level][kc, :], grad)), axis=0),
                      spots[h][level])
            part = back[:HD] + back[HD:]
            dq = part if dq is None else dq + part
        dq_far.append(dq)

    b_copies = []
    for d, zi in z_peers.items():
        b_copies.append(send(g3.at[zi], r3.at[z], b3s.at[d], b3r.at[d], place(x, y, zi, core)))
    b_copies.append(send(g2.at[1 - near_z], r2.at[near_z], b2s, b2r, place(x, y, mate, core)))
    r2[near_z] = g2[near_z]
    r3[z] = g3[z]

    for h in range(MINE):
        kc, vc, qc, dc = columns(h)
        for b in range(2):
            at = slice(b * TOK, (b + 1) * TOK)
            normed = w_loc[h, b] * scale_loc[h][:, at]
            grad = (normed * (p_loc[h, b] - delta_loc[h][:, at])).astype(BF)
            own[b, :, kc] = nn(grad, proj[b, :, qc]) * factor
            own[b, :, vc] = nn(normed.astype(BF), proj[b, :, dc])
            dq = nn(local_t[b][kc, :], grad) + dq_far[h][:, at]
            dq_t[HD * h:HD * (h + 1), at] = (dq * factor).astype(BF)

    def pack(i, col, block):
        width = block.shape[1]
        block = block.astype(BF).reshape(xn, yn, plan.xrows, width)
        for yi in range(yn):
            xs[i, :, :, yi * KV + col:yi * KV + col + width] = block[:, yi]

    def parts_of(i):
        count = 2 if i else 1
        size = plan.xrows // count
        return [(k, pl.ds(k * size, size)) for k in range(count)]

    def start_x(i):
        return [[send(xs.at[i, xi, at], xr.at[i, d, at], xss.at[i, k, d], xrs.at[i, k, d],
                      place(xi, y, z, core)) for d, xi in x_peers.items()]
                for k, at in parts_of(i)]

    def start_z(i, copies, between=None):
        parts = parts_of(i)
        deep = ZN // len(parts)
        flying = {}
        for (k, at), some in zip(parts, copies):
            total = xs[i, x, at].astype(F32)
            for d, copy in zip(x_peers, some):
                copy.wait_recv()
                total = total + xr[i, d, at].astype(F32)
            for j in range(deep):
                rows = total[j * plan.rows_chip:(j + 1) * plan.rows_chip]
                if plan.chunk > plan.rows_chip:
                    rest = jnp.zeros((plan.chunk - plan.rows_chip, plan.lanes), F32)
                    rows = jnp.concatenate([rows, rest], axis=0)
                zs[i, k * deep + j] = rows.astype(BF)
            for d, zi in z_peers.items():
                copy = pltpu.make_async_remote_copy(
                    src_ref=zs.at[i, zi], dst_ref=zr.at[i, d], send_sem=zss.at[i, d],
                    recv_sem=zrs.at[i, d], device_id=place(x, y, zi, core),
                    device_id_type=MESH)
                flying[d] = copy
                if len(parts) == 1:
                    copy.start()
                else:
                    pl.when(zi // deep == k)(copy.start)
            if between is not None and k == 0:
                between()
        started.extend(flying.values())
        return flying

    def start_y(i, copies):
        total = zs[i, z].astype(F32)
        for d, copy in copies.items():
            copy.wait_recv()
            total = total + zr[i, d].astype(F32)
        ys[i] = total.astype(BF)
        return [send(ys.at[i], yr.at[d, i], yss.at[d, i], yrs.at[d, i], who)
                for d, who in enumerate(y_peers)]

    dq = [nt(eye_b, dq_t[:, b * TOK:(b + 1) * TOK]).astype(BF) for b in range(2)]
    q_out[...] = dq[1]
    q_swap = send(q_out, q_in, ds_.at[0], dr_.at[0], sibling)
    og_swap.wait_recv()
    turn(og_t, og_in, 1)
    pack(0, 0, nt(og_t[...], att_t[...]))
    tok_swap.wait_recv()
    turn(tok_t, tok_in, 1)
    pack(0, QW, nt(tok_t[...], dq_t[...]))
    x_first = start_x(0)
    spreads = []
    for h in range(MINE):
        row, col = iota((TOK, TOK), 0), iota((TOK, TOK), 1)
        spreads.append(one_hot(row == jnp.where(
            col < PAIR * ROWS2, (col % ROWS2) * SPAN2 + phase2[h],
            (col % ROWS3) * SPAN3 + phase3[h])))
    for copy in b_copies:
        copy.wait_recv()
    back = jnp.concatenate([r2[...].reshape(PAIR * ROWS2, PAY),
                            r3[...].reshape(ZN * ROWS3, PAY)], axis=0)

    def finish(b):
        parts = []
        for h in range(MINE):
            cols = slice(2 * HD * h, 2 * HD * (h + 1))
            got = slice(b * KV + 2 * HD * h, b * KV + 2 * HD * (h + 1))
            parts.append(own[b, :, cols] + nn(spreads[h], back[:, got]))
        return jnp.concatenate(parts, axis=1).astype(BF)

    theirs = finish(1)
    d_out[...] = theirs
    swap = send(d_out, d_in, ds_.at[1], dr_.at[1], sibling)
    mine = finish(0)
    pack(1, 0, nn(tok_t[...], jnp.concatenate([mine, theirs], axis=0)))
    x_second = start_x(1)

    shares = nt(wn[0], jnp.concatenate([mine, dq[0]], axis=1))
    q_swap.wait_recv()
    swap.wait_recv()
    shares = shares + nt(wn[1], jnp.concatenate([d_in[...], q_in[...]], axis=1))
    pt[...] = shares.astype(BF).reshape(pt.shape)
    c_far, c_near = [], []
    cut = D // 8
    if nh > 1:
        ring = [((head + 1) % nh, 0), ((head + nh - 1) % nh, 1)]
        over = (head + 2) % nh

        def hand(src, slot, way, to):
            return send(src, pr.at[slot, way], cs.at[slot, way], cr.at[slot, way], (seq, to))

        for to, way in ring:
            c_far.append(hand(pt.at[over, pl.ds(way * cut, cut)], 0, way, to))
        for to, way in ring:
            c_near.append(hand(pt.at[to, pl.ds((1 - way) * cut, cut)], 1, way, to))

    def pass_on():
        for copy, (to, way) in zip(c_far, ring if nh > 1 else []):
            copy.wait_recv()
            both = pt[to, way * cut:(way + 1) * cut].astype(F32) + pr[0, way].astype(F32)
            pv[way] = both.astype(BF)
            c_near.append(hand(pv.at[way], 2, way, to))

    z_first = start_z(0, x_first)
    z_second = start_z(1, x_second, pass_on)
    y_first = start_y(0, z_first)
    y_second = start_y(1, z_second)

    total = pt[head].astype(F32)
    for copy in c_near:
        copy.wait_recv()
    if nh > 1:
        low = total[:cut] + pr[2, 0].astype(F32) + pr[1, 1].astype(F32)
        high = total[cut:] + pr[2, 1].astype(F32) + pr[1, 0].astype(F32)
        total = jnp.concatenate([low, high], axis=0)
    gt_out[...] = total.astype(BF)

    sums = []
    for i, copies in enumerate((y_first, y_second)):
        for copy in copies:
            copy.wait_recv()
        own_part = ys[i].astype(F32)
        far_part = yr[0, i].astype(F32)
        if yn > 1:
            own_part = own_part + yr[1, i].astype(F32)
            far_part = far_part + yr[2, i].astype(F32)
            own_part = jnp.where(y == 0, own_part[:, :KV], own_part[:, KV:])
            far_part = jnp.where(y == 0, far_part[:, :KV], far_part[:, KV:])
        n = plan.rows_dev
        own_part, far_part = [jnp.where(core == 0, a[:n], a[n:2 * n])
                              for a in (own_part, far_part)]
        sums.append([jnp.where(core == 0, own_part, far_part),
                     jnp.where(core == 0, far_part, own_part)])
    early, late = sums
    go_out[...] = jnp.concatenate([early[c][:, :QW] for c in range(CORES)], axis=1)
    gw_out[...] = jnp.concatenate(
        [piece for c in range(CORES) for h in range(MINE)
         for piece in (early[c][:, QW + HD * h:QW + HD * (h + 1)],
                       late[c][:, 2 * HD * h:2 * HD * (h + 1)])], axis=1)
    for copy in started:
        copy.wait_send()


def write_out(gt, gw, go, gt_out, gw_out, go_out):
    gt_out[...] = gt[...]
    gw_out[...] = gw[...]
    go_out[...] = go[...]


def per_device(plan, tokens, valid, offsets, qkv_weight, out_weight, out_grad):
    vm = pl.BlockSpec(memory_space=pltpu.VMEM)
    hbm = pl.BlockSpec(memory_space=pltpu.HBM)
    dma = pltpu.SemaphoreType.DMA
    xn, lanes = plan.xn, plan.lanes
    near, wide = pltpu.VMEM((PAIR, ROWS2, PAY), BF), pltpu.VMEM((ZN, ROWS3, PAY), BF)
    square = pltpu.VMEM((MINE, 2, TOK, TOK), F32)
    scratch = [
        pltpu.SMEM((2, HEADS), jnp.int32),
        pltpu.VMEM((1, TOK), jnp.int32),
        pltpu.VMEM((TOK, D), BF),
        pltpu.VMEM((HEADS * 3 * HD, D), BF),
        pltpu.VMEM((HEADS * HD, D), BF),
        pltpu.VMEM((TOK, D), BF),
        pltpu.VMEM((TOK, ALL + QW), BF),
        pltpu.VMEM((ROWS2, KV), BF),
        pltpu.VMEM((ROWS3, KV), BF),
        pltpu.VMEM((TOK, D), BF),
        pltpu.VMEM((TOK, D), BF),
        pltpu.VMEM((2, TOK, ALL + QW), BF),
        square, square,
        pltpu.VMEM((PAIR * CORES, ROWS2, KV), BF),
        pltpu.VMEM((ZN * CORES, ROWS3, KV), BF),
        near, wide, near, wide,
        pltpu.VMEM((2, TOK, KV), F32),
        pltpu.VMEM((QW, 2 * TOK), BF),
        pltpu.VMEM((QW, 2 * TOK), BF),
        pltpu.VMEM((QW, 2 * TOK), BF),
        pltpu.VMEM((D, 2 * TOK), BF),
        pltpu.VMEM((D, 2 * TOK), BF),
        pltpu.VMEM((2, D, ALL), BF),
        pltpu.VMEM((TOK, KV), BF),
        pltpu.VMEM((TOK, KV), BF),
        pltpu.VMEM((TOK, QW), BF),
        pltpu.VMEM((TOK, QW), BF),
        pltpu.VMEM((2, xn, plan.xrows, lanes), BF),
        pltpu.VMEM((2, xn, plan.xrows, lanes), BF),
        pltpu.VMEM((2, ZN, plan.chunk, lanes), BF),
        pltpu.VMEM((2, ZN, plan.chunk, lanes), BF),
        pltpu.VMEM((2, plan.chunk, lanes), BF),
        pltpu.VMEM((3, 2, plan.chunk, lanes), BF),
        pltpu.VMEM((4, D // 4, TOK), BF),
        pltpu.VMEM((3, 2, D // 8, TOK), BF),
        pltpu.VMEM((2, D // 8, TOK), BF),
        dma((16,)), dma((3,)), dma((3,)),
        dma((2, 2)), dma((2, 2)), dma((ZN, 2)), dma((ZN, 2)),
        dma, dma, dma((ZN,)), dma((ZN,)), dma((2,)), dma((2,)), dma((3, 2)), dma((3, 2)),
        dma((2, 2, 4)), dma((2, 2, 4)), dma((2, ZN)), dma((2, ZN)), dma((3, 2)), dma((3, 2)),
    ]
    gt, gw, go = pl.pallas_call(
        functools.partial(body, plan),
        out_shape=(
            jax.ShapeDtypeStruct((D // 4, TOK), BF),
            jax.ShapeDtypeStruct((plan.rows_dev, HEADS * 3 * HD), F32),
            jax.ShapeDtypeStruct((plan.rows_dev, HEADS * HD), F32),
        ),
        in_specs=[hbm] * 6,
        out_specs=(vm, vm, vm),
        scratch_shapes=scratch,
        compiler_params=pltpu.CompilerParams(
            collective_id=0, has_side_effects=True, vmem_limit_bytes=VMEM_BYTES),
        cost_estimate=pl.CostEstimate(flops=2_000_000_000, bytes_accessed=4_000_000,
                                      transcendentals=800_000),
    )(offsets.T, valid.reshape(1, TOK), tokens, qkv_weight.T, out_weight, out_grad)
    hold = pl.pallas_call(
        write_out,
        out_shape=tuple(jax.ShapeDtypeStruct(a.shape, a.dtype) for a in (gt, gw, go)),
        in_specs=[vm] * 3,
        out_specs=(vm, vm, vm),
        compiler_params=pltpu.CompilerParams(vmem_limit_bytes=VMEM_BYTES),
    )(gt, gw, go)
    return hold[0].T, hold[1], hold[2].T


def solution(mesh):
    plan = Plan(mesh.shape["seq"], mesh.shape["head"])
    return jax.shard_map(
        functools.partial(per_device, plan),
        mesh=mesh,
        in_specs=(
            P("seq", None),
            P("seq"),
            P("head", None),
            P(None, "head"),
            P("head", None),
            P("seq", None),
        ),
        out_specs=(P("seq", "head"), P("seq", "head"), P("head", "seq")),
        check_vma=False,
    )
```

```python
import functools
import math

import jax
import jax.numpy as jnp
from jax import lax
from jax.experimental import pallas as pl
from jax.experimental.pallas import tpu as pltpu
from jax.sharding import PartitionSpec as P

BF = jnp.bfloat16
F32 = jnp.float32
MESH = pl.DeviceIdType.MESH

HEADS = 4
HD = 48
TOK = 256
D = 768
CORES = 2
MINE = HEADS // CORES
KV = 2 * HD * MINE
QW = HD * MINE
ALL = KV + QW
PAY = CORES * KV
ZN = 8
PAIR = 2
SPAN2 = 4
SPAN3 = 16
ROWS2 = TOK // SPAN2
ROWS3 = TOK // SPAN3
PICKED = ROWS2 + ROWS3
FAR_FIRST = (4, 3, 5, 2, 6, 1, 7)
TURN = 2
MARK = 2.0**100
MARK_TEST = 2.0**90
LOW = -1e30
VMEM_BYTES = 58 * 1024 * 1024


def nn(a, b):
    return lax.dot_general(a, b, (((1,), (0,)), ((), ())), preferred_element_type=F32)


def nt(a, b):
    return lax.dot_general(a, b, (((1,), (1,)), ((), ())), preferred_element_type=F32)


def iota(shape, dim):
    return lax.broadcasted_iota(jnp.int32, shape, dim)


def one_hot(mask):
    return jnp.where(mask, 1.0, 0.0).astype(BF)


def thirds(x):
    high = x.astype(BF).astype(F32)
    mid = (x - high).astype(BF).astype(F32)
    return [high, mid, (x - high - mid).astype(BF).astype(F32)]


def stack_rows(rows):
    at = iota((16, rows[0].shape[1]), 0)
    out = jnp.zeros(at.shape, F32)
    for i, row in enumerate(rows):
        out = jnp.where(at == i, row, out)
    return out.astype(BF)


def halves(x):
    high = x.astype(BF)
    return [high, (x - high.astype(F32)).astype(BF)]


class Plan:
    def __init__(self, n_seq, n_head):
        self.n_head = n_head
        self.yn = 2 if n_seq >= 32 else 1
        self.xn = n_seq // (CORES * ZN * self.yn)
        self.rows_dev = D // n_seq
        self.rows_chip = CORES * self.rows_dev
        self.chunk = -(-self.rows_chip // 16) * 16
        self.xrows = ZN * self.rows_chip
        self.lanes = self.yn * KV


def body(plan, offs_h, valid_h, tokens_h, wqkv_h, wout_h, ograd_h, gt_out, gw_out, go_out,
         offs, valid, tokens, wqkv, wout, ograd, gt, gw, go,
         p_out, s2, s3, tok_in, og_in, proj, w_loc, p_loc, kv2, kv3, g2, g3, r2, r3, own, att_t, dq_t,
         dat_t, tok_t, og_t, wn, d_out, d_in, q_out, q_in,
         xs, xr, zs, zr, ys, yr, pt, pr, pv,
         ls, os_, es, er, a2s, a2r, a3s, a3r, b2s, b2r, b3s, b3r, ds_, dr_, cs, cr,
         xss, xrs, zss, zrs, yss, yrs):
    xn, yn, nh = plan.xn, plan.yn, plan.n_head
    factor = 1.0 / math.sqrt(HD)
    seq = lax.axis_index("seq")
    head = lax.axis_index("head")
    core = seq % CORES
    other = 1 - core
    z = (seq // CORES) % ZN
    y = (seq // (CORES * ZN)) % yn
    x = seq // (CORES * ZN * yn)

    def place(xi, yi, zi, ci):
        return (((xi * yn + yi) * ZN + zi) * CORES + ci, head)

    near_z = z % PAIR
    mate = z - near_z + 1 - near_z
    pos2 = near_z * CORES
    pos3 = z * CORES
    sibling = place(x, y, z, other)
    z_peers = {d: (z + d) % ZN for d in FAR_FIRST}
    x_peers = {d: (x + d) % xn for d in (2, 1, 3) if d < xn}
    h_peers = {d: (head + d) % nh for d in (1, 3) if d < nh}
    far = (y + 1) % yn
    y_peers = [sibling]
    if yn > 1:
        y_peers += [place(x, far, z, core), place(x, far, z, other)]

    barrier = pltpu.get_barrier_semaphore()
    greeted = [place(x, y, zi, c) for zi in z_peers.values() for c in (core, other)] + y_peers
    greeted += [place(xi, y, z, core) for xi in x_peers.values()]
    greeted += [(seq, to) for to in h_peers.values()]
    for who in greeted:
        pl.semaphore_signal(barrier, inc=1, device_id=who, device_id_type=MESH)

    loads = []

    def load(src, dst):
        copy = pltpu.make_async_copy(src, dst, ls.at[len(loads)])
        copy.start()
        loads.append(copy)
        return copy

    def load_rows(src, dst, base, rows, pieces):
        size = rows // pieces
        return [load(src.at[at], dst.at[at]) for at in
                [pl.ds(pl.multiple_of(base + size * i, 16), size) for i in range(pieces)]]

    w_rows = MINE * 3 * HD
    need_first = load_rows(tokens_h, tokens, 0, TOK, 2)
    for h in range(HEADS):
        need_first += load_rows(wqkv_h, wqkv, 3 * HD * h + HD, 2 * HD, 1)
    need_first += [load(valid_h, valid), load(offs_h, offs)]
    need_then = []
    for h in range(HEADS):
        need_then += load_rows(wqkv_h, wqkv, 3 * HD * h, HD, 1)
    need_then += load_rows(ograd_h, ograd, 0, TOK, 2)
    need_then += load_rows(wout_h, wout, 0, CORES * QW, 1)

    started = []

    def send(src, dst, ssem, rsem, who):
        copy = pltpu.make_async_remote_copy(
            src_ref=src, dst_ref=dst, send_sem=ssem, recv_sem=rsem,
            device_id=who, device_id_type=MESH)
        copy.start()
        started.append(copy)
        return copy

    def rows_of(c, start, size):
        base = c * w_rows + start
        return jnp.concatenate(
            [wqkv[pl.ds(pl.multiple_of(base + 3 * HD * h, 16), size), :] for h in range(MINE)],
            axis=0)

    def out_of(c):
        return wout[pl.ds(pl.multiple_of(c * QW, 16), QW), :]

    eye = iota((TOK, TOK), 0) == iota((TOK, TOK), 1)
    eye_b = one_hot(eye)
    can_mark = iota((TOK, KV), 1) % (2 * HD) == 0
    for copy in need_first:
        copy.wait()
    alive = jnp.sum(jnp.where(eye, valid[...].astype(F32), 0.0), axis=1, keepdims=True)
    marked = can_mark & (alive == 0.0)
    kv_mine, kv_other = rows_of(core, HD, 2 * HD), rows_of(other, HD, 2 * HD)
    p_out[:, :KV] = jnp.where(marked, MARK, nt(tokens[...], kv_other)).astype(BF)
    proj[0, :, :KV] = jnp.where(marked, MARK, nt(tokens[...], kv_mine)).astype(BF)

    def pick_of(g):
        rows = iota((PICKED, TOK), 0)
        want = jnp.where(rows < ROWS2, rows * SPAN2 + offs[0, g],
                         (rows - ROWS2) * SPAN3 + offs[1, g])
        return one_hot(iota((PICKED, TOK), 1) == want)

    picks = [pick_of(core * MINE + h) for h in range(MINE)]
    for h in range(MINE):
        cols = slice(2 * HD * h, 2 * HD * (h + 1))
        chosen = nn(picks[h], proj[0, :, cols]).astype(BF)
        kv2[pos2, :, cols] = chosen[:ROWS2]
        kv3[pos3, :, cols] = chosen[ROWS2:]
        chosen = nn(pick_of(other * MINE + h), p_out[:, cols]).astype(BF)
        s2[:, cols] = chosen[:ROWS2]
        s3[:, cols] = chosen[ROWS2:]

    pl.semaphore_wait(barrier, len(greeted))
    a_copies = []

    def give(source, other_source, to, sems, at, slot, zi, c):
        same = 0 if c is other else 1
        a_copies.append(send(source if same else other_source, to.at[slot + 1 - same],
                             sems[0].at[at, same], sems[1].at[at, same], place(x, y, zi, c)))

    for d, zi in z_peers.items():
        for c in (core, other):
            give(kv3.at[pos3], s3, kv3, (a3s, a3r), d, pos3, zi, c)
    for c in (core, other):
        give(kv2.at[pos2], s2, kv2, (a2s, a2r), 1, pos2, mate, c)
    give(kv3.at[pos3], s3, kv3, (a3s, a3r), 0, pos3, z, other)
    give(kv2.at[pos2], s2, kv2, (a2s, a2r), 0, pos2, z, other)

    for copy in need_then:
        copy.wait()
    q_mine, q_other = rows_of(core, 0, HD), rows_of(other, 0, HD)
    p_out[:, KV:ALL] = nt(tokens[...], q_other).astype(BF)
    p_out[:, ALL:] = nt(ograd[...], out_of(other)).astype(BF)
    swap = send(p_out, proj.at[1], es.at[0], er.at[0], sibling)
    tok_swap = send(tokens, tok_in, es.at[1], er.at[1], sibling)
    og_swap = send(ograd, og_in, es.at[2], er.at[2], sibling)

    phase2 = [offs[0, core * MINE + h] for h in range(MINE)]
    phase3 = [offs[1, core * MINE + h] for h in range(MINE)]
    proj[0, :, KV:ALL] = nt(tokens[...], q_mine).astype(BF)
    proj[0, :, ALL:] = nt(ograd[...], out_of(core)).astype(BF)
    dat_t[:, :TOK] = nt(out_of(core), ograd[...]).astype(BF)
    swap.wait_recv()
    dat_t[:, TOK:] = nt(eye_b[:QW, :QW], proj[1, :, ALL:]).astype(BF)
    eye_kv = one_hot(iota((KV, KV), 0) == iota((KV, KV), 1))
    local_t = [nt(eye_kv, proj[b, :, :KV]).astype(BF) for b in range(2)]
    spots = []
    for h in range(MINE):
        zero2, zero3 = jnp.zeros((ROWS2, TOK), BF), jnp.zeros((ROWS3, TOK), BF)
        one2, one3 = picks[h][:ROWS2], picks[h][ROWS2:]
        spots.append([
            jnp.concatenate([jnp.concatenate([one, zero], axis=1),
                             jnp.concatenate([zero, one], axis=1)], axis=0)
            for one, zero in ((one2, zero2), (one3, zero3))])

    def columns(h):
        return (slice(2 * HD * h, 2 * HD * h + HD), slice(2 * HD * h + HD, 2 * HD * (h + 1)),
                slice(KV + HD * h, KV + HD * (h + 1)), slice(ALL + HD * h, ALL + HD * (h + 1)))

    def soft(k, q):
        keep = k[:, 0:1].astype(F32) < MARK_TEST
        s = jnp.where(keep, nt(k, q) * factor, LOW)
        peak = jnp.max(s, axis=0, keepdims=True)
        w = jnp.exp(s - peak)
        return peak, w, jnp.sum(w, axis=0, keepdims=True)

    local = []
    few = []
    for h in range(MINE):
        kc, vc, qc, dc = columns(h)
        parts = []
        for b in range(2):
            peak, w, den = soft(proj[b, :, kc], proj[b, :, qc])
            w_loc[h, b] = w
            p_loc[h, b] = nt(proj[b, :, vc], proj[b, :, dc])
            parts.append((peak, den, nn(local_t[b][vc, :], w.astype(BF))))
        local.append([jnp.concatenate([parts[0][i], parts[1][i]], axis=1) for i in range(3)])
        chosen = [[nn(picks[h], proj[b, :, c]).astype(BF) for b in range(2)] for c in (qc, dc)]
        few.append([[jnp.concatenate([pair[0][at], pair[1][at]], axis=0) for pair in chosen]
                    for at in (slice(0, ROWS2), slice(ROWS2, PICKED))])

    row = iota((D, 1), 0)
    inner = (row % plan.xrows + (z + TURN) * plan.rows_chip) % plan.xrows
    order = one_hot(iota((D, D), 1) == row - row % plan.xrows + inner)

    def turn(to, block, b):
        to[:, b * TOK:(b + 1) * TOK] = nt(order, block[...]).astype(BF)

    turn(tok_t, tokens, 0)
    turn(og_t, ograd, 0)
    eye_d = one_hot(iota((D, D), 0) == iota((D, D), 1))
    wn[0] = nt(eye_d, jnp.concatenate([kv_mine, q_mine], axis=0)).astype(BF)
    wn[1] = nt(eye_d, jnp.concatenate([kv_other, q_other], axis=0)).astype(BF)

    for copy in a_copies:
        copy.wait_recv()

    lane = iota((1, 2 * TOK), 1)
    rows_far = [kv2[...].reshape(TOK, KV), kv3[...].reshape(TOK, KV)]
    cols_far = [nt(eye_kv, r).astype(BF) for r in rows_far]
    units = [(h, level) for h in range(MINE) for level in range(2)]
    members = [[lane % SPAN2 == phase2[h], lane % SPAN3 == phase3[h]] for h in range(MINE)]
    col = [columns(h) for h in range(MINE)]
    soft_far = {u: soft(rows_far[u[1]][:, col[u[0]][0]], few[u[0]][u[1]][0]) for u in units}
    prod_far = {u: nt(rows_far[u[1]][:, col[u[0]][1]], few[u[0]][u[1]][1]) for u in units}
    num_far = {u: nn(cols_far[u[1]][col[u[0]][1], :], soft_far[u][1].astype(BF)) for u in units}
    full = {}
    for u in units:
        peak, _, den = soft_far[u]
        full[u] = nn(jnp.concatenate([stack_rows(thirds(peak) + thirds(den))]
                                     + halves(num_far[u]), axis=0), spots[u[0]][u[1]])
    scale_loc, delta_loc, wanted = [], [], []
    for h in range(MINE):
        peaks, dens, nums = [local[h][0]], [local[h][1]], [local[h][2]]
        for level in range(2):
            got = full[h, level]
            peaks.append(jnp.where(members[h][level], got[0:1] + got[1:2] + got[2:3], LOW))
            dens.append(got[3:4] + got[4:5] + got[5:6])
            nums.append(got[16:16 + HD] + got[16 + HD:16 + 2 * HD])
        top = jnp.maximum(jnp.maximum(peaks[0], peaks[1]), peaks[2])
        scales = [jnp.exp(peak - top) for peak in peaks]
        inv = 1.0 / sum(scale * den for scale, den in zip(scales, dens))
        att = (sum(scale * num for scale, num in zip(scales, nums)) * inv).astype(BF)
        hr = slice(HD * h, HD * (h + 1))
        att_t[hr, :] = att
        delta = jnp.sum(dat_t[hr, :].astype(F32) * att.astype(F32), axis=0, keepdims=True)
        scale_loc.append(scales[0] * inv)
        delta_loc.append(delta)
        wanted.append(stack_rows(thirds(scales[1] * inv) + thirds(scales[2] * inv)
                                 + thirds(delta)))
    stats = {u: nt(wanted[u[0]], spots[u[0]][u[1]]) for u in units}
    grads = {}
    for u in units:
        i, got = 3 * u[1], stats[u]
        normed = soft_far[u][1] * (got[i:i + 1] + got[i + 1:i + 2] + got[i + 2:i + 3])
        delta_few = got[6:7] + got[7:8] + got[8:9]
        grads[u] = ((normed * (prod_far[u] - delta_few)).astype(BF), normed.astype(BF))
    for u in units:
        kc, vc, _, _ = col[u[0]]
        q, d = few[u[0]][u[1]]
        to, n = ((g2, PAIR), (g3, ZN))[u[1]]
        dk = (nn(grads[u][0], q) * factor).astype(BF).reshape(n, CORES, -1, HD)
        dv = nn(grads[u][1], d).astype(BF).reshape(n, CORES, -1, HD)
        for part in range(CORES):
            put = part * KV
            to[:, :, put + kc.start:put + kc.stop] = dk[:, part]
            to[:, :, put + vc.start:put + vc.stop] = dv[:, part]

    b_copies = []
    for d, zi in z_peers.items():
        b_copies.append(send(g3.at[zi], r3.at[z], b3s.at[d], b3r.at[d], place(x, y, zi, core)))
    b_copies.append(send(g2.at[1 - near_z], r2.at[near_z], b2s, b2r, place(x, y, mate, core)))
    r2[near_z] = g2[near_z]
    r3[z] = g3[z]

    dq_far = []
    for h in range(MINE):
        parts = []
        for level in range(2):
            dq = nn(cols_far[level][col[h][0], :], grads[h, level][0])
            dq = nn(jnp.concatenate(halves(dq), axis=0), spots[h][level])
            parts.append(dq[:HD] + dq[HD:])
        dq_far.append(parts[0] + parts[1])
    for h in range(MINE):
        kc, vc, qc, dc = columns(h)
        for b in range(2):
            at = slice(b * TOK, (b + 1) * TOK)
            normed = w_loc[h, b] * scale_loc[h][:, at]
            grad = (normed * (p_loc[h, b] - delta_loc[h][:, at])).astype(BF)
            own[b, :, kc] = nn(grad, proj[b, :, qc]) * factor
            own[b, :, vc] = nn(normed.astype(BF), proj[b, :, dc])
            dq = nn(local_t[b][kc, :], grad) + dq_far[h][:, at]
            dq_t[HD * h:HD * (h + 1), at] = (dq * factor).astype(BF)

    def pack(i, col, block):
        width = block.shape[1]
        block = block.astype(BF).reshape(xn, yn, plan.xrows, width)
        for yi in range(yn):
            xs[i, :, :, yi * KV + col:yi * KV + col + width] = block[:, yi]

    def parts_of(i):
        count = 2 if i else 1
        size = plan.xrows // count
        return [(k, pl.ds(k * size, size)) for k in range(count)]

    def start_x(i):
        return [[send(xs.at[i, xi, at], xr.at[i, d, at], xss.at[i, k, d], xrs.at[i, k, d],
                      place(xi, y, z, core)) for d, xi in x_peers.items()]
                for k, at in parts_of(i)]

    def start_z(i, copies, between=None):
        parts = parts_of(i)
        deep = ZN // len(parts)
        flying = {}
        for (k, at), some in zip(parts, copies):
            total = xs[i, x, at].astype(F32)
            for d, copy in zip(x_peers, some):
                copy.wait_recv()
                total = total + xr[i, d, at].astype(F32)
            here = [(k * deep + j + TURN) % ZN for j in range(deep)]
            for j, d in enumerate(here):
                rows = total[j * plan.rows_chip:(j + 1) * plan.rows_chip]
                if plan.chunk > plan.rows_chip:
                    rest = jnp.zeros((plan.chunk - plan.rows_chip, plan.lanes), F32)
                    rows = jnp.concatenate([rows, rest], axis=0)
                zs[i, d] = rows.astype(BF)
            for d, zi in z_peers.items():
                if d in here:
                    flying[d] = send(zs.at[i, d], zr.at[i, d], zss.at[i, d], zrs.at[i, d],
                                     place(x, y, zi, core))
        if between is not None:
            between()
        return flying

    def start_y(i, copies):
        total = zs[i, 0].astype(F32)
        for d, copy in copies.items():
            copy.wait_recv()
            total = total + zr[i, d].astype(F32)
        ys[i] = total.astype(BF)
        return [send(ys.at[i], yr.at[d, i], yss.at[d, i], yrs.at[d, i], who)
                for d, who in enumerate(y_peers)]

    dq = [nt(eye_b, dq_t[:, b * TOK:(b + 1) * TOK]).astype(BF) for b in range(2)]
    q_out[...] = dq[1]
    q_swap = send(q_out, q_in, ds_.at[0], dr_.at[0], sibling)
    og_swap.wait_recv()
    turn(og_t, og_in, 1)
    pack(0, 0, nt(og_t[...], att_t[...]))
    tok_swap.wait_recv()
    turn(tok_t, tok_in, 1)
    pack(0, QW, nt(tok_t[...], dq_t[...]))
    x_first = start_x(0)
    spreads = []
    for h in range(MINE):
        row, col = iota((TOK, TOK), 0), iota((TOK, TOK), 1)
        spreads.append(one_hot(row == jnp.where(
            col < PAIR * ROWS2, (col % ROWS2) * SPAN2 + phase2[h],
            (col % ROWS3) * SPAN3 + phase3[h])))
    for copy in b_copies:
        copy.wait_recv()
    back = jnp.concatenate([r2[...].reshape(PAIR * ROWS2, PAY),
                            r3[...].reshape(ZN * ROWS3, PAY)], axis=0)

    def finish(b):
        parts = []
        for h in range(MINE):
            cols = slice(2 * HD * h, 2 * HD * (h + 1))
            got = slice(b * KV + 2 * HD * h, b * KV + 2 * HD * (h + 1))
            parts.append(own[b, :, cols] + nn(spreads[h], back[:, got]))
        return jnp.concatenate(parts, axis=1).astype(BF)

    theirs = finish(1)
    d_out[...] = theirs
    swap = send(d_out, d_in, ds_.at[1], dr_.at[1], sibling)
    mine = finish(0)
    pack(1, 0, nn(tok_t[...], jnp.concatenate([mine, theirs], axis=0)))
    x_second = start_x(1)

    shares = nt(wn[0], jnp.concatenate([mine, dq[0]], axis=1))
    q_swap.wait_recv()
    swap.wait_recv()
    shares = shares + nt(wn[1], jnp.concatenate([d_in[...], q_in[...]], axis=1))
    pt[...] = shares.astype(BF).reshape(pt.shape)
    c_far, c_near = [], []
    cut = D // 8
    if nh > 1:
        ring = [((head + 1) % nh, 0), ((head + nh - 1) % nh, 1)]
        over = (head + 2) % nh

        def hand(src, slot, way, to):
            return send(src, pr.at[slot, way], cs.at[slot, way], cr.at[slot, way], (seq, to))

        for to, way in ring:
            c_far.append(hand(pt.at[over, pl.ds(way * cut, cut)], 0, way, to))
        for to, way in ring:
            c_near.append(hand(pt.at[to, pl.ds((1 - way) * cut, cut)], 1, way, to))

    def pass_on():
        for copy, (to, way) in zip(c_far, ring if nh > 1 else []):
            copy.wait_recv()
            both = pt[to, way * cut:(way + 1) * cut].astype(F32) + pr[0, way].astype(F32)
            pv[way] = both.astype(BF)
            c_near.append(hand(pv.at[way], 2, way, to))

    z_first = start_z(0, x_first)
    z_second = start_z(1, x_second, pass_on)
    y_first = start_y(0, z_first)
    y_second = start_y(1, z_second)

    total = pt[head].astype(F32)
    for copy in c_near:
        copy.wait_recv()
    if nh > 1:
        low = total[:cut] + pr[2, 0].astype(F32) + pr[1, 1].astype(F32)
        high = total[cut:] + pr[2, 1].astype(F32) + pr[1, 0].astype(F32)
        total = jnp.concatenate([low, high], axis=0)
    gt[...] = total.astype(BF)
    stores = [pltpu.make_async_copy(gt, gt_out, os_.at[0])]
    stores[0].start()

    sums = []
    for i, copies in enumerate((y_first, y_second)):
        for copy in copies:
            copy.wait_recv()
        own_part = ys[i].astype(F32)
        far_part = yr[0, i].astype(F32)
        if yn > 1:
            own_part = own_part + yr[1, i].astype(F32)
            far_part = far_part + yr[2, i].astype(F32)
            own_part = jnp.where(y == 0, own_part[:, :KV], own_part[:, KV:])
            far_part = jnp.where(y == 0, far_part[:, :KV], far_part[:, KV:])
        n = plan.rows_dev
        own_part, far_part = [jnp.where(core == 0, a[:n], a[n:2 * n])
                              for a in (own_part, far_part)]
        sums.append([jnp.where(core == 0, own_part, far_part),
                     jnp.where(core == 0, far_part, own_part)])
    early, late = sums
    go[...] = jnp.concatenate([early[c][:, :QW] for c in range(CORES)], axis=1)
    gw[...] = jnp.concatenate(
        [piece for c in range(CORES) for h in range(MINE)
         for piece in (early[c][:, QW + HD * h:QW + HD * (h + 1)],
                       late[c][:, 2 * HD * h:2 * HD * (h + 1)])], axis=1)
    stores.append(pltpu.make_async_copy(gw, gw_out, os_.at[1]))
    stores.append(pltpu.make_async_copy(go, go_out, os_.at[2]))
    for copy in stores[1:]:
        copy.start()
    for copy in started:
        copy.wait_send()
    for copy in stores:
        copy.wait()


def write_out(*refs):
    sources, results, stage, sems = refs[:3], refs[3:6], refs[6:9], refs[9]
    loads = [pltpu.make_async_copy(a, b, sems.at[0, i])
             for i, (a, b) in enumerate(zip(sources, stage))]
    stores = [pltpu.make_async_copy(a, b, sems.at[1, i])
              for i, (a, b) in enumerate(zip(stage, results))]
    for copy in loads:
        copy.start()
    for load, store in zip(loads, stores):
        load.wait()
        store.start()
    for copy in stores:
        copy.wait()


def per_device(plan, tokens, valid, offsets, qkv_weight, out_weight, out_grad):
    hbm = pl.BlockSpec(memory_space=pltpu.HBM)
    dma = pltpu.SemaphoreType.DMA
    xn, lanes = plan.xn, plan.lanes
    near, wide = pltpu.VMEM((PAIR, ROWS2, PAY), BF), pltpu.VMEM((ZN, ROWS3, PAY), BF)
    square = pltpu.VMEM((MINE, 2, TOK, TOK), F32)
    scratch = [
        pltpu.SMEM((2, HEADS), jnp.int32),
        pltpu.VMEM((1, TOK), jnp.int32),
        pltpu.VMEM((TOK, D), BF),
        pltpu.VMEM((HEADS * 3 * HD, D), BF),
        pltpu.VMEM((HEADS * HD, D), BF),
        pltpu.VMEM((TOK, D), BF),
        pltpu.VMEM((D // 4, TOK), BF),
        pltpu.VMEM((plan.rows_dev, HEADS * 3 * HD), F32),
        pltpu.VMEM((plan.rows_dev, HEADS * HD), F32),
        pltpu.VMEM((TOK, ALL + QW), BF),
        pltpu.VMEM((ROWS2, KV), BF),
        pltpu.VMEM((ROWS3, KV), BF),
        pltpu.VMEM((TOK, D), BF),
        pltpu.VMEM((TOK, D), BF),
        pltpu.VMEM((2, TOK, ALL + QW), BF),
        square, square,
        pltpu.VMEM((PAIR * CORES, ROWS2, KV), BF),
        pltpu.VMEM((ZN * CORES, ROWS3, KV), BF),
        near, wide, near, wide,
        pltpu.VMEM((2, TOK, KV), F32),
        pltpu.VMEM((QW, 2 * TOK), BF),
        pltpu.VMEM((QW, 2 * TOK), BF),
        pltpu.VMEM((QW, 2 * TOK), BF),
        pltpu.VMEM((D, 2 * TOK), BF),
        pltpu.VMEM((D, 2 * TOK), BF),
        pltpu.VMEM((2, D, ALL), BF),
        pltpu.VMEM((TOK, KV), BF),
        pltpu.VMEM((TOK, KV), BF),
        pltpu.VMEM((TOK, QW), BF),
        pltpu.VMEM((TOK, QW), BF),
        pltpu.VMEM((2, xn, plan.xrows, lanes), BF),
        pltpu.VMEM((2, xn, plan.xrows, lanes), BF),
        pltpu.VMEM((2, ZN, plan.chunk, lanes), BF),
        pltpu.VMEM((2, ZN, plan.chunk, lanes), BF),
        pltpu.VMEM((2, plan.chunk, lanes), BF),
        pltpu.VMEM((3, 2, plan.chunk, lanes), BF),
        pltpu.VMEM((4, D // 4, TOK), BF),
        pltpu.VMEM((3, 2, D // 8, TOK), BF),
        pltpu.VMEM((2, D // 8, TOK), BF),
        dma((16,)), dma((3,)), dma((3,)), dma((3,)),
        dma((2, 2)), dma((2, 2)), dma((ZN, 2)), dma((ZN, 2)),
        dma, dma, dma((ZN,)), dma((ZN,)), dma((2,)), dma((2,)), dma((3, 2)), dma((3, 2)),
        dma((2, 2, 4)), dma((2, 2, 4)), dma((2, ZN)), dma((2, ZN)), dma((3, 2)), dma((3, 2)),
    ]
    gt, gw, go = pl.pallas_call(
        functools.partial(body, plan),
        out_shape=(
            jax.ShapeDtypeStruct((D // 4, TOK), BF),
            jax.ShapeDtypeStruct((plan.rows_dev, HEADS * 3 * HD), F32),
            jax.ShapeDtypeStruct((plan.rows_dev, HEADS * HD), F32),
        ),
        in_specs=[hbm] * 6,
        out_specs=(hbm, hbm, hbm),
        scratch_shapes=scratch,
        compiler_params=pltpu.CompilerParams(
            collective_id=0, has_side_effects=True, vmem_limit_bytes=VMEM_BYTES),
        cost_estimate=pl.CostEstimate(flops=2_000_000_000, bytes_accessed=4_000_000,
                                      transcendentals=800_000),
    )(offsets.T, valid.reshape(1, TOK), tokens, qkv_weight.T, out_weight, out_grad)
    hold = pl.pallas_call(
        write_out,
        out_shape=tuple(jax.ShapeDtypeStruct(a.shape, a.dtype) for a in (gt, gw, go)),
        in_specs=[hbm] * 3,
        out_specs=(hbm, hbm, hbm),
        scratch_shapes=[pltpu.VMEM(a.shape, a.dtype) for a in (gt, gw, go)] + [dma((2, 3))],
        compiler_params=pltpu.CompilerParams(vmem_limit_bytes=VMEM_BYTES),
    )(gt, gw, go)
    return hold[0].T, hold[1], hold[2].T


def solution(mesh):
    plan = Plan(mesh.shape["seq"], mesh.shape["head"])
    return jax.shard_map(
        functools.partial(per_device, plan),
        mesh=mesh,
        in_specs=(
            P("seq", None),
            P("seq"),
            P("head", None),
            P(None, "head"),
            P("head", None),
            P("seq", None),
        ),
        out_specs=(P("seq", "head"), P("seq", "head"), P("head", "seq")),
        check_vma=False,
    )
```

```python
import functools
import math

import jax
import jax.numpy as jnp
from jax import lax
from jax.experimental import pallas as pl
from jax.experimental.pallas import tpu as pltpu
from jax.sharding import PartitionSpec as P

BF = jnp.bfloat16
F32 = jnp.float32
MESH = pl.DeviceIdType.MESH

HEADS = 4
HD = 48
TOK = 256
D = 768
CORES = 2
MINE = HEADS // CORES
KV = 2 * HD * MINE
QW = HD * MINE
ALL = KV + QW
PAY = CORES * KV
ZN = 8
PAIR = 2
SPAN2 = 4
SPAN3 = 16
ROWS2 = TOK // SPAN2
ROWS3 = TOK // SPAN3
PICKED = ROWS2 + ROWS3
FAR_FIRST = (4, 3, 5, 2, 6, 1, 7)
TURN = 2
MARK = 2.0**100
MARK_TEST = 2.0**90
LOW = -1e30
VMEM_BYTES = 58 * 1024 * 1024


def nn(a, b):
    return lax.dot_general(a, b, (((1,), (0,)), ((), ())), preferred_element_type=F32)


def nt(a, b):
    return lax.dot_general(a, b, (((1,), (1,)), ((), ())), preferred_element_type=F32)


def iota(shape, dim):
    return lax.broadcasted_iota(jnp.int32, shape, dim)


def one_hot(mask):
    return jnp.where(mask, 1.0, 0.0).astype(BF)


def thirds(x):
    high = x.astype(BF).astype(F32)
    mid = (x - high).astype(BF).astype(F32)
    return [high, mid, (x - high - mid).astype(BF).astype(F32)]


def stack_rows(rows):
    at = iota((16, rows[0].shape[1]), 0)
    out = jnp.zeros(at.shape, F32)
    for i, row in enumerate(rows):
        out = jnp.where(at == i, row, out)
    return out.astype(BF)


def halves(x):
    high = x.astype(BF)
    return [high, (x - high.astype(F32)).astype(BF)]


def fold(rows):
    n = rows.shape[0] // 2
    return jnp.concatenate(
        [rows[:, :128], jnp.concatenate([rows[:n, 128:], rows[n:, 128:]], axis=1)], axis=0)


def unfold(rows):
    n = 2 * rows.shape[0] // 3
    return jnp.concatenate(
        [rows[:n], jnp.concatenate([rows[n:, :64], rows[n:, 64:]], axis=0)], axis=1)


class Plan:
    def __init__(self, n_seq, n_head):
        self.n_head = n_head
        self.yn = 2 if n_seq >= 32 else 1
        self.xn = n_seq // (CORES * ZN * self.yn)
        self.rows_dev = D // n_seq
        self.rows_chip = CORES * self.rows_dev
        self.chunk = -(-self.rows_chip // 16) * 16
        self.xrows = ZN * self.rows_chip
        self.lanes = self.yn * KV


def body(plan, offs_h, valid_h, tokens_h, wqkv_h, wout_h, ograd_h, gt_out, gw_out, go_out,
         offs, valid, tokens, wqkv, wout, ograd, gt, gw, go,
         p_out, s2, s3, tok_in, og_in, proj, w_loc, p_loc, kv2, kv3, g2, g3, r2, r3, own, att_t, dq_t,
         dat_t, tok_t, og_t, wn, d_out, d_in, q_out, q_in,
         xs, xr, zs, zr, ys, yr, pt, pr, pv,
         ls, os_, es, er, a2s, a2r, a3s, a3r, b2s, b2r, b3s, b3r, ds_, dr_, cs, cr,
         xss, xrs, zss, zrs, yss, yrs):
    xn, yn, nh = plan.xn, plan.yn, plan.n_head
    factor = 1.0 / math.sqrt(HD)
    seq = lax.axis_index("seq")
    head = lax.axis_index("head")
    core = seq % CORES
    other = 1 - core
    z = (seq // CORES) % ZN
    y = (seq // (CORES * ZN)) % yn
    x = seq // (CORES * ZN * yn)

    def place(xi, yi, zi, ci):
        return (((xi * yn + yi) * ZN + zi) * CORES + ci, head)

    near_z = z % PAIR
    mate = z - near_z + 1 - near_z
    pos2 = near_z * CORES
    pos3 = z * CORES
    sibling = place(x, y, z, other)
    z_peers = {d: (z + d) % ZN for d in FAR_FIRST}
    x_peers = {d: (x + d) % xn for d in (2, 1, 3) if d < xn}
    h_peers = {d: (head + d) % nh for d in (1, 3) if d < nh}
    far = (y + 1) % yn
    y_peers = [sibling]
    if yn > 1:
        y_peers += [place(x, far, z, core), place(x, far, z, other)]

    barrier = pltpu.get_barrier_semaphore()
    greeted = [place(x, y, zi, c) for zi in z_peers.values() for c in (core, other)] + y_peers
    greeted += [place(xi, y, z, core) for xi in x_peers.values()]
    greeted += [(seq, to) for to in h_peers.values()]
    for who in greeted:
        pl.semaphore_signal(barrier, inc=1, device_id=who, device_id_type=MESH)

    loads = []

    def load(src, dst):
        copy = pltpu.make_async_copy(src, dst, ls.at[len(loads)])
        copy.start()
        loads.append(copy)
        return copy

    def load_rows(src, dst, base, rows, pieces):
        size = rows // pieces
        return [load(src.at[at], dst.at[at]) for at in
                [pl.ds(pl.multiple_of(base + size * i, 16), size) for i in range(pieces)]]

    w_rows = MINE * 3 * HD
    need_first = load_rows(tokens_h, tokens, 0, TOK, 2)
    for h in range(HEADS):
        need_first += load_rows(wqkv_h, wqkv, 3 * HD * h + HD, 2 * HD, 1)
    need_first += [load(valid_h, valid), load(offs_h, offs)]
    need_then = []
    for h in range(HEADS):
        need_then += load_rows(wqkv_h, wqkv, 3 * HD * h, HD, 1)
    need_then += load_rows(ograd_h, ograd, 0, TOK, 2)
    need_then += load_rows(wout_h, wout, 0, CORES * QW, 1)

    started = []

    def send(src, dst, ssem, rsem, who):
        copy = pltpu.make_async_remote_copy(
            src_ref=src, dst_ref=dst, send_sem=ssem, recv_sem=rsem,
            device_id=who, device_id_type=MESH)
        copy.start()
        started.append(copy)
        return copy

    def rows_of(c, start, size):
        base = c * w_rows + start
        return jnp.concatenate(
            [wqkv[pl.ds(pl.multiple_of(base + 3 * HD * h, 16), size), :] for h in range(MINE)],
            axis=0)

    def out_of(c):
        return wout[pl.ds(pl.multiple_of(c * QW, 16), QW), :]

    eye = iota((TOK, TOK), 0) == iota((TOK, TOK), 1)
    eye_b = one_hot(eye)
    can_mark = iota((TOK, KV), 1) % (2 * HD) == 0
    for copy in need_first:
        copy.wait()
    alive = jnp.sum(jnp.where(eye, valid[...].astype(F32), 0.0), axis=1, keepdims=True)
    marked = can_mark & (alive == 0.0)
    kv_mine, kv_other = rows_of(core, HD, 2 * HD), rows_of(other, HD, 2 * HD)
    p_out[:, :KV] = jnp.where(marked, MARK, nt(tokens[...], kv_other)).astype(BF)
    proj[0, :, :KV] = jnp.where(marked, MARK, nt(tokens[...], kv_mine)).astype(BF)

    def pick_of(g):
        rows = iota((PICKED, TOK), 0)
        want = jnp.where(rows < ROWS2, rows * SPAN2 + offs[0, g],
                         (rows - ROWS2) * SPAN3 + offs[1, g])
        return one_hot(iota((PICKED, TOK), 1) == want)

    picks = [pick_of(core * MINE + h) for h in range(MINE)]
    def choose(which, rows):
        return jnp.concatenate(
            [nn(which[h], rows[:, 2 * HD * h:2 * HD * (h + 1)]) for h in range(MINE)],
            axis=1).astype(BF)

    chosen = choose([pick_of(other * MINE + h) for h in range(MINE)], p_out[:, :KV])
    s2[...] = fold(chosen[:ROWS2])
    s3[...] = chosen[ROWS2:]
    chosen = choose(picks, proj[0, :, :KV])
    kv2[pos2] = fold(chosen[:ROWS2])
    kv3[pos3] = chosen[ROWS2:]

    pl.semaphore_wait(barrier, len(greeted))
    near_copies, wide_copies = [], []

    def give_wide(d, zi, c):
        same = 0 if c is other else 1
        wide_copies.append(send(kv3.at[pos3] if same else s3, kv3.at[pos3 + 1 - same],
                                a3s.at[d, same], a3r.at[d, same], place(x, y, zi, c)))

    def give_near(at, zi, c):
        same = 0 if c is other else 1
        near_copies.append(send(kv2.at[pos2] if same else s2, kv2.at[pos2 + 1 - same],
                                a2s.at[at, same], a2r.at[at, same], place(x, y, zi, c)))

    for d, zi in z_peers.items():
        for c in (core, other):
            give_wide(d, zi, c)
        if d == FAR_FIRST[2]:
            for c in (core, other):
                give_near(1, mate, c)
    give_near(0, z, other)
    give_wide(0, z, other)

    for copy in need_then:
        copy.wait()
    q_mine, q_other = rows_of(core, 0, HD), rows_of(other, 0, HD)
    p_out[:, KV:ALL] = nt(tokens[...], q_other).astype(BF)
    p_out[:, ALL:] = nt(ograd[...], out_of(other)).astype(BF)
    swap = send(p_out, proj.at[1], es.at[0], er.at[0], sibling)
    tok_swap = send(tokens, tok_in, es.at[1], er.at[1], sibling)
    og_swap = send(ograd, og_in, es.at[2], er.at[2], sibling)

    phase2 = [offs[0, core * MINE + h] for h in range(MINE)]
    phase3 = [offs[1, core * MINE + h] for h in range(MINE)]
    proj[0, :, KV:ALL] = nt(tokens[...], q_mine).astype(BF)
    proj[0, :, ALL:] = nt(ograd[...], out_of(core)).astype(BF)
    dat_t[:, :TOK] = nt(out_of(core), ograd[...]).astype(BF)
    swap.wait_recv()
    dat_t[:, TOK:] = nt(eye_b[:QW, :QW], proj[1, :, ALL:]).astype(BF)
    eye_kv = one_hot(iota((KV, KV), 0) == iota((KV, KV), 1))
    local_t = [nt(eye_kv, proj[b, :, :KV]).astype(BF) for b in range(2)]
    spots = []
    for h in range(MINE):
        zero2, zero3 = jnp.zeros((ROWS2, TOK), BF), jnp.zeros((ROWS3, TOK), BF)
        one2, one3 = picks[h][:ROWS2], picks[h][ROWS2:]
        spots.append([
            jnp.concatenate([jnp.concatenate([one, zero], axis=1),
                             jnp.concatenate([zero, one], axis=1)], axis=0)
            for one, zero in ((one2, zero2), (one3, zero3))])

    def columns(h):
        return (slice(2 * HD * h, 2 * HD * h + HD), slice(2 * HD * h + HD, 2 * HD * (h + 1)),
                slice(KV + HD * h, KV + HD * (h + 1)), slice(ALL + HD * h, ALL + HD * (h + 1)))

    def soft(k, q):
        keep = k[:, 0:1].astype(F32) < MARK_TEST
        s = jnp.where(keep, nt(k, q) * factor, LOW)
        peak = jnp.max(s, axis=0, keepdims=True)
        w = jnp.exp(s - peak)
        return peak, w, jnp.sum(w, axis=0, keepdims=True)

    local = []
    few = []
    for h in range(MINE):
        kc, vc, qc, dc = columns(h)
        parts = []
        for b in range(2):
            peak, w, den = soft(proj[b, :, kc], proj[b, :, qc])
            w_loc[h, b] = w
            p_loc[h, b] = nt(proj[b, :, vc], proj[b, :, dc])
            parts.append((peak, den, nn(local_t[b][vc, :], w.astype(BF))))
        local.append([jnp.concatenate([parts[0][i], parts[1][i]], axis=1) for i in range(3)])
        chosen = [[nn(picks[h], proj[b, :, c]).astype(BF) for b in range(2)] for c in (qc, dc)]
        few.append([[jnp.concatenate([pair[0][at], pair[1][at]], axis=0) for pair in chosen]
                    for at in (slice(0, ROWS2), slice(ROWS2, PICKED))])

    row = iota((D, 1), 0)
    inner = (row % plan.xrows + (z + TURN) * plan.rows_chip) % plan.xrows
    order = one_hot(iota((D, D), 1) == row - row % plan.xrows + inner)

    def turn(to, block, b):
        to[:, b * TOK:(b + 1) * TOK] = nt(order, block[...]).astype(BF)

    turn(tok_t, tokens, 0)
    turn(og_t, ograd, 0)
    eye_d = one_hot(iota((D, D), 0) == iota((D, D), 1))
    wn[0] = nt(eye_d, jnp.concatenate([kv_mine, q_mine], axis=0)).astype(BF)
    wn[1] = nt(eye_d, jnp.concatenate([kv_other, q_other], axis=0)).astype(BF)

    lane = iota((1, 2 * TOK), 1)
    members = [[lane % SPAN2 == phase2[h], lane % SPAN3 == phase3[h]] for h in range(MINE)]
    col = [columns(h) for h in range(MINE)]
    units = [(h, level) for h in range(MINE) for level in range(2)]
    rows_far, cols_far, soft_far, prod_far, full = [], [], {}, {}, {}
    for level in range(2):
        for copy in (near_copies, wide_copies)[level]:
            copy.wait_recv()
        if level == 0:
            rows_far.append(jnp.concatenate([unfold(kv2[i]) for i in range(PAIR * CORES)], axis=0))
        else:
            rows_far.append(kv3[...].reshape(TOK, KV))
        cols_far.append(nt(eye_kv, rows_far[level]).astype(BF))
        for h in range(MINE):
            kc, vc, _, _ = col[h]
            q, d = few[h][level]
            soft_far[h, level] = soft(rows_far[level][:, kc], q)
            prod_far[h, level] = nt(rows_far[level][:, vc], d)
        for h in range(MINE):
            peak, w, den = soft_far[h, level]
            num = nn(cols_far[level][col[h][1], :], w.astype(BF))
            full[h, level] = nn(jnp.concatenate(
                [stack_rows(thirds(peak) + thirds(den))] + halves(num), axis=0), spots[h][level])
    scale_loc, delta_loc, wanted = [], [], []
    for h in range(MINE):
        peaks, dens, nums = [local[h][0]], [local[h][1]], [local[h][2]]
        for level in range(2):
            got = full[h, level]
            peaks.append(jnp.where(members[h][level], got[0:1] + got[1:2] + got[2:3], LOW))
            dens.append(got[3:4] + got[4:5] + got[5:6])
            nums.append(got[16:16 + HD] + got[16 + HD:16 + 2 * HD])
        top = jnp.maximum(jnp.maximum(peaks[0], peaks[1]), peaks[2])
        scales = [jnp.exp(peak - top) for peak in peaks]
        inv = 1.0 / sum(scale * den for scale, den in zip(scales, dens))
        att = (sum(scale * num for scale, num in zip(scales, nums)) * inv).astype(BF)
        hr = slice(HD * h, HD * (h + 1))
        att_t[hr, :] = att
        delta = jnp.sum(dat_t[hr, :].astype(F32) * att.astype(F32), axis=0, keepdims=True)
        scale_loc.append(scales[0] * inv)
        delta_loc.append(delta)
        wanted.append(stack_rows(thirds(scales[1] * inv) + thirds(scales[2] * inv)
                                 + thirds(delta)))
    stats = {u: nt(wanted[u[0]], spots[u[0]][u[1]]) for u in units}
    grads = {}
    for u in units:
        i, got = 3 * u[1], stats[u]
        normed = soft_far[u][1] * (got[i:i + 1] + got[i + 1:i + 2] + got[i + 2:i + 3])
        delta_few = got[6:7] + got[7:8] + got[8:9]
        grads[u] = ((normed * (prod_far[u] - delta_few)).astype(BF), normed.astype(BF))
    for u in units:
        kc, vc, _, _ = col[u[0]]
        q, d = few[u[0]][u[1]]
        to, n = ((g2, PAIR), (g3, ZN))[u[1]]
        dk = (nn(grads[u][0], q) * factor).astype(BF).reshape(n, CORES, -1, HD)
        dv = nn(grads[u][1], d).astype(BF).reshape(n, CORES, -1, HD)
        for part in range(CORES):
            put = part * KV
            to[:, :, put + kc.start:put + kc.stop] = dk[:, part]
            to[:, :, put + vc.start:put + vc.stop] = dv[:, part]

    b_copies = []
    for d, zi in z_peers.items():
        b_copies.append(send(g3.at[zi], r3.at[z], b3s.at[d], b3r.at[d], place(x, y, zi, core)))
    b_copies.append(send(g2.at[1 - near_z], r2.at[near_z], b2s, b2r, place(x, y, mate, core)))
    r2[near_z] = g2[near_z]
    r3[z] = g3[z]

    dq_far = []
    for h in range(MINE):
        parts = []
        for level in range(2):
            dq = nn(cols_far[level][col[h][0], :], grads[h, level][0])
            dq = nn(jnp.concatenate(halves(dq), axis=0), spots[h][level])
            parts.append(dq[:HD] + dq[HD:])
        dq_far.append(parts[0] + parts[1])
    for h in range(MINE):
        kc, vc, qc, dc = columns(h)
        for b in range(2):
            at = slice(b * TOK, (b + 1) * TOK)
            normed = w_loc[h, b] * scale_loc[h][:, at]
            grad = (normed * (p_loc[h, b] - delta_loc[h][:, at])).astype(BF)
            own[b, :, kc] = nn(grad, proj[b, :, qc]) * factor
            own[b, :, vc] = nn(normed.astype(BF), proj[b, :, dc])
            dq = nn(local_t[b][kc, :], grad) + dq_far[h][:, at]
            dq_t[HD * h:HD * (h + 1), at] = (dq * factor).astype(BF)

    def pack(i, col, block):
        width = block.shape[1]
        block = block.astype(BF).reshape(xn, yn, plan.xrows, width)
        for yi in range(yn):
            xs[i, :, :, yi * KV + col:yi * KV + col + width] = block[:, yi]

    def parts_of(i):
        count = 2 if i else 1
        size = plan.xrows // count
        return [(k, pl.ds(k * size, size)) for k in range(count)]

    def start_x(i):
        return [[send(xs.at[i, xi, at], xr.at[i, d, at], xss.at[i, k, d], xrs.at[i, k, d],
                      place(xi, y, z, core)) for d, xi in x_peers.items()]
                for k, at in parts_of(i)]

    def start_z(i, copies, between=None):
        parts = parts_of(i)
        deep = ZN // len(parts)
        flying = {}
        for (k, at), some in zip(parts, copies):
            total = xs[i, x, at].astype(F32)
            for d, copy in zip(x_peers, some):
                copy.wait_recv()
                total = total + xr[i, d, at].astype(F32)
            here = [(k * deep + j + TURN) % ZN for j in range(deep)]
            for j, d in enumerate(here):
                rows = total[j * plan.rows_chip:(j + 1) * plan.rows_chip]
                if plan.chunk > plan.rows_chip:
                    rest = jnp.zeros((plan.chunk - plan.rows_chip, plan.lanes), F32)
                    rows = jnp.concatenate([rows, rest], axis=0)
                zs[i, d] = rows.astype(BF)
            for d, zi in z_peers.items():
                if d in here:
                    flying[d] = send(zs.at[i, d], zr.at[i, d], zss.at[i, d], zrs.at[i, d],
                                     place(x, y, zi, core))
            if between is not None:
                between(k)
        return flying

    def start_y(i, copies):
        total = zs[i, 0].astype(F32)
        for d, copy in copies.items():
            copy.wait_recv()
            total = total + zr[i, d].astype(F32)
        ys[i] = total.astype(BF)
        return [send(ys.at[i], yr.at[d, i], yss.at[d, i], yrs.at[d, i], who)
                for d, who in enumerate(y_peers)]

    dq = [nt(eye_b, dq_t[:, b * TOK:(b + 1) * TOK]).astype(BF) for b in range(2)]
    q_out[...] = dq[1]
    q_swap = send(q_out, q_in, ds_.at[0], dr_.at[0], sibling)
    og_swap.wait_recv()
    turn(og_t, og_in, 1)
    pack(0, 0, nt(og_t[...], att_t[...]))
    tok_swap.wait_recv()
    turn(tok_t, tok_in, 1)
    pack(0, QW, nt(tok_t[...], dq_t[...]))
    x_first = start_x(0)
    spreads = []
    for h in range(MINE):
        row, col = iota((TOK, TOK), 0), iota((TOK, TOK), 1)
        spreads.append(one_hot(row == jnp.where(
            col < PAIR * ROWS2, (col % ROWS2) * SPAN2 + phase2[h],
            (col % ROWS3) * SPAN3 + phase3[h])))
    for copy in b_copies:
        copy.wait_recv()
    back = jnp.concatenate([r2[...].reshape(PAIR * ROWS2, PAY),
                            r3[...].reshape(ZN * ROWS3, PAY)], axis=0)

    def finish(b):
        parts = []
        for h in range(MINE):
            cols = slice(2 * HD * h, 2 * HD * (h + 1))
            got = slice(b * KV + 2 * HD * h, b * KV + 2 * HD * (h + 1))
            parts.append(own[b, :, cols] + nn(spreads[h], back[:, got]))
        return jnp.concatenate(parts, axis=1).astype(BF)

    theirs = finish(1)
    d_out[...] = theirs
    swap = send(d_out, d_in, ds_.at[1], dr_.at[1], sibling)
    mine = finish(0)
    both = jnp.concatenate([mine, theirs], axis=0)
    rows_x = yn * plan.xrows
    x_late = [{}, {}]
    for d in list(x_peers) + [0]:
        xi = (x + d) % xn
        block = nn(tok_t[pl.ds(pl.multiple_of(xi * rows_x, 16), rows_x), :], both).astype(BF)
        for yi in range(yn):
            xs[1, xi, :, yi * KV:(yi + 1) * KV] = block[yi * plan.xrows:(yi + 1) * plan.xrows]
        if d:
            k, at = parts_of(1)[0]
            x_late[k][d] = send(xs.at[1, xi, at], xr.at[1, d, at], xss.at[1, k, d],
                                xrs.at[1, k, d], place(xi, y, z, core))
    for d, xi in x_peers.items():
        k, at = parts_of(1)[1]
        x_late[k][d] = send(xs.at[1, xi, at], xr.at[1, d, at], xss.at[1, k, d],
                            xrs.at[1, k, d], place(xi, y, z, core))
    x_second = [list(some.values()) for some in x_late]

    shares = nt(wn[0], jnp.concatenate([mine, dq[0]], axis=1))
    q_swap.wait_recv()
    swap.wait_recv()
    shares = shares + nt(wn[1], jnp.concatenate([d_in[...], q_in[...]], axis=1))
    pt[...] = shares.astype(BF).reshape(pt.shape)
    c_far, c_near = [], []
    cut = D // 8
    if nh > 1:
        ring = [((head + 1) % nh, 0), ((head + nh - 1) % nh, 1)]
        over = (head + 2) % nh

        def hand(src, slot, way, to, at=None, part=0):
            dst = pr.at[slot, way] if at is None else pr.at[slot, way, at]
            return send(src, dst, cs.at[slot, way, part], cr.at[slot, way, part], (seq, to))

        for part in range(2):
            for to, way in ring:
                at = pl.ds(part * cut // 2, cut // 2)
                c_far.append(hand(pt.at[over, pl.ds(way * cut + part * cut // 2, cut // 2)],
                                  0, way, to, at, part))
        for to, way in ring:
            c_near.append(hand(pt.at[to, pl.ds((1 - way) * cut, cut)], 1, way, to))

    def pass_on(part):
        for copy, (to, way) in zip(c_far[2 * part:2 * part + 2], ring if nh > 1 else []):
            at = slice(part * cut // 2, (part + 1) * cut // 2)
            copy.wait_recv()
            base = way * cut
            sum_of = (pt[to, base + at.start:base + at.stop].astype(F32)
                      + pr[0, way, at].astype(F32))
            pv[way, at] = sum_of.astype(BF)
            c_near.append(hand(pv.at[way, pl.ds(at.start, cut // 2)], 2, way, to,
                               pl.ds(at.start, cut // 2), part))

    z_first = start_z(0, x_first)
    z_second = start_z(1, x_second, pass_on)
    y_first = start_y(0, z_first)
    y_second = start_y(1, z_second)

    total = pt[head].astype(F32)
    for copy in c_near:
        copy.wait_recv()
    if nh > 1:
        low = total[:cut] + pr[2, 0].astype(F32) + pr[1, 1].astype(F32)
        high = total[cut:] + pr[2, 1].astype(F32) + pr[1, 0].astype(F32)
        total = jnp.concatenate([low, high], axis=0)
    gt[...] = total.astype(BF)
    stores = [pltpu.make_async_copy(gt, gt_out, os_.at[0])]
    stores[0].start()

    sums = []
    for i, copies in enumerate((y_first, y_second)):
        for copy in copies:
            copy.wait_recv()
        own_part = ys[i].astype(F32)
        far_part = yr[0, i].astype(F32)
        if yn > 1:
            own_part = own_part + yr[1, i].astype(F32)
            far_part = far_part + yr[2, i].astype(F32)
            own_part = jnp.where(y == 0, own_part[:, :KV], own_part[:, KV:])
            far_part = jnp.where(y == 0, far_part[:, :KV], far_part[:, KV:])
        n = plan.rows_dev
        own_part, far_part = [jnp.where(core == 0, a[:n], a[n:2 * n])
                              for a in (own_part, far_part)]
        sums.append([jnp.where(core == 0, own_part, far_part),
                     jnp.where(core == 0, far_part, own_part)])
    early, late = sums
    go[...] = jnp.concatenate([early[c][:, :QW] for c in range(CORES)], axis=1)
    gw[...] = jnp.concatenate(
        [piece for c in range(CORES) for h in range(MINE)
         for piece in (early[c][:, QW + HD * h:QW + HD * (h + 1)],
                       late[c][:, 2 * HD * h:2 * HD * (h + 1)])], axis=1)
    stores.append(pltpu.make_async_copy(gw, gw_out, os_.at[1]))
    stores.append(pltpu.make_async_copy(go, go_out, os_.at[2]))
    for copy in stores[1:]:
        copy.start()
    for copy in started:
        copy.wait_send()
    for copy in stores:
        copy.wait()


def write_out(*refs):
    sources, results, stage, sems = refs[:3], refs[3:6], refs[6:9], refs[9]
    loads = [pltpu.make_async_copy(a, b, sems.at[0, i])
             for i, (a, b) in enumerate(zip(sources, stage))]
    stores = [pltpu.make_async_copy(a, b, sems.at[1, i])
              for i, (a, b) in enumerate(zip(stage, results))]
    for copy in loads:
        copy.start()
    for load, store in zip(loads, stores):
        load.wait()
        store.start()
    for copy in stores:
        copy.wait()


def per_device(plan, tokens, valid, offsets, qkv_weight, out_weight, out_grad):
    hbm = pl.BlockSpec(memory_space=pltpu.HBM)
    dma = pltpu.SemaphoreType.DMA
    xn, lanes = plan.xn, plan.lanes
    near, wide = pltpu.VMEM((PAIR, ROWS2, PAY), BF), pltpu.VMEM((ZN, ROWS3, PAY), BF)
    square = pltpu.VMEM((MINE, 2, TOK, TOK), F32)
    scratch = [
        pltpu.SMEM((2, HEADS), jnp.int32),
        pltpu.VMEM((1, TOK), jnp.int32),
        pltpu.VMEM((TOK, D), BF),
        pltpu.VMEM((HEADS * 3 * HD, D), BF),
        pltpu.VMEM((HEADS * HD, D), BF),
        pltpu.VMEM((TOK, D), BF),
        pltpu.VMEM((D // 4, TOK), BF),
        pltpu.VMEM((plan.rows_dev, HEADS * 3 * HD), F32),
        pltpu.VMEM((plan.rows_dev, HEADS * HD), F32),
        pltpu.VMEM((TOK, ALL + QW), BF),
        pltpu.VMEM((ROWS2 * KV // 128, 128), BF),
        pltpu.VMEM((ROWS3, KV), BF),
        pltpu.VMEM((TOK, D), BF),
        pltpu.VMEM((TOK, D), BF),
        pltpu.VMEM((2, TOK, ALL + QW), BF),
        square, square,
        pltpu.VMEM((PAIR * CORES, ROWS2 * KV // 128, 128), BF),
        pltpu.VMEM((ZN * CORES, ROWS3, KV), BF),
        near, wide, near, wide,
        pltpu.VMEM((2, TOK, KV), F32),
        pltpu.VMEM((QW, 2 * TOK), BF),
        pltpu.VMEM((QW, 2 * TOK), BF),
        pltpu.VMEM((QW, 2 * TOK), BF),
        pltpu.VMEM((D, 2 * TOK), BF),
        pltpu.VMEM((D, 2 * TOK), BF),
        pltpu.VMEM((2, D, ALL), BF),
        pltpu.VMEM((TOK, KV), BF),
        pltpu.VMEM((TOK, KV), BF),
        pltpu.VMEM((TOK, QW), BF),
        pltpu.VMEM((TOK, QW), BF),
        pltpu.VMEM((2, xn, plan.xrows, lanes), BF),
        pltpu.VMEM((2, xn, plan.xrows, lanes), BF),
        pltpu.VMEM((2, ZN, plan.chunk, lanes), BF),
        pltpu.VMEM((2, ZN, plan.chunk, lanes), BF),
        pltpu.VMEM((2, plan.chunk, lanes), BF),
        pltpu.VMEM((3, 2, plan.chunk, lanes), BF),
        pltpu.VMEM((4, D // 4, TOK), BF),
        pltpu.VMEM((3, 2, D // 8, TOK), BF),
        pltpu.VMEM((2, D // 8, TOK), BF),
        dma((16,)), dma((3,)), dma((3,)), dma((3,)),
        dma((2, 2)), dma((2, 2)), dma((ZN, 2)), dma((ZN, 2)),
        dma, dma, dma((ZN,)), dma((ZN,)), dma((2,)), dma((2,)), dma((3, 2, 2)), dma((3, 2, 2)),
        dma((2, 2, 4)), dma((2, 2, 4)), dma((2, ZN)), dma((2, ZN)), dma((3, 2)), dma((3, 2)),
    ]
    gt, gw, go = pl.pallas_call(
        functools.partial(body, plan),
        out_shape=(
            jax.ShapeDtypeStruct((D // 4, TOK), BF),
            jax.ShapeDtypeStruct((plan.rows_dev, HEADS * 3 * HD), F32),
            jax.ShapeDtypeStruct((plan.rows_dev, HEADS * HD), F32),
        ),
        in_specs=[hbm] * 6,
        out_specs=(hbm, hbm, hbm),
        scratch_shapes=scratch,
        compiler_params=pltpu.CompilerParams(
            collective_id=0, has_side_effects=True, vmem_limit_bytes=VMEM_BYTES),
        cost_estimate=pl.CostEstimate(flops=2_000_000_000, bytes_accessed=4_000_000,
                                      transcendentals=800_000),
    )(offsets.T, valid.reshape(1, TOK), tokens, qkv_weight.T, out_weight, out_grad)
    hold = pl.pallas_call(
        write_out,
        out_shape=tuple(jax.ShapeDtypeStruct(a.shape, a.dtype) for a in (gt, gw, go)),
        in_specs=[hbm] * 3,
        out_specs=(hbm, hbm, hbm),
        scratch_shapes=[pltpu.VMEM(a.shape, a.dtype) for a in (gt, gw, go)] + [dma((2, 3))],
        compiler_params=pltpu.CompilerParams(vmem_limit_bytes=VMEM_BYTES),
    )(gt, gw, go)
    return hold[0].T, hold[1], hold[2].T


def solution(mesh):
    plan = Plan(mesh.shape["seq"], mesh.shape["head"])
    return jax.shard_map(
        functools.partial(per_device, plan),
        mesh=mesh,
        in_specs=(
            P("seq", None),
            P("seq"),
            P("head", None),
            P(None, "head"),
            P("head", None),
            P("seq", None),
        ),
        out_specs=(P("seq", "head"), P("seq", "head"), P("head", "seq")),
        check_vma=False,
    )
```

```python
import functools
import math

import jax
import jax.numpy as jnp
from jax import lax
from jax.experimental import pallas as pl
from jax.experimental.pallas import tpu as pltpu
from jax.sharding import PartitionSpec as P

BF = jnp.bfloat16
F32 = jnp.float32
MESH = pl.DeviceIdType.MESH

HEADS = 4
HD = 48
TOK = 256
D = 768
CORES = 2
MINE = HEADS // CORES
KV = 2 * HD * MINE
QW = HD * MINE
ALL = KV + QW
PAY = CORES * KV
ZN = 8
PAIR = 2
SPAN2 = 4
SPAN3 = 16
ROWS2 = TOK // SPAN2
ROWS3 = TOK // SPAN3
PICKED = ROWS2 + ROWS3
FAR_FIRST = (4, 3, 5, 2, 6, 1, 7)
TURN = 2
MARK = 2.0**100
MARK_TEST = 2.0**90
LOW = -1e30
VMEM_BYTES = 53 * 1024 * 1024 + 700 * 1024


def nn(a, b):
    return lax.dot_general(a, b, (((1,), (0,)), ((), ())), preferred_element_type=F32)


def nt(a, b):
    return lax.dot_general(a, b, (((1,), (1,)), ((), ())), preferred_element_type=F32)


def iota(shape, dim):
    return lax.broadcasted_iota(jnp.int32, shape, dim)


def one_hot(mask):
    return jnp.where(mask, 1.0, 0.0).astype(BF)


def thirds(x):
    high = x.astype(BF).astype(F32)
    mid = (x - high).astype(BF).astype(F32)
    return [high, mid, (x - high - mid).astype(BF).astype(F32)]


def stack_rows(rows):
    at = iota((16, rows[0].shape[1]), 0)
    out = jnp.zeros(at.shape, F32)
    for i, row in enumerate(rows):
        out = jnp.where(at == i, row, out)
    return out.astype(BF)


def halves(x):
    high = x.astype(BF)
    return [high, (x - high.astype(F32)).astype(BF)]


class Plan:
    def __init__(self, n_seq, n_head):
        self.n_head = n_head
        self.yn = 2 if n_seq >= 32 else 1
        self.xn = n_seq // (CORES * ZN * self.yn)
        self.rows_dev = D // n_seq
        self.rows_chip = CORES * self.rows_dev
        self.chunk = -(-self.rows_chip // 16) * 16
        self.xrows = ZN * self.rows_chip
        self.lanes = self.yn * KV


def body(plan, offs_h, valid_h, tokens_h, wqkv_h, wout_h, ograd_h, gt_out, gw_out, go_out,
         offs, valid, tokens, wqkv, wout, ograd,
         p_out, s2, s3, tok_in, og_in, proj, w_loc, p_loc, kv2, kv3, g2, g3, r2, r3, own, att_t, dq_t,
         dat_t, tok_t, og_t, wn, d_out, d_in, q_out, q_in,
         xs, xr, zs, zr, ys, yr, pt, pr, pv,
         ls, es, er, a2s, a2r, a3s, a3r, b2s, b2r, b3s, b3r, ds_, dr_, cs, cr,
         xss, xrs, zss, zrs, yss, yrs):
    xn, yn, nh = plan.xn, plan.yn, plan.n_head
    factor = 1.0 / math.sqrt(HD)
    seq = lax.axis_index("seq")
    head = lax.axis_index("head")
    core = seq % CORES
    other = 1 - core
    z = (seq // CORES) % ZN
    y = (seq // (CORES * ZN)) % yn
    x = seq // (CORES * ZN * yn)

    def place(xi, yi, zi, ci):
        return (((xi * yn + yi) * ZN + zi) * CORES + ci, head)

    near_z = z % PAIR
    mate = z - near_z + 1 - near_z
    pos2 = near_z * CORES
    pos3 = z * CORES
    sibling = place(x, y, z, other)
    z_peers = {d: (z + d) % ZN for d in FAR_FIRST}
    x_peers = {d: (x + d) % xn for d in (2, 1, 3) if d < xn}
    h_peers = {d: (head + d) % nh for d in (1, 3) if d < nh}
    far = (y + 1) % yn
    y_peers = [sibling]
    if yn > 1:
        y_peers += [place(x, far, z, core), place(x, far, z, other)]

    barrier = pltpu.get_barrier_semaphore()
    greeted = [place(x, y, zi, c) for zi in z_peers.values() for c in (core, other)] + y_peers
    greeted += [place(xi, y, z, core) for xi in x_peers.values()]
    greeted += [(seq, to) for to in h_peers.values()]
    for who in greeted:
        pl.semaphore_signal(barrier, inc=1, device_id=who, device_id_type=MESH)

    loads = []

    def load(src, dst):
        copy = pltpu.make_async_copy(src, dst, ls.at[len(loads)])
        copy.start()
        loads.append(copy)
        return copy

    def load_rows(src, dst, base, rows, pieces):
        size = rows // pieces
        return [load(src.at[at], dst.at[at]) for at in
                [pl.ds(pl.multiple_of(base + size * i, 16), size) for i in range(pieces)]]

    w_rows = MINE * 3 * HD
    need_first = load_rows(tokens_h, tokens, 0, TOK, 2)
    for h in range(HEADS):
        need_first += load_rows(wqkv_h, wqkv, 3 * HD * h + HD, 2 * HD, 1)
    need_first += [load(valid_h, valid), load(offs_h, offs)]
    need_then = []
    for h in range(HEADS):
        need_then += load_rows(wqkv_h, wqkv, 3 * HD * h, HD, 1)
    need_then += load_rows(ograd_h, ograd, 0, TOK, 2)
    need_then += load_rows(wout_h, wout, 0, CORES * QW, 1)

    started = []

    def send(src, dst, ssem, rsem, who):
        copy = pltpu.make_async_remote_copy(
            src_ref=src, dst_ref=dst, send_sem=ssem, recv_sem=rsem,
            device_id=who, device_id_type=MESH)
        copy.start()
        started.append(copy)
        return copy

    def rows_of(c, start, size):
        base = c * w_rows + start
        return jnp.concatenate(
            [wqkv[pl.ds(pl.multiple_of(base + 3 * HD * h, 16), size), :] for h in range(MINE)],
            axis=0)

    def out_of(c):
        return wout[pl.ds(pl.multiple_of(c * QW, 16), QW), :]

    eye = iota((TOK, TOK), 0) == iota((TOK, TOK), 1)
    eye_b = one_hot(eye)
    can_mark = iota((TOK, KV), 1) % (2 * HD) == 0
    for copy in need_first:
        copy.wait()
    alive = jnp.sum(jnp.where(eye, valid[...].astype(F32), 0.0), axis=1, keepdims=True)
    marked = can_mark & (alive == 0.0)
    kv_mine, kv_other = rows_of(core, HD, 2 * HD), rows_of(other, HD, 2 * HD)
    p_out[:, :KV] = jnp.where(marked, MARK, nt(tokens[...], kv_other)).astype(BF)
    proj[0, :, :KV] = jnp.where(marked, MARK, nt(tokens[...], kv_mine)).astype(BF)

    def pick_of(g):
        rows = iota((PICKED, TOK), 0)
        want = jnp.where(rows < ROWS2, rows * SPAN2 + offs[0, g],
                         (rows - ROWS2) * SPAN3 + offs[1, g])
        return one_hot(iota((PICKED, TOK), 1) == want)

    picks = [pick_of(core * MINE + h) for h in range(MINE)]
    for h in range(MINE):
        cols = slice(2 * HD * h, 2 * HD * (h + 1))
        chosen = nn(picks[h], proj[0, :, cols]).astype(BF)
        kv2[pos2, :, cols] = chosen[:ROWS2]
        kv3[pos3, :, cols] = chosen[ROWS2:]
        chosen = nn(pick_of(other * MINE + h), p_out[:, cols]).astype(BF)
        s2[:, cols] = chosen[:ROWS2]
        s3[:, cols] = chosen[ROWS2:]

    pl.semaphore_wait(barrier, len(greeted))
    a_copies = []

    def give(source, other_source, to, sems, at, slot, zi, c):
        same = 0 if c is other else 1
        a_copies.append(send(source if same else other_source, to.at[slot + 1 - same],
                             sems[0].at[at, same], sems[1].at[at, same], place(x, y, zi, c)))

    for d, zi in z_peers.items():
        for c in (core, other):
            give(kv3.at[pos3], s3, kv3, (a3s, a3r), d, pos3, zi, c)
    for c in (core, other):
        give(kv2.at[pos2], s2, kv2, (a2s, a2r), 1, pos2, mate, c)
    give(kv3.at[pos3], s3, kv3, (a3s, a3r), 0, pos3, z, other)
    give(kv2.at[pos2], s2, kv2, (a2s, a2r), 0, pos2, z, other)

    for copy in need_then:
        copy.wait()
    q_mine, q_other = rows_of(core, 0, HD), rows_of(other, 0, HD)
    p_out[:, KV:ALL] = nt(tokens[...], q_other).astype(BF)
    p_out[:, ALL:] = nt(ograd[...], out_of(other)).astype(BF)
    swap = send(p_out, proj.at[1], es.at[0], er.at[0], sibling)
    tok_swap = send(tokens, tok_in, es.at[1], er.at[1], sibling)
    og_swap = send(ograd, og_in, es.at[2], er.at[2], sibling)

    phase2 = [offs[0, core * MINE + h] for h in range(MINE)]
    phase3 = [offs[1, core * MINE + h] for h in range(MINE)]
    proj[0, :, KV:ALL] = nt(tokens[...], q_mine).astype(BF)
    proj[0, :, ALL:] = nt(ograd[...], out_of(core)).astype(BF)
    dat_t[:, :TOK] = nt(out_of(core), ograd[...]).astype(BF)
    swap.wait_recv()
    dat_t[:, TOK:] = nt(eye_b[:QW, :QW], proj[1, :, ALL:]).astype(BF)
    eye_kv = one_hot(iota((KV, KV), 0) == iota((KV, KV), 1))
    local_t = [nt(eye_kv, proj[b, :, :KV]).astype(BF) for b in range(2)]
    spots = []
    for h in range(MINE):
        zero2, zero3 = jnp.zeros((ROWS2, TOK), BF), jnp.zeros((ROWS3, TOK), BF)
        one2, one3 = picks[h][:ROWS2], picks[h][ROWS2:]
        spots.append([
            jnp.concatenate([jnp.concatenate([one, zero], axis=1),
                             jnp.concatenate([zero, one], axis=1)], axis=0)
            for one, zero in ((one2, zero2), (one3, zero3))])

    def columns(h):
        return (slice(2 * HD * h, 2 * HD * h + HD), slice(2 * HD * h + HD, 2 * HD * (h + 1)),
                slice(KV + HD * h, KV + HD * (h + 1)), slice(ALL + HD * h, ALL + HD * (h + 1)))

    def soft(k, q):
        keep = k[:, 0:1].astype(F32) < MARK_TEST
        s = jnp.where(keep, nt(k, q) * factor, LOW)
        peak = jnp.max(s, axis=0, keepdims=True)
        w = jnp.exp(s - peak)
        return peak, w, jnp.sum(w, axis=0, keepdims=True)

    local = []
    few = []
    for h in range(MINE):
        kc, vc, qc, dc = columns(h)
        parts = []
        for b in range(2):
            peak, w, den = soft(proj[b, :, kc], proj[b, :, qc])
            w_loc[h, b] = w
            p_loc[h, b] = nt(proj[b, :, vc], proj[b, :, dc])
            parts.append((peak, den, nn(local_t[b][vc, :], w.astype(BF))))
        local.append([jnp.concatenate([parts[0][i], parts[1][i]], axis=1) for i in range(3)])
        chosen = [[nn(picks[h], proj[b, :, c]).astype(BF) for b in range(2)] for c in (qc, dc)]
        few.append([[jnp.concatenate([pair[0][at], pair[1][at]], axis=0) for pair in chosen]
                    for at in (slice(0, ROWS2), slice(ROWS2, PICKED))])

    row = iota((D, 1), 0)
    inner = (row % plan.xrows + (z + TURN) * plan.rows_chip) % plan.xrows
    order = one_hot(iota((D, D), 1) == row - row % plan.xrows + inner)

    def turn(to, block, b):
        to[:, b * TOK:(b + 1) * TOK] = nt(order, block[...]).astype(BF)

    turn(tok_t, tokens, 0)
    turn(og_t, ograd, 0)
    eye_d = one_hot(iota((D, D), 0) == iota((D, D), 1))
    wn[0] = nt(eye_d, jnp.concatenate([kv_mine, q_mine], axis=0)).astype(BF)
    wn[1] = nt(eye_d, jnp.concatenate([kv_other, q_other], axis=0)).astype(BF)

    for copy in a_copies:
        copy.wait_recv()

    lane = iota((1, 2 * TOK), 1)
    rows_far = [kv2[...].reshape(TOK, KV), kv3[...].reshape(TOK, KV)]
    cols_far = [nt(eye_kv, r).astype(BF) for r in rows_far]
    units = [(h, level) for h in range(MINE) for level in range(2)]
    members = [[lane % SPAN2 == phase2[h], lane % SPAN3 == phase3[h]] for h in range(MINE)]
    col = [columns(h) for h in range(MINE)]
    soft_far = {u: soft(rows_far[u[1]][:, col[u[0]][0]], few[u[0]][u[1]][0]) for u in units}
    prod_far = {u: nt(rows_far[u[1]][:, col[u[0]][1]], few[u[0]][u[1]][1]) for u in units}
    num_far = {u: nn(cols_far[u[1]][col[u[0]][1], :], soft_far[u][1].astype(BF)) for u in units}
    full = {}
    for u in units:
        peak, _, den = soft_far[u]
        full[u] = nn(jnp.concatenate([stack_rows(thirds(peak) + thirds(den))]
                                     + halves(num_far[u]), axis=0), spots[u[0]][u[1]])
    scale_loc, delta_loc, wanted = [], [], []
    for h in range(MINE):
        peaks, dens, nums = [local[h][0]], [local[h][1]], [local[h][2]]
        for level in range(2):
            got = full[h, level]
            peaks.append(jnp.where(members[h][level], got[0:1] + got[1:2] + got[2:3], LOW))
            dens.append(got[3:4] + got[4:5] + got[5:6])
            nums.append(got[16:16 + HD] + got[16 + HD:16 + 2 * HD])
        top = jnp.maximum(jnp.maximum(peaks[0], peaks[1]), peaks[2])
        scales = [jnp.exp(peak - top) for peak in peaks]
        inv = 1.0 / sum(scale * den for scale, den in zip(scales, dens))
        att = (sum(scale * num for scale, num in zip(scales, nums)) * inv).astype(BF)
        hr = slice(HD * h, HD * (h + 1))
        att_t[hr, :] = att
        delta = jnp.sum(dat_t[hr, :].astype(F32) * att.astype(F32), axis=0, keepdims=True)
        scale_loc.append(scales[0] * inv)
        delta_loc.append(delta)
        wanted.append(stack_rows(thirds(scales[1] * inv) + thirds(scales[2] * inv)
                                 + thirds(delta)))
    stats = {u: nt(wanted[u[0]], spots[u[0]][u[1]]) for u in units}
    grads = {}
    for u in units:
        i, got = 3 * u[1], stats[u]
        normed = soft_far[u][1] * (got[i:i + 1] + got[i + 1:i + 2] + got[i + 2:i + 3])
        delta_few = got[6:7] + got[7:8] + got[8:9]
        grads[u] = ((normed * (prod_far[u] - delta_few)).astype(BF), normed.astype(BF))
    for u in units:
        kc, vc, _, _ = col[u[0]]
        q, d = few[u[0]][u[1]]
        to, n = ((g2, PAIR), (g3, ZN))[u[1]]
        dk = (nn(grads[u][0], q) * factor).astype(BF).reshape(n, CORES, -1, HD)
        dv = nn(grads[u][1], d).astype(BF).reshape(n, CORES, -1, HD)
        for part in range(CORES):
            put = part * KV
            to[:, :, put + kc.start:put + kc.stop] = dk[:, part]
            to[:, :, put + vc.start:put + vc.stop] = dv[:, part]

    b_copies = []
    for d, zi in z_peers.items():
        b_copies.append(send(g3.at[zi], r3.at[z], b3s.at[d], b3r.at[d], place(x, y, zi, core)))
    b_copies.append(send(g2.at[1 - near_z], r2.at[near_z], b2s, b2r, place(x, y, mate, core)))
    r2[near_z] = g2[near_z]
    r3[z] = g3[z]

    dq_far = []
    for h in range(MINE):
        parts = []
        for level in range(2):
            dq = nn(cols_far[level][col[h][0], :], grads[h, level][0])
            dq = nn(jnp.concatenate(halves(dq), axis=0), spots[h][level])
            parts.append(dq[:HD] + dq[HD:])
        dq_far.append(parts[0] + parts[1])
    for h in range(MINE):
        kc, vc, qc, dc = columns(h)
        for b in range(2):
            at = slice(b * TOK, (b + 1) * TOK)
            normed = w_loc[h, b] * scale_loc[h][:, at]
            grad = (normed * (p_loc[h, b] - delta_loc[h][:, at])).astype(BF)
            own[b, :, kc] = nn(grad, proj[b, :, qc]) * factor
            own[b, :, vc] = nn(normed.astype(BF), proj[b, :, dc])
            dq = nn(local_t[b][kc, :], grad) + dq_far[h][:, at]
            dq_t[HD * h:HD * (h + 1), at] = (dq * factor).astype(BF)

    def pack(i, col, block):
        width = block.shape[1]
        block = block.astype(BF).reshape(xn, yn, plan.xrows, width)
        for yi in range(yn):
            xs[i, :, :, yi * KV + col:yi * KV + col + width] = block[:, yi]

    def parts_of(i):
        count = 2 if i else 1
        size = plan.xrows // count
        return [(k, pl.ds(k * size, size)) for k in range(count)]

    def start_x(i):
        return [[send(xs.at[i, xi, at], xr.at[i, d, at], xss.at[i, k, d], xrs.at[i, k, d],
                      place(xi, y, z, core)) for d, xi in x_peers.items()]
                for k, at in parts_of(i)]

    def start_z(i, copies, between=None):
        parts = parts_of(i)
        deep = ZN // len(parts)
        flying = {}
        for (k, at), some in zip(parts, copies):
            total = xs[i, x, at].astype(F32)
            for d, copy in zip(x_peers, some):
                copy.wait_recv()
                total = total + xr[i, d, at].astype(F32)
            here = [(k * deep + j + TURN) % ZN for j in range(deep)]
            for j, d in enumerate(here):
                rows = total[j * plan.rows_chip:(j + 1) * plan.rows_chip]
                if plan.chunk > plan.rows_chip:
                    rest = jnp.zeros((plan.chunk - plan.rows_chip, plan.lanes), F32)
                    rows = jnp.concatenate([rows, rest], axis=0)
                zs[i, d] = rows.astype(BF)
            for d, zi in z_peers.items():
                if d in here:
                    flying[d] = send(zs.at[i, d], zr.at[i, d], zss.at[i, d], zrs.at[i, d],
                                     place(x, y, zi, core))
        if between is not None:
            between()
        return flying

    def start_y(i, copies):
        total = zs[i, 0].astype(F32)
        for d, copy in copies.items():
            copy.wait_recv()
            total = total + zr[i, d].astype(F32)
        ys[i] = total.astype(BF)
        return [send(ys.at[i], yr.at[d, i], yss.at[d, i], yrs.at[d, i], who)
                for d, who in enumerate(y_peers)]

    dq = [nt(eye_b, dq_t[:, b * TOK:(b + 1) * TOK]).astype(BF) for b in range(2)]
    q_out[...] = dq[1]
    q_swap = send(q_out, q_in, ds_.at[0], dr_.at[0], sibling)
    og_swap.wait_recv()
    turn(og_t, og_in, 1)
    pack(0, 0, nt(og_t[...], att_t[...]))
    tok_swap.wait_recv()
    turn(tok_t, tok_in, 1)
    pack(0, QW, nt(tok_t[...], dq_t[...]))
    x_first = start_x(0)
    spreads = []
    for h in range(MINE):
        row, col = iota((TOK, TOK), 0), iota((TOK, TOK), 1)
        spreads.append(one_hot(row == jnp.where(
            col < PAIR * ROWS2, (col % ROWS2) * SPAN2 + phase2[h],
            (col % ROWS3) * SPAN3 + phase3[h])))
    for copy in b_copies:
        copy.wait_recv()
    back = jnp.concatenate([r2[...].reshape(PAIR * ROWS2, PAY),
                            r3[...].reshape(ZN * ROWS3, PAY)], axis=0)

    def finish(b):
        parts = []
        for h in range(MINE):
            cols = slice(2 * HD * h, 2 * HD * (h + 1))
            got = slice(b * KV + 2 * HD * h, b * KV + 2 * HD * (h + 1))
            parts.append(own[b, :, cols] + nn(spreads[h], back[:, got]))
        return jnp.concatenate(parts, axis=1).astype(BF)

    theirs = finish(1)
    d_out[...] = theirs
    swap = send(d_out, d_in, ds_.at[1], dr_.at[1], sibling)
    mine = finish(0)
    pack(1, 0, nn(tok_t[...], jnp.concatenate([mine, theirs], axis=0)))
    x_second = start_x(1)

    shares = nt(wn[0], jnp.concatenate([mine, dq[0]], axis=1))
    q_swap.wait_recv()
    swap.wait_recv()
    shares = shares + nt(wn[1], jnp.concatenate([d_in[...], q_in[...]], axis=1))
    pt[...] = shares.astype(BF).reshape(pt.shape)
    c_far, c_near = [], []
    cut = D // 8
    if nh > 1:
        ring = [((head + 1) % nh, 0), ((head + nh - 1) % nh, 1)]
        over = (head + 2) % nh

        def hand(src, slot, way, to):
            return send(src, pr.at[slot, way], cs.at[slot, way], cr.at[slot, way], (seq, to))

        for to, way in ring:
            c_far.append(hand(pt.at[over, pl.ds(way * cut, cut)], 0, way, to))
        for to, way in ring:
            c_near.append(hand(pt.at[to, pl.ds((1 - way) * cut, cut)], 1, way, to))

    def pass_on():
        for copy, (to, way) in zip(c_far, ring if nh > 1 else []):
            copy.wait_recv()
            both = pt[to, way * cut:(way + 1) * cut].astype(F32) + pr[0, way].astype(F32)
            pv[way] = both.astype(BF)
            c_near.append(hand(pv.at[way], 2, way, to))

    z_first = start_z(0, x_first)
    z_second = start_z(1, x_second, pass_on)
    y_first = start_y(0, z_first)
    y_second = start_y(1, z_second)
    flying = y_second + c_near
    for copy in started:
        if not any(copy is other_copy for other_copy in flying):
            copy.wait_send()

    total = pt[head].astype(F32)
    for copy in c_near:
        copy.wait_recv()
    if nh > 1:
        low = total[:cut] + pr[2, 0].astype(F32) + pr[1, 1].astype(F32)
        high = total[cut:] + pr[2, 1].astype(F32) + pr[1, 0].astype(F32)
        total = jnp.concatenate([low, high], axis=0)
    gt_out[...] = total.astype(BF)

    sums = []
    for i, copies in enumerate((y_first, y_second)):
        for copy in copies:
            copy.wait_recv()
        own_part = ys[i].astype(F32)
        far_part = yr[0, i].astype(F32)
        if yn > 1:
            own_part = own_part + yr[1, i].astype(F32)
            far_part = far_part + yr[2, i].astype(F32)
            own_part = jnp.where(y == 0, own_part[:, :KV], own_part[:, KV:])
            far_part = jnp.where(y == 0, far_part[:, :KV], far_part[:, KV:])
        n = plan.rows_dev
        own_part, far_part = [jnp.where(core == 0, a[:n], a[n:2 * n])
                              for a in (own_part, far_part)]
        sums.append([jnp.where(core == 0, own_part, far_part),
                     jnp.where(core == 0, far_part, own_part)])
    early, late = sums
    go_out[...] = jnp.concatenate([early[c][:, :QW] for c in range(CORES)], axis=1)
    gw_out[...] = jnp.concatenate(
        [piece for c in range(CORES) for h in range(MINE)
         for piece in (early[c][:, QW + HD * h:QW + HD * (h + 1)],
                       late[c][:, 2 * HD * h:2 * HD * (h + 1)])], axis=1)
    for copy in flying:
        copy.wait_send()


def write_out(*refs):
    copies = [pltpu.make_async_copy(a, b, refs[6].at[i])
              for i, (a, b) in enumerate(zip(refs[:3], refs[3:6]))]
    for copy in copies:
        copy.start()
    for copy in copies:
        copy.wait()


def per_device(plan, tokens, valid, offsets, qkv_weight, out_weight, out_grad):
    vm = pl.BlockSpec(memory_space=pltpu.VMEM)
    hbm = pl.BlockSpec(memory_space=pltpu.HBM)
    dma = pltpu.SemaphoreType.DMA
    xn, lanes = plan.xn, plan.lanes
    near, wide = pltpu.VMEM((PAIR, ROWS2, PAY), BF), pltpu.VMEM((ZN, ROWS3, PAY), BF)
    square = pltpu.VMEM((MINE, 2, TOK, TOK), F32)
    scratch = [
        pltpu.SMEM((2, HEADS), jnp.int32),
        pltpu.VMEM((1, TOK), jnp.int32),
        pltpu.VMEM((TOK, D), BF),
        pltpu.VMEM((HEADS * 3 * HD, D), BF),
        pltpu.VMEM((HEADS * HD, D), BF),
        pltpu.VMEM((TOK, D), BF),
        pltpu.VMEM((TOK, ALL + QW), BF),
        pltpu.VMEM((ROWS2, KV), BF),
        pltpu.VMEM((ROWS3, KV), BF),
        pltpu.VMEM((TOK, D), BF),
        pltpu.VMEM((TOK, D), BF),
        pltpu.VMEM((2, TOK, ALL + QW), BF),
        square, square,
        pltpu.VMEM((PAIR * CORES, ROWS2, KV), BF),
        pltpu.VMEM((ZN * CORES, ROWS3, KV), BF),
        near, wide, near, wide,
        pltpu.VMEM((2, TOK, KV), F32),
        pltpu.VMEM((QW, 2 * TOK), BF),
        pltpu.VMEM((QW, 2 * TOK), BF),
        pltpu.VMEM((QW, 2 * TOK), BF),
        pltpu.VMEM((D, 2 * TOK), BF),
        pltpu.VMEM((D, 2 * TOK), BF),
        pltpu.VMEM((2, D, ALL), BF),
        pltpu.VMEM((TOK, KV), BF),
        pltpu.VMEM((TOK, KV), BF),
        pltpu.VMEM((TOK, QW), BF),
        pltpu.VMEM((TOK, QW), BF),
        pltpu.VMEM((2, xn, plan.xrows, lanes), BF),
        pltpu.VMEM((2, xn, plan.xrows, lanes), BF),
        pltpu.VMEM((2, ZN, plan.chunk, lanes), BF),
        pltpu.VMEM((2, ZN, plan.chunk, lanes), BF),
        pltpu.VMEM((2, plan.chunk, lanes), BF),
        pltpu.VMEM((3, 2, plan.chunk, lanes), BF),
        pltpu.VMEM((4, D // 4, TOK), BF),
        pltpu.VMEM((3, 2, D // 8, TOK), BF),
        pltpu.VMEM((2, D // 8, TOK), BF),
        dma((16,)), dma((3,)), dma((3,)),
        dma((2, 2)), dma((2, 2)), dma((ZN, 2)), dma((ZN, 2)),
        dma, dma, dma((ZN,)), dma((ZN,)), dma((2,)), dma((2,)), dma((3, 2)), dma((3, 2)),
        dma((2, 2, 4)), dma((2, 2, 4)), dma((2, ZN)), dma((2, ZN)), dma((3, 2)), dma((3, 2)),
    ]
    gt, gw, go = pl.pallas_call(
        functools.partial(body, plan),
        out_shape=(
            jax.ShapeDtypeStruct((D // 4, TOK), BF),
            jax.ShapeDtypeStruct((plan.rows_dev, HEADS * 3 * HD), F32),
            jax.ShapeDtypeStruct((plan.rows_dev, HEADS * HD), F32),
        ),
        in_specs=[hbm] * 6,
        out_specs=(vm, vm, vm),
        scratch_shapes=scratch,
        compiler_params=pltpu.CompilerParams(
            collective_id=0, has_side_effects=True, vmem_limit_bytes=VMEM_BYTES),
        cost_estimate=pl.CostEstimate(flops=2_000_000_000, bytes_accessed=4_000_000,
                                      transcendentals=800_000),
    )(offsets.T, valid.reshape(1, TOK), tokens, qkv_weight.T, out_weight, out_grad)
    hold = pl.pallas_call(
        write_out,
        out_shape=tuple(jax.ShapeDtypeStruct(a.shape, a.dtype) for a in (gt, gw, go)),
        in_specs=[vm] * 3,
        out_specs=(hbm, hbm, hbm),
        scratch_shapes=[dma((3,))],
        compiler_params=pltpu.CompilerParams(vmem_limit_bytes=1024 * 1024),
    )(gt, gw, go)
    return hold[0].T, hold[1], hold[2].T


def solution(mesh):
    plan = Plan(mesh.shape["seq"], mesh.shape["head"])
    return jax.shard_map(
        functools.partial(per_device, plan),
        mesh=mesh,
        in_specs=(
            P("seq", None),
            P("seq"),
            P("head", None),
            P(None, "head"),
            P("head", None),
            P("seq", None),
        ),
        out_specs=(P("seq", "head"), P("seq", "head"), P("head", "seq")),
        check_vma=False,
    )
```

```python
import functools
import math

import jax
import jax.numpy as jnp
from jax import lax
from jax.experimental import pallas as pl
from jax.experimental.pallas import tpu as pltpu
from jax.sharding import PartitionSpec as P

BF = jnp.bfloat16
F32 = jnp.float32
MESH = pl.DeviceIdType.MESH

HEADS = 4
HD = 48
TOK = 256
D = 768
CORES = 2
MINE = HEADS // CORES
KV = 2 * HD * MINE
QW = HD * MINE
ALL = KV + QW
PAY = CORES * KV
ZN = 8
PAIR = 2
SPAN2 = 4
SPAN3 = 16
ROWS2 = TOK // SPAN2
ROWS3 = TOK // SPAN3
PICKED = ROWS2 + ROWS3
FAR_FIRST = (4, 3, 5, 2, 6, 1, 7)
TURN = 2
MARK = 2.0**100
MARK_TEST = 2.0**90
LOW = -1e30
VMEM_BYTES = 53 * 1024 * 1024 + 700 * 1024


def nn(a, b):
    return lax.dot_general(a, b, (((1,), (0,)), ((), ())), preferred_element_type=F32)


def nt(a, b):
    return lax.dot_general(a, b, (((1,), (1,)), ((), ())), preferred_element_type=F32)


def iota(shape, dim):
    return lax.broadcasted_iota(jnp.int32, shape, dim)


def one_hot(mask):
    return jnp.where(mask, 1.0, 0.0).astype(BF)


def thirds(x):
    high = x.astype(BF).astype(F32)
    mid = (x - high).astype(BF).astype(F32)
    return [high, mid, (x - high - mid).astype(BF).astype(F32)]


def stack_rows(rows):
    at = iota((16, rows[0].shape[1]), 0)
    out = jnp.zeros(at.shape, F32)
    for i, row in enumerate(rows):
        out = jnp.where(at == i, row, out)
    return out.astype(BF)


def halves(x):
    high = x.astype(BF)
    return [high, (x - high.astype(F32)).astype(BF)]


class Plan:
    def __init__(self, n_seq, n_head):
        self.n_head = n_head
        self.yn = 2 if n_seq >= 32 else 1
        self.xn = n_seq // (CORES * ZN * self.yn)
        self.rows_dev = D // n_seq
        self.rows_chip = CORES * self.rows_dev
        self.chunk = -(-self.rows_chip // 16) * 16
        self.xrows = ZN * self.rows_chip
        self.lanes = self.yn * KV


def body(plan, offs_h, valid_h, tokens_h, wqkv_h, wout_h, ograd_h, gt_out, gw_out, go_out,
         offs, valid, tokens, wqkv, wout, ograd,
         p_out, s2, s3, tok_in, og_in, proj, w_loc, p_loc, kv2, kv3, g2, g3, r2, r3, own, att_t, dq_t,
         dat_t, tok_t, og_t, wn, d_out, d_in, q_out, q_in,
         xs, xr, zs, zr, ys, yr, pt, pr, pv, ours,
         ls, es, er, a2s, a2r, a3s, a3r, b2s, b2r, b3s, b3r, ds_, dr_, cs, cr,
         xss, xrs, zss, zrs, yss, yrs):
    xn, yn, nh = plan.xn, plan.yn, plan.n_head
    factor = 1.0 / math.sqrt(HD)
    seq = lax.axis_index("seq")
    head = lax.axis_index("head")
    core = seq % CORES
    other = 1 - core
    z = (seq // CORES) % ZN
    y = (seq // (CORES * ZN)) % yn
    x = seq // (CORES * ZN * yn)

    def place(xi, yi, zi, ci):
        return (((xi * yn + yi) * ZN + zi) * CORES + ci, head)

    near_z = z % PAIR
    mate = z - near_z + 1 - near_z
    pos2 = near_z * CORES
    pos3 = z * CORES
    sibling = place(x, y, z, other)
    z_peers = {d: (z + d) % ZN for d in FAR_FIRST}
    x_peers = {d: (x + d) % xn for d in (2, 1, 3) if d < xn}
    h_peers = {d: (head + d) % nh for d in (1, 3) if d < nh}
    far = (y + 1) % yn
    y_peers = [sibling]
    if yn > 1:
        y_peers += [place(x, far, z, core), place(x, far, z, other)]

    barrier = pltpu.get_barrier_semaphore()
    greeted = [place(x, y, zi, c) for zi in z_peers.values() for c in (core, other)] + y_peers
    greeted += [place(xi, y, z, core) for xi in x_peers.values()]
    greeted += [(seq, to) for to in h_peers.values()]
    def greet(some):
        for who in some:
            pl.semaphore_signal(barrier, inc=1, device_id=who, device_id_type=MESH)

    soon = CORES * len(z_peers) + 1
    greet(greeted[:soon])

    loads = []

    def load(src, dst):
        copy = pltpu.make_async_copy(src, dst, ls.at[len(loads)])
        copy.start()
        loads.append(copy)
        return copy

    def load_rows(src, dst, base, rows, pieces):
        size = rows // pieces
        return [load(src.at[at], dst.at[at]) for at in
                [pl.ds(pl.multiple_of(base + size * i, 16), size) for i in range(pieces)]]

    w_rows = MINE * 3 * HD
    need_first = load_rows(tokens_h, tokens, 0, TOK, 2)
    for h in range(HEADS):
        need_first += load_rows(wqkv_h, wqkv, 3 * HD * h + HD, 2 * HD, 1)
    need_first += [load(valid_h, valid), load(offs_h, offs)]
    need_then = []
    for h in range(HEADS):
        need_then += load_rows(wqkv_h, wqkv, 3 * HD * h, HD, 1)
    need_then += load_rows(ograd_h, ograd, 0, TOK, 2)
    need_then += load_rows(wout_h, wout, 0, CORES * QW, 1)

    greet(greeted[soon:])

    started = []

    def send(src, dst, ssem, rsem, who):
        copy = pltpu.make_async_remote_copy(
            src_ref=src, dst_ref=dst, send_sem=ssem, recv_sem=rsem,
            device_id=who, device_id_type=MESH)
        copy.start()
        started.append(copy)
        return copy

    def rows_of(c, start, size):
        base = c * w_rows + start
        return jnp.concatenate(
            [wqkv[pl.ds(pl.multiple_of(base + 3 * HD * h, 16), size), :] for h in range(MINE)],
            axis=0)

    def out_of(c):
        return wout[pl.ds(pl.multiple_of(c * QW, 16), QW), :]

    eye = iota((TOK, TOK), 0) == iota((TOK, TOK), 1)
    eye_b = one_hot(eye)
    can_mark = iota((TOK, KV), 1) % (2 * HD) == 0
    for copy in need_first:
        copy.wait()
    alive = jnp.sum(jnp.where(eye, valid[...].astype(F32), 0.0), axis=1, keepdims=True)
    marked = can_mark & (alive == 0.0)
    kv_mine, kv_other = rows_of(core, HD, 2 * HD), rows_of(other, HD, 2 * HD)
    p_out[:, :KV] = jnp.where(marked, MARK, nt(tokens[...], kv_other)).astype(BF)
    proj[0, :, :KV] = jnp.where(marked, MARK, nt(tokens[...], kv_mine)).astype(BF)

    def pick_of(g):
        rows = iota((PICKED, TOK), 0)
        want = jnp.where(rows < ROWS2, rows * SPAN2 + offs[0, g],
                         (rows - ROWS2) * SPAN3 + offs[1, g])
        return one_hot(iota((PICKED, TOK), 1) == want)

    picks = [pick_of(core * MINE + h) for h in range(MINE)]
    for h in range(MINE):
        cols = slice(2 * HD * h, 2 * HD * (h + 1))
        chosen = nn(picks[h], proj[0, :, cols]).astype(BF)
        kv2[pos2, :, cols] = chosen[:ROWS2]
        kv3[pos3, :, cols] = chosen[ROWS2:]
        chosen = nn(pick_of(other * MINE + h), p_out[:, cols]).astype(BF)
        s2[:, cols] = chosen[:ROWS2]
        s3[:, cols] = chosen[ROWS2:]

    pl.semaphore_wait(barrier, len(greeted))
    a_copies = []

    def give(source, other_source, to, sems, at, slot, zi, c):
        same = 0 if c is other else 1
        a_copies.append(send(source if same else other_source, to.at[slot + 1 - same],
                             sems[0].at[at, same], sems[1].at[at, same], place(x, y, zi, c)))

    for d, zi in z_peers.items():
        for c in (core, other):
            give(kv3.at[pos3], s3, kv3, (a3s, a3r), d, pos3, zi, c)
    for c in (core, other):
        give(kv2.at[pos2], s2, kv2, (a2s, a2r), 1, pos2, mate, c)
    give(kv3.at[pos3], s3, kv3, (a3s, a3r), 0, pos3, z, other)
    give(kv2.at[pos2], s2, kv2, (a2s, a2r), 0, pos2, z, other)

    for copy in need_then:
        copy.wait()
    q_mine, q_other = rows_of(core, 0, HD), rows_of(other, 0, HD)
    p_out[:, KV:ALL] = nt(tokens[...], q_other).astype(BF)
    p_out[:, ALL:] = nt(ograd[...], out_of(other)).astype(BF)
    swap = send(p_out, proj.at[1], es.at[0], er.at[0], sibling)
    tok_swap = send(tokens, tok_in, es.at[1], er.at[1], sibling)
    og_swap = send(ograd, og_in, es.at[2], er.at[2], sibling)

    phase2 = [offs[0, core * MINE + h] for h in range(MINE)]
    phase3 = [offs[1, core * MINE + h] for h in range(MINE)]
    proj[0, :, KV:ALL] = nt(tokens[...], q_mine).astype(BF)
    proj[0, :, ALL:] = nt(ograd[...], out_of(core)).astype(BF)
    dat_t[:, :TOK] = nt(out_of(core), ograd[...]).astype(BF)
    swap.wait_recv()
    dat_t[:, TOK:] = nt(eye_b[:QW, :QW], proj[1, :, ALL:]).astype(BF)
    eye_kv = one_hot(iota((KV, KV), 0) == iota((KV, KV), 1))
    local_t = [nt(eye_kv, proj[b, :, :KV]).astype(BF) for b in range(2)]
    spots = []
    for h in range(MINE):
        zero2, zero3 = jnp.zeros((ROWS2, TOK), BF), jnp.zeros((ROWS3, TOK), BF)
        one2, one3 = picks[h][:ROWS2], picks[h][ROWS2:]
        spots.append([
            jnp.concatenate([jnp.concatenate([one, zero], axis=1),
                             jnp.concatenate([zero, one], axis=1)], axis=0)
            for one, zero in ((one2, zero2), (one3, zero3))])

    def columns(h):
        return (slice(2 * HD * h, 2 * HD * h + HD), slice(2 * HD * h + HD, 2 * HD * (h + 1)),
                slice(KV + HD * h, KV + HD * (h + 1)), slice(ALL + HD * h, ALL + HD * (h + 1)))

    def soft(k, q):
        keep = k[:, 0:1].astype(F32) < MARK_TEST
        s = jnp.where(keep, nt(k, q) * factor, LOW)
        peak = jnp.max(s, axis=0, keepdims=True)
        w = jnp.exp(s - peak)
        return peak, w, jnp.sum(w, axis=0, keepdims=True)

    local = []
    few = []
    for h in range(MINE):
        kc, vc, qc, dc = columns(h)
        parts = []
        for b in range(2):
            peak, w, den = soft(proj[b, :, kc], proj[b, :, qc])
            w_loc[h, b] = w
            p_loc[h, b] = nt(proj[b, :, vc], proj[b, :, dc])
            parts.append((peak, den, nn(local_t[b][vc, :], w.astype(BF))))
        local.append([jnp.concatenate([parts[0][i], parts[1][i]], axis=1) for i in range(3)])
        chosen = [[nn(picks[h], proj[b, :, c]).astype(BF) for b in range(2)] for c in (qc, dc)]
        few.append([[jnp.concatenate([pair[0][at], pair[1][at]], axis=0) for pair in chosen]
                    for at in (slice(0, ROWS2), slice(ROWS2, PICKED))])

    row = iota((D, 1), 0)
    inner = (row % plan.xrows + (z + TURN) * plan.rows_chip) % plan.xrows
    order = one_hot(iota((D, D), 1) == row - row % plan.xrows + inner)

    def turn(to, block, b):
        to[:, b * TOK:(b + 1) * TOK] = nt(order, block[...]).astype(BF)

    turn(tok_t, tokens, 0)
    turn(og_t, ograd, 0)
    eye_d = one_hot(iota((D, D), 0) == iota((D, D), 1))
    wn[0] = nt(eye_d, jnp.concatenate([kv_mine, q_mine], axis=0)).astype(BF)
    wn[1] = nt(eye_d, jnp.concatenate([kv_other, q_other], axis=0)).astype(BF)

    for copy in a_copies:
        copy.wait_recv()

    lane = iota((1, 2 * TOK), 1)
    rows_far = [kv2[...].reshape(TOK, KV), kv3[...].reshape(TOK, KV)]
    cols_far = [nt(eye_kv, r).astype(BF) for r in rows_far]
    units = [(h, level) for h in range(MINE) for level in range(2)]
    members = [[lane % SPAN2 == phase2[h], lane % SPAN3 == phase3[h]] for h in range(MINE)]
    col = [columns(h) for h in range(MINE)]
    soft_far = {u: soft(rows_far[u[1]][:, col[u[0]][0]], few[u[0]][u[1]][0]) for u in units}
    prod_far = {u: nt(rows_far[u[1]][:, col[u[0]][1]], few[u[0]][u[1]][1]) for u in units}
    num_far = {u: nn(cols_far[u[1]][col[u[0]][1], :], soft_far[u][1].astype(BF)) for u in units}
    full = {}
    for u in units:
        peak, _, den = soft_far[u]
        full[u] = nn(jnp.concatenate([stack_rows(thirds(peak) + thirds(den))]
                                     + halves(num_far[u]), axis=0), spots[u[0]][u[1]])
    scale_loc, delta_loc, wanted = [], [], []
    for h in range(MINE):
        peaks, dens, nums = [local[h][0]], [local[h][1]], [local[h][2]]
        for level in range(2):
            got = full[h, level]
            peaks.append(jnp.where(members[h][level], got[0:1] + got[1:2] + got[2:3], LOW))
            dens.append(got[3:4] + got[4:5] + got[5:6])
            nums.append(got[16:16 + HD] + got[16 + HD:16 + 2 * HD])
        top = jnp.maximum(jnp.maximum(peaks[0], peaks[1]), peaks[2])
        scales = [jnp.exp(peak - top) for peak in peaks]
        inv = 1.0 / sum(scale * den for scale, den in zip(scales, dens))
        att = (sum(scale * num for scale, num in zip(scales, nums)) * inv).astype(BF)
        hr = slice(HD * h, HD * (h + 1))
        att_t[hr, :] = att
        delta = jnp.sum(dat_t[hr, :].astype(F32) * att.astype(F32), axis=0, keepdims=True)
        scale_loc.append(scales[0] * inv)
        delta_loc.append(delta)
        wanted.append(stack_rows(thirds(scales[1] * inv) + thirds(scales[2] * inv)
                                 + thirds(delta)))
    stats = {u: nt(wanted[u[0]], spots[u[0]][u[1]]) for u in units}
    grads = {}
    b_copies = []
    for level in (1, 0):
        for h in range(MINE):
            i, got = 3 * level, stats[h, level]
            normed = soft_far[h, level][1] * (got[i:i + 1] + got[i + 1:i + 2] + got[i + 2:i + 3])
            delta_few = got[6:7] + got[7:8] + got[8:9]
            grads[h, level] = ((normed * (prod_far[h, level] - delta_few)).astype(BF),
                               normed.astype(BF))
        for h in range(MINE):
            kc, vc, _, _ = col[h]
            q, d = few[h][level]
            to, n = ((g2, PAIR), (g3, ZN))[level]
            dk = (nn(grads[h, level][0], q) * factor).astype(BF).reshape(n, CORES, -1, HD)
            dv = nn(grads[h, level][1], d).astype(BF).reshape(n, CORES, -1, HD)
            for part in range(CORES):
                put = part * KV
                to[:, :, put + kc.start:put + kc.stop] = dk[:, part]
                to[:, :, put + vc.start:put + vc.stop] = dv[:, part]
        if level:
            for d, zi in z_peers.items():
                b_copies.append(send(g3.at[zi], r3.at[z], b3s.at[d], b3r.at[d],
                                     place(x, y, zi, core)))
        else:
            b_copies.append(send(g2.at[1 - near_z], r2.at[near_z], b2s, b2r,
                                 place(x, y, mate, core)))

    r2[near_z] = g2[near_z]
    r3[z] = g3[z]

    dq_far = []
    for h in range(MINE):
        parts = []
        for level in range(2):
            dq = nn(cols_far[level][col[h][0], :], grads[h, level][0])
            dq = nn(jnp.concatenate(halves(dq), axis=0), spots[h][level])
            parts.append(dq[:HD] + dq[HD:])
        dq_far.append(parts[0] + parts[1])
    for h in range(MINE):
        kc, vc, qc, dc = columns(h)
        for b in range(2):
            at = slice(b * TOK, (b + 1) * TOK)
            normed = w_loc[h, b] * scale_loc[h][:, at]
            grad = (normed * (p_loc[h, b] - delta_loc[h][:, at])).astype(BF)
            own[b, :, kc] = nn(grad, proj[b, :, qc]) * factor
            own[b, :, vc] = nn(normed.astype(BF), proj[b, :, dc])
            dq = nn(local_t[b][kc, :], grad) + dq_far[h][:, at]
            dq_t[HD * h:HD * (h + 1), at] = (dq * factor).astype(BF)

    def pack(i, col, block):
        width = block.shape[1]
        block = block.astype(BF).reshape(xn, yn, plan.xrows, width)
        for yi in range(yn):
            xs[i, :, :, yi * KV + col:yi * KV + col + width] = block[:, yi]

    def parts_of(i):
        count = 2 if i else 1
        size = plan.xrows // count
        return [(k, pl.ds(k * size, size)) for k in range(count)]

    def start_x(i):
        return [[send(xs.at[i, xi, at], xr.at[i, d, at], xss.at[i, k, d], xrs.at[i, k, d],
                      place(xi, y, z, core)) for d, xi in x_peers.items()]
                for k, at in parts_of(i)]

    def start_z(i, copies, between=None):
        parts = parts_of(i)
        deep = ZN // len(parts)
        flying = {}
        for (k, at), some in zip(parts, copies):
            total = xs[i, x, at].astype(F32)
            for d, copy in zip(x_peers, some):
                copy.wait_recv()
                total = total + xr[i, d, at].astype(F32)
            here = [(k * deep + j + TURN) % ZN for j in range(deep)]
            for j, d in enumerate(here):
                rows = total[j * plan.rows_chip:(j + 1) * plan.rows_chip]
                if plan.chunk > plan.rows_chip:
                    rest = jnp.zeros((plan.chunk - plan.rows_chip, plan.lanes), F32)
                    rows = jnp.concatenate([rows, rest], axis=0)
                zs[i, d] = rows.astype(BF)
            for d, zi in z_peers.items():
                if d in here:
                    flying[d] = send(zs.at[i, d], zr.at[i, d], zss.at[i, d], zrs.at[i, d],
                                     place(x, y, zi, core))
        if between is not None:
            between()
        return flying

    def start_y(i, copies):
        total = zs[i, 0].astype(F32)
        for d, copy in copies.items():
            copy.wait_recv()
            total = total + zr[i, d].astype(F32)
        ys[i] = total.astype(BF)
        return [send(ys.at[i], yr.at[d, i], yss.at[d, i], yrs.at[d, i], who)
                for d, who in enumerate(y_peers)]

    dq = [nt(eye_b, dq_t[:, b * TOK:(b + 1) * TOK]).astype(BF) for b in range(2)]
    q_out[...] = dq[1]
    q_swap = send(q_out, q_in, ds_.at[0], dr_.at[0], sibling)
    og_swap.wait_recv()
    turn(og_t, og_in, 1)
    pack(0, 0, nt(og_t[...], att_t[...]))
    tok_swap.wait_recv()
    turn(tok_t, tok_in, 1)
    pack(0, QW, nt(tok_t[...], dq_t[...]))
    x_first = start_x(0)
    spreads = []
    for h in range(MINE):
        row, col = iota((TOK, TOK), 0), iota((TOK, TOK), 1)
        spreads.append(one_hot(row == jnp.where(
            col < PAIR * ROWS2, (col % ROWS2) * SPAN2 + phase2[h],
            (col % ROWS3) * SPAN3 + phase3[h])))
    for copy in b_copies:
        copy.wait_recv()
    back = jnp.concatenate([r2[...].reshape(PAIR * ROWS2, PAY),
                            r3[...].reshape(ZN * ROWS3, PAY)], axis=0)

    def finish(b):
        parts = []
        for h in range(MINE):
            cols = slice(2 * HD * h, 2 * HD * (h + 1))
            got = slice(b * KV + 2 * HD * h, b * KV + 2 * HD * (h + 1))
            parts.append(own[b, :, cols] + nn(spreads[h], back[:, got]))
        return jnp.concatenate(parts, axis=1).astype(BF)

    theirs = finish(1)
    d_out[...] = theirs
    swap = send(d_out, d_in, ds_.at[1], dr_.at[1], sibling)
    mine = finish(0)
    pack(1, 0, nn(tok_t[...], jnp.concatenate([mine, theirs], axis=0)))
    x_second = start_x(1)

    ours[...] = nt(wn[0], jnp.concatenate([mine, dq[0]], axis=1)).reshape(ours.shape)
    q_swap.wait_recv()
    swap.wait_recv()
    got_rows = jnp.concatenate([d_in[...], q_in[...]], axis=1)

    def share(to):
        rows = pl.ds(pl.multiple_of(to * (D // 4), 16), D // 4)
        pt[to] = (ours[to] + nt(wn[1, rows, :], got_rows)).astype(BF)

    c_far, c_near = [], []
    cut = D // 8
    if nh > 1:
        ring = [((head + 1) % nh, 0), ((head + nh - 1) % nh, 1)]
        over = (head + 2) % nh

        def hand(src, slot, way, to):
            return send(src, pr.at[slot, way], cs.at[slot, way], cr.at[slot, way], (seq, to))

        share(over)
        for to, way in ring:
            c_far.append(hand(pt.at[over, pl.ds(way * cut, cut)], 0, way, to))
        for to, way in ring:
            share(to)
            c_near.append(hand(pt.at[to, pl.ds((1 - way) * cut, cut)], 1, way, to))
    share(head)

    def pass_on():
        for copy, (to, way) in zip(c_far, ring if nh > 1 else []):
            copy.wait_recv()
            both = pt[to, way * cut:(way + 1) * cut].astype(F32) + pr[0, way].astype(F32)
            pv[way] = both.astype(BF)
            c_near.append(hand(pv.at[way], 2, way, to))

    z_first = start_z(0, x_first)
    z_second = start_z(1, x_second, pass_on)
    y_first = start_y(0, z_first)
    y_second = start_y(1, z_second)
    flying = y_second + c_near
    for copy in started:
        if not any(copy is other_copy for other_copy in flying):
            copy.wait_send()

    total = pt[head].astype(F32)
    for copy in c_near:
        copy.wait_recv()
    if nh > 1:
        low = total[:cut] + pr[2, 0].astype(F32) + pr[1, 1].astype(F32)
        high = total[cut:] + pr[2, 1].astype(F32) + pr[1, 0].astype(F32)
        total = jnp.concatenate([low, high], axis=0)
    gt_out[...] = total.astype(BF)

    sums = []
    for i, copies in enumerate((y_first, y_second)):
        for copy in copies:
            copy.wait_recv()
        own_part = ys[i].astype(F32)
        far_part = yr[0, i].astype(F32)
        if yn > 1:
            own_part = own_part + yr[1, i].astype(F32)
            far_part = far_part + yr[2, i].astype(F32)
            own_part = jnp.where(y == 0, own_part[:, :KV], own_part[:, KV:])
            far_part = jnp.where(y == 0, far_part[:, :KV], far_part[:, KV:])
        n = plan.rows_dev
        own_part, far_part = [jnp.where(core == 0, a[:n], a[n:2 * n])
                              for a in (own_part, far_part)]
        sums.append([jnp.where(core == 0, own_part, far_part),
                     jnp.where(core == 0, far_part, own_part)])
    early, late = sums
    go_out[...] = jnp.concatenate([early[c][:, :QW] for c in range(CORES)], axis=1)
    gw_out[...] = jnp.concatenate(
        [piece for c in range(CORES) for h in range(MINE)
         for piece in (early[c][:, QW + HD * h:QW + HD * (h + 1)],
                       late[c][:, 2 * HD * h:2 * HD * (h + 1)])], axis=1)
    for copy in flying:
        copy.wait_send()


def write_out(*refs):
    copies = [pltpu.make_async_copy(a, b, refs[6].at[i])
              for i, (a, b) in enumerate(zip(refs[:3], refs[3:6]))]
    for copy in copies:
        copy.start()
    for copy in copies:
        copy.wait()


def per_device(plan, tokens, valid, offsets, qkv_weight, out_weight, out_grad):
    vm = pl.BlockSpec(memory_space=pltpu.VMEM)
    hbm = pl.BlockSpec(memory_space=pltpu.HBM)
    dma = pltpu.SemaphoreType.DMA
    xn, lanes = plan.xn, plan.lanes
    near, wide = pltpu.VMEM((PAIR, ROWS2, PAY), BF), pltpu.VMEM((ZN, ROWS3, PAY), BF)
    square = pltpu.VMEM((MINE, 2, TOK, TOK), F32)
    scratch = [
        pltpu.SMEM((2, HEADS), jnp.int32),
        pltpu.VMEM((1, TOK), jnp.int32),
        pltpu.VMEM((TOK, D), BF),
        pltpu.VMEM((HEADS * 3 * HD, D), BF),
        pltpu.VMEM((HEADS * HD, D), BF),
        pltpu.VMEM((TOK, D), BF),
        pltpu.VMEM((TOK, ALL + QW), BF),
        pltpu.VMEM((ROWS2, KV), BF),
        pltpu.VMEM((ROWS3, KV), BF),
        pltpu.VMEM((TOK, D), BF),
        pltpu.VMEM((TOK, D), BF),
        pltpu.VMEM((2, TOK, ALL + QW), BF),
        square, square,
        pltpu.VMEM((PAIR * CORES, ROWS2, KV), BF),
        pltpu.VMEM((ZN * CORES, ROWS3, KV), BF),
        near, wide, near, wide,
        pltpu.VMEM((2, TOK, KV), F32),
        pltpu.VMEM((QW, 2 * TOK), BF),
        pltpu.VMEM((QW, 2 * TOK), BF),
        pltpu.VMEM((QW, 2 * TOK), BF),
        pltpu.VMEM((D, 2 * TOK), BF),
        pltpu.VMEM((D, 2 * TOK), BF),
        pltpu.VMEM((2, D, ALL), BF),
        pltpu.VMEM((TOK, KV), BF),
        pltpu.VMEM((TOK, KV), BF),
        pltpu.VMEM((TOK, QW), BF),
        pltpu.VMEM((TOK, QW), BF),
        pltpu.VMEM((2, xn, plan.xrows, lanes), BF),
        pltpu.VMEM((2, xn, plan.xrows, lanes), BF),
        pltpu.VMEM((2, ZN, plan.chunk, lanes), BF),
        pltpu.VMEM((2, ZN, plan.chunk, lanes), BF),
        pltpu.VMEM((2, plan.chunk, lanes), BF),
        pltpu.VMEM((3, 2, plan.chunk, lanes), BF),
        pltpu.VMEM((4, D // 4, TOK), BF),
        pltpu.VMEM((3, 2, D // 8, TOK), BF),
        pltpu.VMEM((2, D // 8, TOK), BF),
        pltpu.VMEM((4, D // 4, TOK), F32),
        dma((16,)), dma((3,)), dma((3,)),
        dma((2, 2)), dma((2, 2)), dma((ZN, 2)), dma((ZN, 2)),
        dma, dma, dma((ZN,)), dma((ZN,)), dma((2,)), dma((2,)), dma((3, 2)), dma((3, 2)),
        dma((2, 2, 4)), dma((2, 2, 4)), dma((2, ZN)), dma((2, ZN)), dma((3, 2)), dma((3, 2)),
    ]
    gt, gw, go = pl.pallas_call(
        functools.partial(body, plan),
        out_shape=(
            jax.ShapeDtypeStruct((D // 4, TOK), BF),
            jax.ShapeDtypeStruct((plan.rows_dev, HEADS * 3 * HD), F32),
            jax.ShapeDtypeStruct((plan.rows_dev, HEADS * HD), F32),
        ),
        in_specs=[hbm] * 6,
        out_specs=(vm, vm, vm),
        scratch_shapes=scratch,
        compiler_params=pltpu.CompilerParams(
            collective_id=0, has_side_effects=True, vmem_limit_bytes=VMEM_BYTES),
        cost_estimate=pl.CostEstimate(flops=2_000_000_000, bytes_accessed=4_000_000,
                                      transcendentals=800_000),
    )(offsets.T, valid.reshape(1, TOK), tokens, qkv_weight.T, out_weight, out_grad)
    hold = pl.pallas_call(
        write_out,
        out_shape=tuple(jax.ShapeDtypeStruct(a.shape, a.dtype) for a in (gt, gw, go)),
        in_specs=[vm] * 3,
        out_specs=(hbm, hbm, hbm),
        scratch_shapes=[dma((3,))],
        compiler_params=pltpu.CompilerParams(vmem_limit_bytes=1024 * 1024),
    )(gt, gw, go)
    return hold[0].T, hold[1], hold[2].T


def solution(mesh):
    plan = Plan(mesh.shape["seq"], mesh.shape["head"])
    return jax.shard_map(
        functools.partial(per_device, plan),
        mesh=mesh,
        in_specs=(
            P("seq", None),
            P("seq"),
            P("head", None),
            P(None, "head"),
            P("head", None),
            P("seq", None),
        ),
        out_specs=(P("seq", "head"), P("seq", "head"), P("head", "seq")),
        check_vma=False,
    )
```
